32 devices in a mesh: graphs: 32 (over z, y, x, core).
Axes of the slice: x: 2, y: 2, z: 4, core: 2. Of those that a mesh axis runs over, the one named last changes fastest.
Arguments:
- node_input: bfloat16 [196608, 256], P('graphs'), may hold values from -16 to 16
- edge_input: bfloat16 [393216, 256], P('graphs'), may hold values from -6 to 6
- node_count: int32 [3072], P('graphs'), may hold values from 16 to 64, as said below
- edge_count: int32 [3072], P('graphs'), may hold values from 32 to 128, as said below
- edge_source: int32 [3072, 128], P('graphs'), may hold values from 0 to 63, as said below
- edge_target: int32 [3072, 128], P('graphs'), may hold values from 0 to 63, as said below
- gcn_weight: bfloat16 [256, 1024], replicated, may hold values from -0.375 to 0.375
- edge_weight: bfloat16 [256, 256], replicated, may hold values from -0.375 to 0.375
- attend_weight: bfloat16 [256, 768], replicated, may hold values from -0.375 to 0.375
- attend_out: bfloat16 [256, 256], replicated, may hold values from -2 to 2
- local_gain: float32 [256], replicated, may hold values from 0.1 to 1.9
- local_shift: float32 [256], replicated, may hold values from -3 to 3
- attend_gain: float32 [256], replicated, may hold values from 0.1 to 1.9
- attend_shift: float32 [256], replicated, may hold values from -3 to 3
- hidden_weight: bfloat16 [256, 512], replicated, may hold values from -0.375 to 0.375
- hidden_bias: float32 [512], replicated, may hold values from -3 to 3
- output_weight: bfloat16 [512, 256], replicated, may hold values from -0.25 to 0.25
- final_gain: float32 [256], replicated, may hold values from 0.1 to 1.9
- final_shift: float32 [256], replicated, may hold values from -3 to 3
- cotangent: bfloat16 [196608, 256], P('graphs'), may hold values from -16 to 16
Outputs:
- result: bfloat16 [196608, 256], P('graphs')
- node_grad: float32 [196608, 256], P('graphs')
- edge_grad: float32 [393216, 256], P('graphs')
- gcn_weight_grad: float32 [256, 1024], replicated
- edge_weight_grad: float32 [256, 256], replicated
- attend_weight_grad: float32 [256, 768], replicated
- attend_out_grad: float32 [256, 256], replicated
- local_gain_grad: float32 [256], replicated
- local_shift_grad: float32 [256], replicated
- attend_gain_grad: float32 [256], replicated
- attend_shift_grad: float32 [256], replicated
- hidden_weight_grad: float32 [256, 512], replicated
- hidden_bias_grad: float32 [512], replicated
- output_weight_grad: float32 [512, 256], replicated
- final_gain_grad: float32 [256], replicated
- final_shift_grad: float32 [256], replicated
The draws below stay inside these ranges and needn't reach their ends.
Inputs may be any that keep to these rules, and one draw needn't show every extreme that they name: `node_count`: some graph has exactly 64 nodes and some exactly 16. Some graph has exactly 128 edges and some exactly 32; edge slots from edge_count on are padding. `edge_source`: below its graph's node_count. `edge_target`: below its graph's node_count.
All inputs are finite; a program needn't handle non-finite values.
Results may differ from the reference program's by a relative error of at most 0.039.
Values sent between devices are 32-bit elements; how exact they have to be, the bound alone decides.
No kernel may reach another device: no remote copies, remote signals or barrier semaphores. Data moves between devices by JAX's collectives and lax.ppermute only.
A program may use at most 320 MiB of HBM per device.

```python
import jax
import jax.numpy as jnp
from jax import lax

D = 256
HEADS = 8
HEAD_SIZE = 32
FF = 512
NP = 64
EP = 128
BLOCK_GRAPHS = 8
GRAPHS = 3072
EDGES = 393216


def graph_draw(key):
    count_key, edge_key, source_key, target_key, pick_key = jax.random.split(key, 5)
    fewest_nodes = NP // 4
    fewest_edges = EP // 4
    picks = jax.random.permutation(pick_key, GRAPHS)
    graph_ids = jnp.arange(GRAPHS)
    counts = jax.random.randint(count_key, (GRAPHS,), fewest_nodes, NP + 1)
    counts = jnp.where(graph_ids == picks[0], NP, counts)
    counts = jnp.where(graph_ids == picks[1], fewest_nodes, counts)
    edges = jax.random.randint(edge_key, (GRAPHS,), fewest_edges, EP + 1)
    edges = jnp.where(graph_ids == picks[2], EP, edges)
    edges = jnp.where(graph_ids == picks[3], fewest_edges, edges)
    sources = jax.random.randint(source_key, (GRAPHS, EP), 0, 1 << 20) % counts[:, None]
    targets = jax.random.randint(target_key, (GRAPHS, EP), 0, 1 << 20) % counts[:, None]
    slot_ids = jnp.arange(EP)
    full_graph = (graph_ids == picks[0])[:, None]
    first_slot = full_graph & (slot_ids[None, :] == 0)
    second_slot = full_graph & (slot_ids[None, :] == 1)
    sources = jnp.where(first_slot, NP - 1, jnp.where(second_slot, 0, sources))
    targets = jnp.where(first_slot, 0, jnp.where(second_slot, NP - 1, targets))
    return (counts.astype(jnp.int32), edges.astype(jnp.int32), sources.astype(jnp.int32), targets.astype(jnp.int32))


def draw_node_count(key, part):
    return graph_draw(key)[0]


def draw_edge_count(key, part):
    return graph_draw(key)[1]


def draw_edge_source(key, part):
    return graph_draw(key)[2]


def draw_edge_target(key, part):
    return graph_draw(key)[3]


def row_scales(key, node_rows):
    ramp = 0.6 + 1.2 * jnp.arange(node_rows, dtype=jnp.float32) / node_rows
    rough = jnp.exp(jax.random.uniform(key, (node_rows,), jnp.float32, -0.8, 0.8))
    return (ramp * rough)[:, None]


def scaled_rows(key):
    scale_key, value_key = jax.random.split(key, 2)
    node_rows = GRAPHS * NP
    scales = row_scales(scale_key, node_rows)
    values = jnp.clip(jax.random.normal(value_key, (node_rows, D), jnp.float32), -4.0, 4.0)
    return (values * scales).astype(jnp.bfloat16)


def draw_node_input(key, part):
    key = jax.random.fold_in(key, 11)
    return scaled_rows(key)


def draw_cotangent(key, part):
    key = jax.random.fold_in(key, 12)
    return scaled_rows(key)


def levels(own_key, dims, cuts, smallest, largest):
    level = 1.0
    for axis_at, parts in cuts:
        draws = jax.random.uniform(jax.random.fold_in(jax.random.fold_in(own_key, 6), axis_at), (parts,), jnp.float32, smallest / len(cuts), largest / len(cuts))
        level = level * jnp.repeat(jnp.exp(draws), dims[axis_at] // parts).reshape((-1,) + (1,) * (len(dims) - 1 - axis_at))
    return level


def gaussian(rng, shape, scale, reach, cuts=(), kind=jnp.bfloat16):
    loudness = levels(rng, shape, cuts, -0.22, 0.18) if cuts else 1.0
    values = jax.random.normal(rng, shape, jnp.float32) * scale * loudness
    return jnp.minimum(jnp.maximum(values, -reach), reach).astype(kind)


def setup_inputs(seed: int = 0) -> dict:
    splits = jax.random.split(jax.random.key(seed), 21)
    return {
        "node_input": draw_node_input(jax.random.fold_in(splits[20], 71), 0),
        "edge_input": gaussian(splits[1], (EDGES, D), 1.0, 6.0, ((0, 32),)),
        "node_count": draw_node_count(jax.random.fold_in(splits[20], 71), 0),
        "edge_count": draw_edge_count(jax.random.fold_in(splits[20], 71), 0),
        "edge_source": draw_edge_source(jax.random.fold_in(splits[20], 71), 0),
        "edge_target": draw_edge_target(jax.random.fold_in(splits[20], 71), 0),
        "gcn_weight": gaussian(splits[6], (D, 4 * D), D ** -0.5, 0.375),
        "edge_weight": gaussian(splits[7], (D, D), D ** -0.5, 0.375),
        "attend_weight": gaussian(splits[8], (D, 3 * D), D ** -0.5, 0.375),
        "attend_out": gaussian(splits[9], (D, D), (D // 32) ** -0.5, 2.0),
        "local_gain": jnp.clip(1.0 + 0.18 * jax.random.normal(splits[10], (D,), jnp.float32), 0.1, 1.9),
        "local_shift": gaussian(splits[11], (D,), 0.5, 3.0, (), jnp.float32),
        "attend_gain": jnp.clip(1.0 + 0.18 * jax.random.normal(splits[12], (D,), jnp.float32), 0.1, 1.9),
        "attend_shift": gaussian(splits[13], (D,), 0.5, 3.0, (), jnp.float32),
        "hidden_weight": gaussian(splits[14], (D, FF), D ** -0.5, 0.375),
        "hidden_bias": gaussian(splits[15], (FF,), 0.5, 3.0, (), jnp.float32),
        "output_weight": gaussian(splits[16], (FF, D), FF ** -0.5, 0.25),
        "final_gain": jnp.clip(1.0 + 0.18 * jax.random.normal(splits[17], (D,), jnp.float32), 0.1, 1.9),
        "final_shift": gaussian(splits[18], (D,), 0.5, 3.0, (), jnp.float32),
        "cotangent": draw_cotangent(jax.random.fold_in(splits[20], 71), 0),
    }


exact_prec = lax.Precision.HIGHEST

@jax.custom_vjp
def low(v):
    return lax.optimization_barrier(v.astype(jnp.bfloat16)).astype(jnp.float32)

@jax.custom_vjp
def low_back(v):
    return v

def low_keep(v):
    return (low(v), None)

def low_pass(kept, grad):
    return (grad,)

def back_keep(v):
    return (v, None)

def back_low(kept, grad):
    return (low(grad),)
low.defvjp(low_keep, low_pass)
low_back.defvjp(back_keep, back_low)

def matmul_hi(left, right):
    return jnp.dot(left, right, precision=exact_prec)

def per_graph(values, slots):
    return values.reshape(GRAPHS, slots, values.shape[-1])

def batch_norm(values, gain, shift, node_mask, node_total):
    center = lax.optimization_barrier(jnp.sum(node_mask * values, axis=0)) / node_total
    spread = lax.optimization_barrier(jnp.sum(node_mask * values * values, axis=0)) / node_total - center * center
    return (values - center) * lax.rsqrt(spread + 1e-05) * gain + shift

def attend_block(operands):
    block_qkv, key_mask = operands
    query_rows = low(block_qkv[:, :, 0])
    key_rows = low(block_qkv[:, :, 1])
    value_rows = low(block_qkv[:, :, 2])
    scores = low_back(jnp.einsum('gqhc,gkhc->ghqk', query_rows, key_rows, precision=exact_prec) * HEAD_SIZE ** (-0.5))
    scores = jnp.where(key_mask[:, None, None, :] > 0, scores, -1e+30)
    attn_probs = jax.nn.softmax(scores, axis=-1)
    return jnp.einsum('ghqk,gkhc->gqhc', low(attn_probs), value_rows, precision=exact_prec)

def forward(node_vals, edge_vals, params, consts):
    gcn_weight, edge_weight, attend_weight, attend_out, local_gain, local_shift, attend_gain, attend_shift, hidden_weight, hidden_bias, output_weight, final_gain, final_shift = params
    node_mask, edge_mask, source_hot, target_hot, key_mask, node_total = consts
    node_low = low(node_vals)
    node_proj = low_back(matmul_hi(node_low, gcn_weight))
    self_part = node_proj[:, :D]
    source_part = low(node_proj[:, D:2 * D])
    target_part = low(node_proj[:, 2 * D:3 * D])
    sender_part = low(node_proj[:, 3 * D:])
    edge_proj = matmul_hi(low(edge_vals), edge_weight)
    from_target = jnp.einsum('gen,gnd->ged', target_hot, per_graph(target_part, NP), precision=exact_prec)
    from_source = jnp.einsum('gen,gnd->ged', source_hot, per_graph(sender_part, NP), precision=exact_prec)
    edge_hat = low_back(edge_proj + (from_target + from_source).reshape(-1, D))
    gate_sig = jax.nn.sigmoid(edge_hat)
    edge_gate = low(gate_sig * edge_mask)
    message_src = low_back(jnp.einsum('gen,gnd->ged', source_hot, per_graph(source_part, NP), precision=exact_prec).reshape(-1, D))
    message = low(edge_gate * message_src)
    numerator = low_back(jnp.einsum('gen,ged->gnd', target_hot, per_graph(message, EP), precision=exact_prec).reshape(-1, D))
    denominator = low_back(jnp.einsum('gen,ged->gnd', target_hot, per_graph(edge_gate, EP), precision=exact_prec).reshape(-1, D))
    local_pre = node_vals + self_part + numerator / (denominator + 1e-06)
    local_out = batch_norm(local_pre, local_gain, local_shift, node_mask, node_total)
    qkv = low_back(matmul_hi(node_low, attend_weight))
    blocked = qkv.reshape(GRAPHS // BLOCK_GRAPHS, BLOCK_GRAPHS, NP, 3, HEADS, HEAD_SIZE)
    attended = lax.map(jax.checkpoint(attend_block), (blocked, key_mask))
    attended = low_back(attended.reshape(-1, D))
    attn_vals = low_back(matmul_hi(low(attended), attend_out))
    attend_val = batch_norm(node_vals + attn_vals, attend_gain, attend_shift, node_mask, node_total)
    mixed_sum = local_out + attend_val
    pre_act = low_back(matmul_hi(low(mixed_sum), hidden_weight) + hidden_bias)
    branch_out = low_back(matmul_hi(low(jax.nn.silu(pre_act)), output_weight))
    return node_mask * batch_norm(mixed_sum + branch_out, final_gain, final_shift, node_mask, node_total)

def reference(node_input, edge_input, node_count, edge_count, edge_source, edge_target, gcn_weight, edge_weight, attend_weight, attend_out, local_gain, local_shift, attend_gain, attend_shift, hidden_weight, hidden_bias, output_weight, final_gain, final_shift, cotangent):
    node_slots = jnp.arange(NP, dtype=jnp.int32)
    edge_slots = jnp.arange(EP, dtype=jnp.int32)
    node_grid = (node_slots[None, :] < node_count[:, None]).astype(jnp.float32)
    node_mask = node_grid.reshape(-1, 1)
    edge_mask = (edge_slots[None, :] < edge_count[:, None]).astype(jnp.float32).reshape(-1, 1)
    source_hot = (edge_source[:, :, None] == node_slots[None, None, :]).astype(jnp.float32)
    target_hot = (edge_target[:, :, None] == node_slots[None, None, :]).astype(jnp.float32)
    key_mask = node_grid.reshape(GRAPHS // BLOCK_GRAPHS, BLOCK_GRAPHS, NP)
    node_total = jnp.sum(node_count).astype(jnp.float32)
    consts = (node_mask, edge_mask, source_hot, target_hot, key_mask, node_total)
    params = tuple((item.astype(jnp.float32) for item in (gcn_weight, edge_weight, attend_weight, attend_out, local_gain, local_shift, attend_gain, attend_shift, hidden_weight, hidden_bias, output_weight, final_gain, final_shift)))

    def layer(node_vals, edge_vals, weights):
        return forward(node_vals, edge_vals, weights, consts)
    result, pullback = jax.vjp(layer, node_input.astype(jnp.float32), edge_input.astype(jnp.float32), params)
    node_grad, edge_grad, grads = pullback(cotangent.astype(jnp.float32))
    return (result.astype(jnp.bfloat16), node_grad, edge_grad, grads[0], grads[1], grads[2], grads[3], grads[4], grads[5], grads[6], grads[7], grads[8], grads[9], grads[10], grads[11], grads[12])
```

```python
import functools

import jax
import jax.numpy as jnp
from jax import lax
from jax.experimental import pallas as pl
from jax.experimental.pallas import tpu as pltpu
from jax.sharding import PartitionSpec as P

HEAD_SIZE = 32
HALF = 128
GROUP = 8
EPS = 1e-05
F32 = jnp.float32
LOW = jnp.bfloat16
VMEM_BYTES = 48 * 1024 * 1024


def dot(left, right):
    return jnp.dot(left, right, preferred_element_type=F32)


def dot_nt(left, right):
    return lax.dot_general(left, right, (((1,), (1,)), ((), ())), preferred_element_type=F32)


def dot_tn(left, right):
    return lax.dot_general(left, right, (((0,), (0,)), ((), ())), preferred_element_type=F32)


def sigmoid(values):
    return 0.5 * jnp.tanh(0.5 * values) + 0.5


def norm_rows(total, squares, count):
    center = total / count
    return center, lax.rsqrt(squares / count - center * center + EPS)


def one_hot(index_row, slots):
    grid = lax.broadcasted_iota(jnp.int32, (slots, index_row.shape[1]), 0)
    return jnp.where(grid == index_row, 1.0, 0.0)


def row_mask(counts, first, graphs, slots, width):
    grid = lax.broadcasted_iota(jnp.int32, (slots, width), 0)
    return jnp.concatenate(
        [jnp.where(grid < counts[first + at], 1.0, 0.0) for at in range(graphs)], axis=0
    )


def head_blocks(rows):
    head = lax.broadcasted_iota(jnp.int32, rows.shape, 1) // HEAD_SIZE
    wide = rows.astype(F32)
    return jnp.concatenate(
        [jnp.where(head == at, wide, 0.0).astype(LOW) for at in range(HALF // HEAD_SIZE)], axis=0
    )


def head_merge(stacked, slots):
    head = lax.broadcasted_iota(jnp.int32, (slots, HALF), 1) // HEAD_SIZE
    merged = stacked[:slots]
    for at in range(1, HALF // HEAD_SIZE):
        merged = jnp.where(head == at, stacked[at * slots : (at + 1) * slots], merged)
    return merged


def column_sum(values):
    return jnp.sum(values, axis=0, keepdims=True)


def add_rows(stat_ref, rows):
    for at, row in enumerate(rows):
        stat_ref[at : at + 1, :] += row


def forward_kernel(
    node_count,
    edge_count,
    node_ref,
    edge_ref,
    source_ref,
    target_ref,
    gcn_weight,
    edge_weight,
    attend_weight,
    attend_out,
    local_ref,
    attend_ref,
    inverse_ref,
    ratio_ref,
    gate_ref,
    sent_ref,
    slope_ref,
    qkv_ref,
    prob_ref,
    attended_ref,
    stat_ref,
):
    step = pl.program_id(0)
    first = step * GROUP
    width = node_ref.shape[1]
    slots = node_ref.shape[0] // GROUP
    edges = edge_ref.shape[0] // GROUP

    @pl.when(step == 0)
    def _():
        stat_ref[...] = jnp.zeros_like(stat_ref)

    node = node_ref[...]
    inputs = node.astype(F32)
    proj = dot(node, gcn_weight[...])
    parts = proj[:, width:].astype(LOW)
    edge_proj = dot(edge_ref[...], edge_weight[...])
    qkv = dot(node, attend_weight[...]).astype(LOW)
    qkv_ref[...] = qkv
    edge_grid = lax.broadcasted_iota(jnp.int32, (edges, width), 0)
    node_grid = lax.broadcasted_iota(jnp.int32, (slots, 2 * HALF), 0)
    nothing = jnp.zeros((slots, width), LOW)
    for at in range(GROUP):
        rows = slice(at * slots, (at + 1) * slots)
        edge_rows = slice(at * edges, (at + 1) * edges)
        hot = jnp.concatenate(
            [one_hot(source_ref[at : at + 1, :], slots), one_hot(target_ref[at : at + 1, :], slots)],
            axis=0,
        ).astype(LOW)
        source_part = parts[rows, :width]
        target_part = parts[rows, width : 2 * width]
        sender_part = parts[rows, 2 * width :]
        spread = jnp.concatenate(
            [
                jnp.concatenate([sender_part, source_part], axis=1),
                jnp.concatenate([target_part, nothing], axis=1),
            ],
            axis=0,
        )
        gathered = dot_tn(hot, spread)
        edge_hat = edge_proj[edge_rows] + gathered[:, :width]
        sent = gathered[:, width:]
        edge_mask = jnp.where(edge_grid < edge_count[first + at], 1.0, 0.0)
        gate_sig = sigmoid(edge_hat)
        gate = (gate_sig * edge_mask).astype(LOW)
        message = (gate.astype(F32) * sent).astype(LOW)
        gate_ref[edge_rows, :] = gate
        sent_ref[edge_rows, :] = sent.astype(LOW)
        slope_ref[edge_rows, :] = (edge_mask * gate_sig * (1.0 - gate_sig)).astype(LOW)
        pooled = dot(hot[slots:], jnp.concatenate([message, gate], axis=1))
        inverse = 1.0 / (pooled[:, width:] + 1e-06)
        ratio = pooled[:, :width] * inverse
        inverse_ref[rows, :] = inverse
        ratio_ref[rows, :] = ratio
        local_ref[rows, :] = inputs[rows] + proj[rows, :width] + ratio
        for half in range(width // HALF):
            lanes = slice(half * HALF, (half + 1) * HALF)
            wide = slice(half * 2 * HALF, (half + 1) * 2 * HALF)
            query = qkv[rows, lanes]
            key = qkv[rows, width + half * HALF : width + (half + 1) * HALF]
            value = qkv[rows, 2 * width + half * HALF : 2 * width + (half + 1) * HALF]
            scores = dot_nt(key, head_blocks(query)) * HEAD_SIZE ** (-0.5)
            scores = jnp.where(node_grid < node_count[first + at], scores, -1e30)
            expo = jnp.exp(scores - jnp.max(scores, axis=0, keepdims=True))
            probs = (expo / column_sum(expo)).astype(LOW)
            prob_ref[rows, wide] = probs
            attended_ref[rows, lanes] = head_merge(dot_tn(probs, value), slots).astype(LOW)
    attend_pre = inputs + dot(attended_ref[...], attend_out[...])
    attend_ref[...] = attend_pre
    local_pre = local_ref[...]
    mask = row_mask(node_count, first, GROUP, slots, width)
    local_kept = mask * local_pre
    attend_kept = mask * attend_pre
    add_rows(
        stat_ref,
        (
            column_sum(local_kept),
            column_sum(local_kept * local_pre),
            column_sum(attend_kept),
            column_sum(attend_kept * attend_pre),
            column_sum(mask),
        ),
    )


def mix_kernel(
    node_count,
    local_ref,
    attend_ref,
    cotangent_ref,
    branch_stats,
    gains,
    hidden_weight,
    hidden_bias,
    output_weight,
    local_hat_ref,
    attend_hat_ref,
    mixed_ref,
    pre_ref,
    final_ref,
    stat_ref,
):
    step = pl.program_id(0)
    first = step * GROUP
    width = local_ref.shape[1]
    slots = local_ref.shape[0] // GROUP

    @pl.when(step == 0)
    def _():
        stat_ref[...] = jnp.zeros_like(stat_ref)

    count = branch_stats[4:5, :]
    local_center, local_inv = norm_rows(branch_stats[0:1, :], branch_stats[1:2, :], count)
    attend_center, attend_inv = norm_rows(branch_stats[2:3, :], branch_stats[3:4, :], count)
    local_hat = (local_ref[...] - local_center) * local_inv
    attend_hat = (attend_ref[...] - attend_center) * attend_inv
    local_hat_ref[...] = local_hat.astype(LOW)
    attend_hat_ref[...] = attend_hat.astype(LOW)
    scaled = local_hat * gains[0:1, :] + attend_hat * gains[2:3, :]
    mixed = (scaled + (gains[1:2, :] + gains[3:4, :])).astype(LOW)
    mixed_ref[...] = mixed
    pre = dot(mixed, hidden_weight[...]) + hidden_bias[...]
    pre_ref[...] = pre.astype(LOW)
    final = scaled + dot((pre * sigmoid(pre)).astype(LOW), output_weight[...])
    final_ref[...] = final
    mask = row_mask(node_count, first, GROUP, slots, width)
    kept = mask * final
    up = mask * cotangent_ref[...].astype(F32)
    add_rows(
        stat_ref,
        (column_sum(kept), column_sum(kept * final), column_sum(up), column_sum(up * final)),
    )


def mix_back_kernel(
    node_count,
    final_ref,
    pre_ref,
    local_hat_ref,
    attend_hat_ref,
    mixed_ref,
    cotangent_ref,
    branch_stats,
    final_stats,
    gains,
    hidden_weight,
    output_weight,
    result_ref,
    d_mixed_ref,
    output_grad,
    hidden_grad,
    bias_grad,
    stat_ref,
    final_grad,
):
    step = pl.program_id(0)
    first = step * GROUP
    width = final_ref.shape[1]
    slots = final_ref.shape[0] // GROUP
    count = branch_stats[4:5, :]
    center, inv = norm_rows(final_stats[0:1, :], final_stats[1:2, :], count)
    shift_grad = final_stats[2:3, :]
    gain_grad = inv * (final_stats[3:4, :] - center * shift_grad)

    @pl.when(step == 0)
    def _():
        stat_ref[...] = jnp.zeros_like(stat_ref)
        output_grad[...] = jnp.zeros_like(output_grad)
        hidden_grad[...] = jnp.zeros_like(hidden_grad)
        bias_grad[...] = jnp.zeros_like(bias_grad)
        final_grad[...] = jnp.zeros_like(final_grad)
        final_grad[0:1, :] = gain_grad
        final_grad[1:2, :] = shift_grad

    mask = row_mask(node_count, first, GROUP, slots, width)
    final_hat = (final_ref[...] - center) * inv
    result_ref[...] = (mask * (final_hat * gains[4:5, :] + gains[5:6, :])).astype(LOW)
    per_node = 1.0 / count
    d_final = (inv * gains[4:5, :]) * (
        mask
        * (
            cotangent_ref[...].astype(F32)
            - (shift_grad * per_node + final_hat * (gain_grad * per_node))
        )
    )
    d_branch = d_final.astype(LOW)
    pre = pre_ref[...].astype(F32)
    sig = sigmoid(pre)
    act = (pre * sig).astype(LOW)
    output_grad[...] += dot_tn(act, d_branch)
    d_pre_wide = dot_nt(d_branch, output_weight[...]) * (sig * (1.0 + pre * (1.0 - sig)))
    d_pre = d_pre_wide.astype(LOW)
    hidden_grad[...] += dot_tn(mixed_ref[...], d_pre)
    bias_grad[0:1, :] += column_sum(d_pre.astype(F32))
    d_mixed = d_final + dot_nt(d_pre, hidden_weight[...])
    d_mixed_ref[...] = d_mixed
    add_rows(
        stat_ref,
        (
            column_sum(d_mixed),
            column_sum(d_mixed * local_hat_ref[...].astype(F32)),
            column_sum(d_mixed * attend_hat_ref[...].astype(F32)),
        ),
    )


def branch_back(d_mixed, hat, mask, scale, shift_grad, gain_grad, count):
    per_node = 1.0 / count
    return scale * (d_mixed - mask * (shift_grad * per_node + hat * (gain_grad * per_node)))


def gcn_back_kernel(
    node_count,
    d_mixed_ref,
    local_hat_ref,
    inverse_ref,
    ratio_ref,
    gate_ref,
    sent_ref,
    slope_ref,
    node_ref,
    edge_ref,
    source_ref,
    target_ref,
    branch_stats,
    back_stats,
    gains,
    gcn_weight,
    edge_weight,
    edge_out_ref,
    node_part_ref,
    gcn_grad,
    edge_grad,
    d_proj,
    d_hats,
):
    step = pl.program_id(0)
    first = step * GROUP
    width = node_ref.shape[1]
    slots = node_ref.shape[0] // GROUP
    edges = edge_ref.shape[0] // GROUP

    @pl.when(step == 0)
    def _():
        gcn_grad[...] = jnp.zeros_like(gcn_grad)
        edge_grad[...] = jnp.zeros_like(edge_grad)

    count = branch_stats[4:5, :]
    _, inv = norm_rows(branch_stats[0:1, :], branch_stats[1:2, :], count)
    mask = row_mask(node_count, first, GROUP, slots, width)
    d_local = branch_back(
        d_mixed_ref[...],
        local_hat_ref[...].astype(F32),
        mask,
        inv * gains[0:1, :],
        back_stats[0:1, :],
        back_stats[1:2, :],
        count,
    )
    numer = d_local * inverse_ref[...]
    d_denom = (-numer * ratio_ref[...]).astype(LOW)
    d_numer = numer.astype(LOW)
    d_proj[:, :width] = d_local.astype(LOW)
    for at in range(GROUP):
        rows = slice(at * slots, (at + 1) * slots)
        edge_rows = slice(at * edges, (at + 1) * edges)
        hot = jnp.concatenate(
            [one_hot(source_ref[at : at + 1, :], slots), one_hot(target_ref[at : at + 1, :], slots)],
            axis=0,
        ).astype(LOW)
        back = dot_tn(hot[slots:], jnp.concatenate([d_numer[rows], d_denom[rows]], axis=1))
        d_message = back[:, :width]
        d_gate = back[:, width:] + d_message * sent_ref[edge_rows, :].astype(F32)
        d_sent = (d_message * gate_ref[edge_rows, :].astype(F32)).astype(LOW)
        d_hat = (d_gate * slope_ref[edge_rows, :].astype(F32)).astype(LOW)
        d_hats[edge_rows, :] = d_hat
        pulled = dot(hot, jnp.concatenate([d_sent, d_hat], axis=1)).astype(LOW)
        d_proj[rows, width : 2 * width] = pulled[:slots, :width]
        d_proj[rows, 2 * width : 3 * width] = pulled[slots:, width:]
        d_proj[rows, 3 * width :] = pulled[:slots, width:]
    edge_grad[...] += dot_tn(edge_ref[...], d_hats[...])
    edge_out_ref[...] = dot_nt(d_hats[...], edge_weight[...])
    gcn_grad[...] += dot_tn(node_ref[...], d_proj[...])
    node_part_ref[...] = d_local + dot_nt(d_proj[...], gcn_weight[...])


def attend_back_kernel(
    node_count,
    d_mixed_ref,
    attend_hat_ref,
    qkv_ref,
    prob_ref,
    attended_ref,
    node_ref,
    node_part_ref,
    branch_stats,
    back_stats,
    gains,
    attend_weight,
    attend_out,
    node_out_ref,
    weight_grad,
    out_grad,
    d_qkv,
):
    step = pl.program_id(0)
    first = step * GROUP
    width = node_ref.shape[1]
    slots = node_ref.shape[0] // GROUP

    @pl.when(step == 0)
    def _():
        weight_grad[...] = jnp.zeros_like(weight_grad)
        out_grad[...] = jnp.zeros_like(out_grad)

    count = branch_stats[4:5, :]
    _, inv = norm_rows(branch_stats[2:3, :], branch_stats[3:4, :], count)
    mask = row_mask(node_count, first, GROUP, slots, width)
    d_attend = branch_back(
        d_mixed_ref[...],
        attend_hat_ref[...].astype(F32),
        mask,
        inv * gains[2:3, :],
        back_stats[0:1, :],
        back_stats[2:3, :],
        count,
    )
    d_attn = d_attend.astype(LOW)
    out_grad[...] += dot_tn(attended_ref[...], d_attn)
    d_att = dot_nt(d_attn, attend_out[...]).astype(LOW)
    scale = HEAD_SIZE ** (-0.5)
    for at in range(GROUP):
        rows = slice(at * slots, (at + 1) * slots)
        for half in range(width // HALF):
            lanes = slice(half * HALF, (half + 1) * HALF)
            key_lanes = slice(width + half * HALF, width + (half + 1) * HALF)
            value_lanes = slice(2 * width + half * HALF, 2 * width + (half + 1) * HALF)
            wide = slice(half * 2 * HALF, (half + 1) * 2 * HALF)
            query_blocks = head_blocks(qkv_ref[rows, lanes])
            d_att_blocks = head_blocks(d_att[rows, lanes])
            key = qkv_ref[rows, key_lanes]
            value = qkv_ref[rows, value_lanes]
            probs = prob_ref[rows, wide]
            probs_wide = probs.astype(F32)
            d_probs = dot_nt(value, d_att_blocks)
            weighted = probs_wide * d_probs
            d_scores = (weighted - probs_wide * column_sum(weighted)).astype(LOW)
            d_qkv[rows, value_lanes] = dot(probs, d_att_blocks).astype(LOW)
            d_qkv[rows, key_lanes] = (dot(d_scores, query_blocks) * scale).astype(LOW)
            d_qkv[rows, lanes] = (head_merge(dot_tn(d_scores, key), slots) * scale).astype(LOW)
    weight_grad[...] += dot_tn(node_ref[...], d_qkv[...])
    node_out_ref[...] = node_part_ref[...] + d_attend + dot_nt(d_qkv[...], attend_weight[...])


def run_blocks(kernel, steps, args, outs, scratch=(), flops=0):
    def spec(kind, shape):
        if kind == "scalar":
            return pl.BlockSpec(memory_space=pltpu.SMEM)
        if kind == "rows":
            return pl.BlockSpec((shape[0] // steps, shape[1]), lambda step: (step, 0))
        return pl.BlockSpec(shape, lambda step: (0,) * len(shape))

    moved = sum(item.size * item.dtype.itemsize for _, item in args)
    shapes = [jax.ShapeDtypeStruct(shape, dtype) for _, shape, dtype in outs]
    moved += sum(item.size * item.dtype.itemsize for item in shapes)
    return pl.pallas_call(
        kernel,
        grid=(steps,),
        in_specs=[spec(kind, item.shape) for kind, item in args],
        out_specs=[spec(kind, shape) for kind, shape, _ in outs],
        out_shape=shapes,
        scratch_shapes=list(scratch),
        compiler_params=pltpu.CompilerParams(
            dimension_semantics=("arbitrary",), vmem_limit_bytes=VMEM_BYTES
        ),
        cost_estimate=pl.CostEstimate(flops=flops, bytes_accessed=moved, transcendentals=0),
    )(*[item for _, item in args])


def all_sum(values, devices):
    other = lax.ppermute(values, "graphs", [(at, at ^ 1) for at in range(devices)])
    values = values + other
    chips = devices // 2
    sent = jnp.broadcast_to(values[None], (chips,) + values.shape)
    groups = [list(range(core, devices, 2)) for core in range(2)]
    return jnp.sum(lax.all_to_all(sent, "graphs", 0, 0, axis_index_groups=groups), axis=0)


def on_device(
    devices,
    node_input,
    edge_input,
    node_count,
    edge_count,
    edge_source,
    edge_target,
    gcn_weight,
    edge_weight,
    attend_weight,
    attend_out,
    local_gain,
    local_shift,
    attend_gain,
    attend_shift,
    hidden_weight,
    hidden_bias,
    output_weight,
    final_gain,
    final_shift,
    cotangent,
):
    graphs, edges = edge_source.shape
    node_rows, width = node_input.shape
    edge_rows = edge_input.shape[0]
    slots = node_rows // graphs
    hidden = hidden_weight.shape[1]
    steps = graphs // GROUP
    gains = jnp.stack(
        [local_gain, local_shift, attend_gain, attend_shift, final_gain, final_shift, final_gain, final_shift]
    )
    node_count_arg = ("scalar", node_count)
    node_arg = ("rows", node_input)
    edge_arg = ("rows", edge_input)
    ends = [("rows", edge_source), ("rows", edge_target)]
    gains_arg = ("whole", gains)
    (
        local_pre,
        attend_pre,
        inverse,
        ratio,
        gate,
        sent,
        slope,
        qkv,
        probs,
        attended,
        branch_stats,
    ) = run_blocks(
        forward_kernel,
        steps,
        [node_count_arg, ("scalar", edge_count), node_arg, edge_arg]
        + ends
        + [("whole", item) for item in (gcn_weight, edge_weight, attend_weight, attend_out)],
        [
            ("rows", (node_rows, width), F32),
            ("rows", (node_rows, width), F32),
            ("rows", (node_rows, width), F32),
            ("rows", (node_rows, width), F32),
            ("rows", (edge_rows, width), LOW),
            ("rows", (edge_rows, width), LOW),
            ("rows", (edge_rows, width), LOW),
            ("rows", (node_rows, 3 * width), LOW),
            ("rows", (node_rows, (width // HEAD_SIZE) * slots), LOW),
            ("rows", (node_rows, width), LOW),
            ("whole", (8, width), F32),
        ],
    )
    branch_stats = all_sum(branch_stats, devices)
    branch_arg = ("whole", branch_stats)
    local_hat, attend_hat, mixed, pre, final, final_stats = run_blocks(
        mix_kernel,
        steps,
        [node_count_arg, ("rows", local_pre), ("rows", attend_pre), ("rows", cotangent)]
        + [branch_arg, gains_arg, ("whole", hidden_weight), ("whole", hidden_bias[None])]
        + [("whole", output_weight)],
        [
            ("rows", (node_rows, width), LOW),
            ("rows", (node_rows, width), LOW),
            ("rows", (node_rows, width), LOW),
            ("rows", (node_rows, hidden), LOW),
            ("rows", (node_rows, width), F32),
            ("whole", (8, width), F32),
        ],
    )
    final_stats = all_sum(final_stats, devices)
    result, d_mixed, output_grad, hidden_grad, bias_grad, back_stats, final_grad = run_blocks(
        mix_back_kernel,
        steps,
        [node_count_arg, ("rows", final), ("rows", pre), ("rows", local_hat), ("rows", attend_hat)]
        + [("rows", mixed), ("rows", cotangent), branch_arg, ("whole", final_stats), gains_arg]
        + [("whole", hidden_weight), ("whole", output_weight)],
        [
            ("rows", (node_rows, width), LOW),
            ("rows", (node_rows, width), F32),
            ("whole", (hidden, width), F32),
            ("whole", (width, hidden), F32),
            ("whole", (8, hidden), F32),
            ("whole", (8, width), F32),
            ("whole", (8, width), F32),
        ],
    )
    back_stats = all_sum(back_stats, devices)
    back_arg = ("whole", back_stats)
    edge_out, node_part, gcn_grad, edge_grad = run_blocks(
        gcn_back_kernel,
        steps,
        [node_count_arg, ("rows", d_mixed), ("rows", local_hat), ("rows", inverse), ("rows", ratio)]
        + [("rows", gate), ("rows", sent), ("rows", slope), node_arg, edge_arg]
        + ends
        + [branch_arg, back_arg, gains_arg, ("whole", gcn_weight), ("whole", edge_weight)],
        [
            ("rows", (edge_rows, width), F32),
            ("rows", (node_rows, width), F32),
            ("whole", gcn_weight.shape, F32),
            ("whole", edge_weight.shape, F32),
        ],
        scratch=[
            pltpu.VMEM((node_rows // steps, 4 * width), LOW),
            pltpu.VMEM((edge_rows // steps, width), LOW),
        ],
    )
    node_out, attend_grad, attend_out_grad = run_blocks(
        attend_back_kernel,
        steps,
        [node_count_arg, ("rows", d_mixed), ("rows", attend_hat), ("rows", qkv), ("rows", probs)]
        + [("rows", attended), node_arg, ("rows", node_part), branch_arg, back_arg, gains_arg]
        + [("whole", attend_weight), ("whole", attend_out)],
        [
            ("rows", (node_rows, width), F32),
            ("whole", attend_weight.shape, F32),
            ("whole", attend_out.shape, F32),
        ],
        scratch=[pltpu.VMEM((node_rows // steps, 3 * width), LOW)],
    )
    gcn_grad, edge_grad, attend_grad, attend_out_grad, hidden_grad, bias_grad, output_grad = lax.psum(
        (gcn_grad, edge_grad, attend_grad, attend_out_grad, hidden_grad, bias_grad[0], output_grad),
        "graphs",
    )
    return (
        result,
        node_out,
        edge_out,
        gcn_grad,
        edge_grad,
        attend_grad,
        attend_out_grad,
        back_stats[1],
        back_stats[0],
        back_stats[2],
        back_stats[0],
        hidden_grad,
        bias_grad,
        output_grad,
        final_grad[0],
        final_grad[1],
    )


def solution(mesh):
    rows = P("graphs", None)
    each = P("graphs")
    return jax.shard_map(
        functools.partial(on_device, mesh.shape["graphs"]),
        mesh=mesh,
        in_specs=(rows, rows, each, each, rows, rows) + (P(),) * 13 + (rows,),
        out_specs=(rows, rows, rows) + (P(),) * 13,
        check_vma=False,
    )
```

```python
import functools

import jax
import jax.numpy as jnp
from jax import lax
from jax.experimental import pallas as pl
from jax.experimental.pallas import tpu as pltpu
from jax.sharding import PartitionSpec as P

HEAD_SIZE = 32
HALF = 128
GROUP = 8
EPS = 1e-05
F32 = jnp.float32
LOW = jnp.bfloat16
VMEM_BYTES = 60 * 1024 * 1024


def dot(left, right):
    return jnp.dot(left, right, preferred_element_type=F32)


def dot_nt(left, right):
    return lax.dot_general(left, right, (((1,), (1,)), ((), ())), preferred_element_type=F32)


def dot_tn(left, right):
    return lax.dot_general(left, right, (((0,), (0,)), ((), ())), preferred_element_type=F32)


def sigmoid(values):
    return 0.5 * jnp.tanh(0.5 * values) + 0.5


def norm_rows(total, squares, count):
    center = total / count
    return center, lax.rsqrt(squares / count - center * center + EPS)


def one_hot(index_row, slots):
    grid = lax.broadcasted_iota(jnp.int32, (slots, index_row.shape[1]), 0)
    return jnp.where(grid == index_row, 1.0, 0.0)


def end_hots(source_ref, target_ref, at, slots):
    ends = [one_hot(ref[at : at + 1, :], slots) for ref in (source_ref, target_ref)]
    return jnp.concatenate(ends, axis=0).astype(LOW)


def row_mask(counts, first, graphs, slots, width):
    grid = lax.broadcasted_iota(jnp.int32, (slots, width), 0)
    return jnp.concatenate(
        [jnp.where(grid < counts[first + at], 1.0, 0.0) for at in range(graphs)], axis=0
    )


def head_blocks(rows):
    head = lax.broadcasted_iota(jnp.int32, rows.shape, 1) // HEAD_SIZE
    wide = rows.astype(F32)
    return jnp.concatenate(
        [jnp.where(head == at, wide, 0.0).astype(LOW) for at in range(HALF // HEAD_SIZE)], axis=0
    )


def head_merge(stacked, slots):
    head = lax.broadcasted_iota(jnp.int32, (slots, HALF), 1) // HEAD_SIZE
    merged = stacked[:slots]
    for at in range(1, HALF // HEAD_SIZE):
        merged = jnp.where(head == at, stacked[at * slots : (at + 1) * slots], merged)
    return merged


def column_sum(values):
    return jnp.sum(values, axis=0, keepdims=True)


def add_rows(stat_ref, rows):
    for at, row in enumerate(rows):
        stat_ref[at : at + 1, :] += row


def forward_kernel(
    node_count,
    edge_count,
    node_ref,
    edge_ref,
    source_ref,
    target_ref,
    gcn_weight,
    edge_weight,
    attend_weight,
    attend_out,
    local_ref,
    attend_ref,
    inverse_ref,
    ratio_ref,
    gate_ref,
    sent_ref,
    slope_ref,
    qkv_ref,
    prob_ref,
    attended_ref,
    stat_ref,
):
    step = pl.program_id(0)
    first = step * GROUP
    width = node_ref.shape[1]
    slots = node_ref.shape[0] // GROUP
    edges = edge_ref.shape[0] // GROUP

    @pl.when(step == 0)
    def _():
        stat_ref[...] = jnp.zeros_like(stat_ref)

    node = node_ref[...]
    inputs = node.astype(F32)
    proj = dot(node, gcn_weight[...])
    parts = proj[:, width:].astype(LOW)
    edge_proj = dot(edge_ref[...], edge_weight[...])
    qkv = dot(node, attend_weight[...]).astype(LOW)
    qkv_ref[...] = qkv
    edge_grid = lax.broadcasted_iota(jnp.int32, (edges, width), 0)
    node_grid = lax.broadcasted_iota(jnp.int32, (slots, 2 * HALF), 0)
    nothing = jnp.zeros((slots, width), LOW)
    hots, gathered = [], []
    for at in range(GROUP):
        rows = slice(at * slots, (at + 1) * slots)
        hots.append(end_hots(source_ref, target_ref, at, slots))
        spread = jnp.concatenate(
            [
                jnp.concatenate([parts[rows, 2 * width :], parts[rows, :width]], axis=1),
                jnp.concatenate([parts[rows, width : 2 * width], nothing], axis=1),
            ],
            axis=0,
        )
        gathered.append(dot_tn(hots[at], spread))
    scores = {}
    for at in range(GROUP):
        rows = slice(at * slots, (at + 1) * slots)
        for half in range(width // HALF):
            query = qkv[rows, half * HALF : (half + 1) * HALF]
            key = qkv[rows, width + half * HALF : width + (half + 1) * HALF]
            scores[at, half] = dot_nt(key, head_blocks(query))
    messages = []
    for at in range(GROUP):
        edge_rows = slice(at * edges, (at + 1) * edges)
        sent = gathered[at][:, width:]
        edge_mask = jnp.where(edge_grid < edge_count[first + at], 1.0, 0.0)
        gate_sig = sigmoid(edge_proj[edge_rows] + gathered[at][:, :width])
        kept = gate_sig * edge_mask
        gate = kept.astype(LOW)
        gate_ref[edge_rows, :] = gate
        sent_ref[edge_rows, :] = sent.astype(LOW)
        slope_ref[edge_rows, :] = (kept * (1.0 - gate_sig)).astype(LOW)
        message = (gate.astype(F32) * sent).astype(LOW)
        messages.append(jnp.concatenate([message, gate], axis=1))
    pooled = [dot(hots[at][slots:], messages[at]) for at in range(GROUP)]
    probs = {}
    for at in range(GROUP):
        rows = slice(at * slots, (at + 1) * slots)
        key_kept = node_grid < node_count[first + at]
        for half in range(width // HALF):
            held = jnp.where(key_kept, scores[at, half] * HEAD_SIZE ** (-0.5), -1e30)
            expo = jnp.exp(held - jnp.max(held, axis=0, keepdims=True))
            probs[at, half] = (expo / column_sum(expo)).astype(LOW)
            prob_ref[rows, half * 2 * HALF : (half + 1) * 2 * HALF] = probs[at, half]
    spreads = {}
    for at in range(GROUP):
        rows = slice(at * slots, (at + 1) * slots)
        for half in range(width // HALF):
            value = qkv[rows, 2 * width + half * HALF : 2 * width + (half + 1) * HALF]
            spreads[at, half] = dot_tn(probs[at, half], value)
    for at in range(GROUP):
        rows = slice(at * slots, (at + 1) * slots)
        inverse = 1.0 / (pooled[at][:, width:] + 1e-06)
        ratio = pooled[at][:, :width] * inverse
        inverse_ref[rows, :] = inverse
        ratio_ref[rows, :] = ratio
        local_ref[rows, :] = inputs[rows] + proj[rows, :width] + ratio
    for at in range(GROUP):
        rows = slice(at * slots, (at + 1) * slots)
        for half in range(width // HALF):
            merged = head_merge(spreads[at, half], slots)
            attended_ref[rows, half * HALF : (half + 1) * HALF] = merged.astype(LOW)
    attend_pre = inputs + dot(attended_ref[...], attend_out[...])
    attend_ref[...] = attend_pre
    local_pre = local_ref[...]
    mask = row_mask(node_count, first, GROUP, slots, width)
    local_kept = mask * local_pre
    attend_kept = mask * attend_pre
    add_rows(
        stat_ref,
        (
            column_sum(local_kept),
            column_sum(local_kept * local_pre),
            column_sum(attend_kept),
            column_sum(attend_kept * attend_pre),
            column_sum(mask),
        ),
    )


def mix_kernel(
    node_count,
    local_ref,
    attend_ref,
    cotangent_ref,
    branch_stats,
    gains,
    hidden_weight,
    hidden_bias,
    output_weight,
    local_hat_ref,
    attend_hat_ref,
    mixed_ref,
    pre_ref,
    final_ref,
    stat_ref,
):
    step = pl.program_id(0)
    first = step * GROUP
    width = local_ref.shape[1]
    slots = local_ref.shape[0] // GROUP

    @pl.when(step == 0)
    def _():
        stat_ref[...] = jnp.zeros_like(stat_ref)

    count = branch_stats[4:5, :]
    local_center, local_inv = norm_rows(branch_stats[0:1, :], branch_stats[1:2, :], count)
    attend_center, attend_inv = norm_rows(branch_stats[2:3, :], branch_stats[3:4, :], count)
    local_hat = (local_ref[...] - local_center) * local_inv
    attend_hat = (attend_ref[...] - attend_center) * attend_inv
    local_hat_ref[...] = local_hat.astype(LOW)
    attend_hat_ref[...] = attend_hat.astype(LOW)
    scaled = local_hat * gains[0:1, :] + attend_hat * gains[2:3, :]
    mixed = (scaled + (gains[1:2, :] + gains[3:4, :])).astype(LOW)
    mixed_ref[...] = mixed
    pre = dot(mixed, hidden_weight[...]) + hidden_bias[...]
    pre_ref[...] = pre.astype(LOW)
    final = scaled + dot((pre * sigmoid(pre)).astype(LOW), output_weight[...])
    final_ref[...] = final
    mask = row_mask(node_count, first, GROUP, slots, width)
    kept = mask * final
    up = mask * cotangent_ref[...].astype(F32)
    add_rows(
        stat_ref,
        (column_sum(kept), column_sum(kept * final), column_sum(up), column_sum(up * final)),
    )


def mix_back_kernel(
    node_count,
    final_ref,
    pre_ref,
    local_hat_ref,
    attend_hat_ref,
    mixed_ref,
    cotangent_ref,
    branch_stats,
    final_stats,
    gains,
    hidden_weight,
    output_weight,
    result_ref,
    d_mixed_ref,
    weight_grad,
    stat_ref,
    final_grad,
):
    step = pl.program_id(0)
    first = step * GROUP
    width = final_ref.shape[1]
    slots = final_ref.shape[0] // GROUP
    count = branch_stats[4:5, :]
    center, inv = norm_rows(final_stats[0:1, :], final_stats[1:2, :], count)
    shift_grad = final_stats[2:3, :]
    gain_grad = inv * (final_stats[3:4, :] - center * shift_grad)

    @pl.when(step == 0)
    def _():
        stat_ref[...] = jnp.zeros_like(stat_ref)
        weight_grad[...] = jnp.zeros_like(weight_grad)
        final_grad[...] = jnp.zeros_like(final_grad)
        final_grad[0:1, :] = gain_grad
        final_grad[1:2, :] = shift_grad

    mask = row_mask(node_count, first, GROUP, slots, width)
    final_hat = (final_ref[...] - center) * inv
    result_ref[...] = (mask * (final_hat * gains[4:5, :] + gains[5:6, :])).astype(LOW)
    per_node = 1.0 / count
    d_final = (inv * gains[4:5, :]) * (
        mask
        * (
            cotangent_ref[...].astype(F32)
            - (shift_grad * per_node + final_hat * (gain_grad * per_node))
        )
    )
    d_branch = d_final.astype(LOW)
    pre = pre_ref[...].astype(F32)
    sig = sigmoid(pre)
    act = (pre * sig).astype(LOW)
    weight_grad[2 * width :, :] += dot_tn(act, d_branch)
    d_pre_wide = dot_nt(d_branch, output_weight[...]) * (sig * (1.0 + pre * (1.0 - sig)))
    d_pre = d_pre_wide.astype(LOW)
    mixed = mixed_ref[...]
    for at in range(2):
        weight_grad[at * width : (at + 1) * width, :] += dot_tn(
            mixed, d_pre[:, at * width : (at + 1) * width]
        )
    bias_sum = column_sum(d_pre.astype(F32))
    d_mixed = d_final + dot_nt(d_pre, hidden_weight[...])
    d_mixed_ref[...] = d_mixed
    add_rows(
        stat_ref,
        (
            column_sum(d_mixed),
            column_sum(d_mixed * local_hat_ref[...].astype(F32)),
            column_sum(d_mixed * attend_hat_ref[...].astype(F32)),
            bias_sum[:, :width],
            bias_sum[:, width:],
        ),
    )


def branch_back(d_mixed, hat, mask, scale, shift_grad, gain_grad, count):
    per_node = 1.0 / count
    return scale * (d_mixed - mask * (shift_grad * per_node + hat * (gain_grad * per_node)))


def gcn_back_kernel(
    node_count,
    d_mixed_ref,
    local_hat_ref,
    inverse_ref,
    ratio_ref,
    gate_ref,
    sent_ref,
    slope_ref,
    node_ref,
    edge_ref,
    source_ref,
    target_ref,
    branch_stats,
    back_stats,
    gains,
    gcn_weight,
    edge_weight,
    edge_out_ref,
    node_part_ref,
    weight_grad,
    d_proj,
    d_hats,
):
    step = pl.program_id(0)
    first = step * GROUP
    width = node_ref.shape[1]
    slots = node_ref.shape[0] // GROUP
    edges = edge_ref.shape[0] // GROUP

    @pl.when(step == 0)
    def _():
        weight_grad[...] = jnp.zeros_like(weight_grad)

    count = branch_stats[4:5, :]
    _, inv = norm_rows(branch_stats[0:1, :], branch_stats[1:2, :], count)
    mask = row_mask(node_count, first, GROUP, slots, width)
    d_local = branch_back(
        d_mixed_ref[...],
        local_hat_ref[...].astype(F32),
        mask,
        inv * gains[0:1, :],
        back_stats[0:1, :],
        back_stats[1:2, :],
        count,
    )
    numer = d_local * inverse_ref[...]
    d_denom = (-numer * ratio_ref[...]).astype(LOW)
    d_numer = numer.astype(LOW)
    d_proj[:, :width] = d_local.astype(LOW)
    hots = [end_hots(source_ref, target_ref, at, slots) for at in range(GROUP)]
    backs = []
    for at in range(GROUP):
        rows = slice(at * slots, (at + 1) * slots)
        pair = jnp.concatenate([d_numer[rows], d_denom[rows]], axis=1)
        backs.append(dot_tn(hots[at][slots:], pair))
    pairs = []
    for at in range(GROUP):
        edge_rows = slice(at * edges, (at + 1) * edges)
        d_message = backs[at][:, :width]
        d_gate = backs[at][:, width:] + d_message * sent_ref[edge_rows, :].astype(F32)
        d_sent = (d_message * gate_ref[edge_rows, :].astype(F32)).astype(LOW)
        d_hat = (d_gate * slope_ref[edge_rows, :].astype(F32)).astype(LOW)
        d_hats[edge_rows, :] = d_hat
        pairs.append(jnp.concatenate([d_sent, d_hat], axis=1))
    pulls = [dot(hots[at], pairs[at]) for at in range(GROUP)]
    for at in range(GROUP):
        rows = slice(at * slots, (at + 1) * slots)
        pulled = pulls[at].astype(LOW)
        d_proj[rows, width : 2 * width] = pulled[:slots, :width]
        d_proj[rows, 2 * width : 3 * width] = pulled[slots:, width:]
        d_proj[rows, 3 * width :] = pulled[:slots, width:]
    weight_grad[4 * width :, :] += dot_tn(edge_ref[...], d_hats[...])
    edge_out_ref[...] = dot_nt(d_hats[...], edge_weight[...])
    for at in range(4):
        columns = slice(at * width, (at + 1) * width)
        weight_grad[columns, :] += dot_tn(node_ref[...], d_proj[:, columns])
    node_part_ref[...] = d_local + dot_nt(d_proj[...], gcn_weight[...])


def attend_back_kernel(
    node_count,
    d_mixed_ref,
    attend_hat_ref,
    qkv_ref,
    prob_ref,
    attended_ref,
    node_ref,
    node_part_ref,
    branch_stats,
    back_stats,
    gains,
    attend_weight,
    attend_out,
    node_out_ref,
    weight_grad,
    d_qkv,
):
    step = pl.program_id(0)
    first = step * GROUP
    width = node_ref.shape[1]
    slots = node_ref.shape[0] // GROUP

    @pl.when(step == 0)
    def _():
        weight_grad[...] = jnp.zeros_like(weight_grad)

    count = branch_stats[4:5, :]
    _, inv = norm_rows(branch_stats[2:3, :], branch_stats[3:4, :], count)
    mask = row_mask(node_count, first, GROUP, slots, width)
    d_attend = branch_back(
        d_mixed_ref[...],
        attend_hat_ref[...].astype(F32),
        mask,
        inv * gains[2:3, :],
        back_stats[0:1, :],
        back_stats[2:3, :],
        count,
    )
    d_attn = d_attend.astype(LOW)
    weight_grad[3 * width :, :] += dot_tn(attended_ref[...], d_attn)
    d_att = dot_nt(d_attn, attend_out[...]).astype(LOW)
    scale = HEAD_SIZE ** (-0.5)
    pieces = [(at, half) for at in range(GROUP) for half in range(width // HALF)]

    def place(at, half, part=0):
        first_lane = part * width + half * HALF
        return slice(at * slots, (at + 1) * slots), slice(first_lane, first_lane + HALF)

    def prob_place(at, half):
        return slice(at * slots, (at + 1) * slots), slice(half * 2 * HALF, (half + 1) * 2 * HALF)

    d_att_blocks = {key: head_blocks(d_att[place(*key)]) for key in pieces}
    d_probs = {key: dot_nt(qkv_ref[place(*key, 2)], d_att_blocks[key]) for key in pieces}
    for key in pieces:
        d_values = dot(prob_ref[prob_place(*key)], d_att_blocks[key])
        d_qkv[place(*key, 2)] = d_values.astype(LOW)
    d_scores = {}
    for key in pieces:
        probs = prob_ref[prob_place(*key)].astype(F32)
        weighted = probs * d_probs[key]
        d_scores[key] = (weighted - probs * column_sum(weighted)).astype(LOW)
    for key in pieces:
        d_keys = dot(d_scores[key], head_blocks(qkv_ref[place(*key)]))
        d_qkv[place(*key, 1)] = (d_keys * scale).astype(LOW)
    stacks = {key: dot_tn(d_scores[key], qkv_ref[place(*key, 1)]) for key in pieces}
    for key in pieces:
        d_qkv[place(*key)] = (head_merge(stacks[key], slots) * scale).astype(LOW)
    for at in range(3):
        columns = slice(at * width, (at + 1) * width)
        weight_grad[columns, :] += dot_tn(node_ref[...], d_qkv[:, columns])
    node_out_ref[...] = node_part_ref[...] + d_attend + dot_nt(d_qkv[...], attend_weight[...])


def run_blocks(kernel, steps, args, outs, scratch=(), flops=0):
    def spec(kind, shape):
        if kind == "scalar":
            return pl.BlockSpec(memory_space=pltpu.SMEM)
        if kind == "rows":
            return pl.BlockSpec((shape[0] // steps, shape[1]), lambda step: (step, 0))
        return pl.BlockSpec(shape, lambda step: (0,) * len(shape))

    moved = sum(item.size * item.dtype.itemsize for _, item in args)
    shapes = [jax.ShapeDtypeStruct(shape, dtype) for _, shape, dtype in outs]
    moved += sum(item.size * item.dtype.itemsize for item in shapes)
    return pl.pallas_call(
        kernel,
        grid=(steps,),
        in_specs=[spec(kind, item.shape) for kind, item in args],
        out_specs=[spec(kind, shape) for kind, shape, _ in outs],
        out_shape=shapes,
        scratch_shapes=list(scratch),
        compiler_params=pltpu.CompilerParams(
            dimension_semantics=("arbitrary",), vmem_limit_bytes=VMEM_BYTES
        ),
        cost_estimate=pl.CostEstimate(flops=flops, bytes_accessed=moved, transcendentals=0),
    )(*[item for _, item in args])


def all_sum(values, devices):
    other = lax.ppermute(values, "graphs", [(at, at ^ 1) for at in range(devices)])
    values = values + other
    chips = devices // 2
    sent = jnp.broadcast_to(values[None], (chips,) + values.shape)
    groups = [list(range(core, devices, 2)) for core in range(2)]
    return jnp.sum(lax.all_to_all(sent, "graphs", 0, 0, axis_index_groups=groups), axis=0)


def swap(values, mask, devices):
    return lax.ppermute(values, "graphs", [(at, at ^ mask) for at in range(devices)])


def side(mask):
    return (lax.axis_index("graphs") // mask) % 2


def keep_half(values, mask, devices):
    pair = values.reshape((2, values.shape[0] // 2) + values.shape[1:])
    mine = lax.dynamic_index_in_dim(pair, side(mask), 0, keepdims=False)
    other = lax.dynamic_index_in_dim(pair, 1 - side(mask), 0, keepdims=False)
    return mine + swap(other, mask, devices)


def join_halves(values, mask, devices):
    other = swap(values, mask, devices)
    lower = side(mask) == 0
    return jnp.where(
        lower, jnp.concatenate([values, other]), jnp.concatenate([other, values])
    )


def weight_sums(stacks, devices):
    halves = jnp.concatenate([keep_half(stack, 1, devices) for stack in stacks])
    masks = [1 << bit for bit in range(1, devices.bit_length() - 1)]
    orders = [masks, masks[1::-1] + masks[2:]]
    unit = 2 ** len(masks) * 8
    cut = -(-halves.shape[0] // (2 * unit)) * unit
    parts = [halves[:cut], halves[cut:]]
    for at in range(len(masks)):
        parts = [keep_half(part, order[at], devices) for part, order in zip(parts, orders)]
    for at in reversed(range(len(masks))):
        parts = [join_halves(part, order[at], devices) for part, order in zip(parts, orders)]
    others = [swap(part, 1, devices) for part in parts]
    lower = side(1) == 0
    first = [jnp.where(lower, mine, other) for mine, other in zip(parts, others)]
    second = [jnp.where(lower, other, mine) for mine, other in zip(parts, others)]
    first, second = jnp.concatenate(first), jnp.concatenate(second)
    totals, at = [], 0
    for stack in stacks:
        rows = stack.shape[0] // 2
        totals.append(jnp.concatenate([first[at : at + rows], second[at : at + rows]]))
        at += rows
    return totals


def unstack(totals, shapes):
    arrays = []
    for stack, pair in zip(totals, (shapes[:2], shapes[2:4], shapes[4:])):
        width, at = stack.shape[1], 0
        for rows, columns in pair:
            if rows == width:
                blocks = [stack[at + i * width : at + (i + 1) * width] for i in range(columns // width)]
                arrays.append(jnp.concatenate(blocks, axis=1))
            else:
                arrays.append(stack[at : at + rows])
            at += rows * columns // width
    return arrays


def on_device(
    devices,
    node_input,
    edge_input,
    node_count,
    edge_count,
    edge_source,
    edge_target,
    gcn_weight,
    edge_weight,
    attend_weight,
    attend_out,
    local_gain,
    local_shift,
    attend_gain,
    attend_shift,
    hidden_weight,
    hidden_bias,
    output_weight,
    final_gain,
    final_shift,
    cotangent,
):
    graphs, edges = edge_source.shape
    node_rows, width = node_input.shape
    edge_rows = edge_input.shape[0]
    slots = node_rows // graphs
    hidden = hidden_weight.shape[1]
    steps = graphs // GROUP
    gains = jnp.stack(
        [local_gain, local_shift, attend_gain, attend_shift, final_gain, final_shift, final_gain, final_shift]
    )
    node_count_arg = ("scalar", node_count)
    node_arg = ("rows", node_input)
    edge_arg = ("rows", edge_input)
    ends = [("rows", edge_source), ("rows", edge_target)]
    gains_arg = ("whole", gains)
    (
        local_pre,
        attend_pre,
        inverse,
        ratio,
        gate,
        sent,
        slope,
        qkv,
        probs,
        attended,
        branch_stats,
    ) = run_blocks(
        forward_kernel,
        steps,
        [node_count_arg, ("scalar", edge_count), node_arg, edge_arg]
        + ends
        + [("whole", item) for item in (gcn_weight, edge_weight, attend_weight, attend_out)],
        [
            ("rows", (node_rows, width), F32),
            ("rows", (node_rows, width), F32),
            ("rows", (node_rows, width), F32),
            ("rows", (node_rows, width), F32),
            ("rows", (edge_rows, width), LOW),
            ("rows", (edge_rows, width), LOW),
            ("rows", (edge_rows, width), LOW),
            ("rows", (node_rows, 3 * width), LOW),
            ("rows", (node_rows, (width // HEAD_SIZE) * slots), LOW),
            ("rows", (node_rows, width), LOW),
            ("whole", (8, width), F32),
        ],
    )
    branch_stats = all_sum(branch_stats, devices)
    branch_arg = ("whole", branch_stats)
    local_hat, attend_hat, mixed, pre, final, final_stats = run_blocks(
        mix_kernel,
        steps,
        [node_count_arg, ("rows", local_pre), ("rows", attend_pre), ("rows", cotangent)]
        + [branch_arg, gains_arg, ("whole", hidden_weight), ("whole", hidden_bias[None])]
        + [("whole", output_weight)],
        [
            ("rows", (node_rows, width), LOW),
            ("rows", (node_rows, width), LOW),
            ("rows", (node_rows, width), LOW),
            ("rows", (node_rows, hidden), LOW),
            ("rows", (node_rows, width), F32),
            ("whole", (8, width), F32),
        ],
    )
    final_stats = all_sum(final_stats, devices)
    result, d_mixed, mix_grads, back_stats, final_grad = run_blocks(
        mix_back_kernel,
        steps,
        [node_count_arg, ("rows", final), ("rows", pre), ("rows", local_hat), ("rows", attend_hat)]
        + [("rows", mixed), ("rows", cotangent), branch_arg, ("whole", final_stats), gains_arg]
        + [("whole", hidden_weight), ("whole", output_weight)],
        [
            ("rows", (node_rows, width), LOW),
            ("rows", (node_rows, width), F32),
            ("whole", (2 * hidden, width), F32),
            ("whole", (8, width), F32),
            ("whole", (8, width), F32),
        ],
    )
    back_stats = all_sum(back_stats, devices)
    back_arg = ("whole", back_stats)
    edge_out, node_part, gcn_grads = run_blocks(
        gcn_back_kernel,
        steps,
        [node_count_arg, ("rows", d_mixed), ("rows", local_hat), ("rows", inverse), ("rows", ratio)]
        + [("rows", gate), ("rows", sent), ("rows", slope), node_arg, edge_arg]
        + ends
        + [branch_arg, back_arg, gains_arg, ("whole", gcn_weight), ("whole", edge_weight)],
        [
            ("rows", (edge_rows, width), F32),
            ("rows", (node_rows, width), F32),
            ("whole", (5 * width, width), F32),
        ],
        scratch=[
            pltpu.VMEM((node_rows // steps, 4 * width), LOW),
            pltpu.VMEM((edge_rows // steps, width), LOW),
        ],
    )
    node_out, attend_grads = run_blocks(
        attend_back_kernel,
        steps,
        [node_count_arg, ("rows", d_mixed), ("rows", attend_hat), ("rows", qkv), ("rows", probs)]
        + [("rows", attended), node_arg, ("rows", node_part), branch_arg, back_arg, gains_arg]
        + [("whole", attend_weight), ("whole", attend_out)],
        [
            ("rows", (node_rows, width), F32),
            ("whole", (4 * width, width), F32),
        ],
        scratch=[pltpu.VMEM((node_rows // steps, 3 * width), LOW)],
    )
    totals = weight_sums((mix_grads, gcn_grads, attend_grads), devices)
    hidden_grad, output_grad, gcn_grad, edge_grad, attend_grad, attend_out_grad = unstack(
        totals,
        [hidden_weight.shape, output_weight.shape, gcn_weight.shape]
        + [edge_weight.shape, attend_weight.shape, attend_out.shape],
    )
    return (
        result,
        node_out,
        edge_out,
        gcn_grad,
        edge_grad,
        attend_grad,
        attend_out_grad,
        back_stats[1],
        back_stats[0],
        back_stats[2],
        back_stats[0],
        hidden_grad,
        back_stats[3:5].reshape(-1),
        output_grad,
        final_grad[0],
        final_grad[1],
    )


def solution(mesh):
    rows = P("graphs", None)
    each = P("graphs")
    return jax.shard_map(
        functools.partial(on_device, mesh.shape["graphs"]),
        mesh=mesh,
        in_specs=(rows, rows, each, each, rows, rows) + (P(),) * 13 + (rows,),
        out_specs=(rows, rows, rows) + (P(),) * 13,
        check_vma=False,
    )
```

```python
import functools
import math

import jax
import jax.numpy as jnp
from jax import lax
from jax.experimental import pallas as pl
from jax.experimental.pallas import tpu as pltpu
from jax.sharding import PartitionSpec as P

HEAD_SIZE = 32
HALF = 128
EXP2_SCALE = HEAD_SIZE ** (-0.5) / math.log(2.0)
GROUP = 8
MIX_GROUP = 16
PARTS = 4
EPS = 1e-05
F32 = jnp.float32
LOW = jnp.bfloat16
MIB = 1024 * 1024


def dot(left, right):
    return jnp.dot(left, right, preferred_element_type=F32)


def dot_nt(left, right):
    return lax.dot_general(left, right, (((1,), (1,)), ((), ())), preferred_element_type=F32)


def dot_tn(left, right):
    return lax.dot_general(left, right, (((0,), (0,)), ((), ())), preferred_element_type=F32)


def sigmoid(values):
    return 0.5 * jnp.tanh(0.5 * values) + 0.5


def norm_rows(total, squares, count):
    center = total / count
    return center, lax.rsqrt(squares / count - center * center + EPS)


def one_hot(index_row, slots):
    grid = lax.broadcasted_iota(jnp.int32, (slots, index_row.shape[1]), 0)
    return jnp.where(grid == index_row, 1.0, 0.0)


def end_hots(source_ref, target_ref, at, slots):
    ends = [one_hot(ref[at : at + 1, :], slots) for ref in (source_ref, target_ref)]
    return jnp.concatenate(ends, axis=0).astype(LOW)


def row_mask(counts, first, graphs, slots, width):
    grid = lax.broadcasted_iota(jnp.int32, (slots, width), 0)
    return jnp.concatenate(
        [jnp.where(grid < counts[first + at], 1.0, 0.0) for at in range(graphs)], axis=0
    )


def head_masks(slots):
    head = lax.broadcasted_iota(jnp.int32, (slots, HALF), 1) // HEAD_SIZE
    flat = [jnp.where(head == at, 1.0, 0.0).astype(LOW) for at in range(HALF // HEAD_SIZE)]
    row = lax.broadcasted_iota(jnp.int32, (HALF, 2 * slots), 0) // HEAD_SIZE
    lane = lax.broadcasted_iota(jnp.int32, (HALF, 2 * slots), 1) // slots
    tall = [jnp.where(row == lane + at, 1.0, 0.0).astype(LOW) for at in range(0, HALF // HEAD_SIZE, 2)]
    return flat, tall


def head_blocks(rows, masks):
    return jnp.concatenate([rows * mask for mask in masks[0]], axis=0)


def head_blocks_t(rows, masks):
    turned = rows.T
    twice = jnp.concatenate([turned, turned], axis=1)
    return jnp.concatenate([twice * mask for mask in masks[1]], axis=1)


def heads_turn(wide, slots):
    pairs = [wide[:, at : at + 2 * slots].T for at in range(0, wide.shape[1], 2 * slots)]
    return jnp.concatenate(
        [part for pair in pairs for part in (pair[:slots], pair[slots:])], axis=1
    )


def head_merge(stacked, slots):
    head = lax.broadcasted_iota(jnp.int32, (slots, HALF), 1) // HEAD_SIZE
    merged = stacked[:slots]
    for at in range(1, HALF // HEAD_SIZE):
        merged = jnp.where(head == at, stacked[at * slots : (at + 1) * slots], merged)
    return merged


def column_sum(values):
    return jnp.sum(values, axis=0, keepdims=True)


def add_rows(stats, rows):
    for at, row in enumerate(rows):
        stats[at : at + 1, :] += row


def send_rows(stats, sent_ref):
    @pl.when(pl.program_id(0) == pl.num_programs(0) - 1)
    def _():
        rows = sent_ref.shape[2] // stats.shape[1]
        line = jnp.concatenate([stats[at : at + 1, :] for at in range(rows)], axis=1)
        sent_ref[...] = jnp.broadcast_to(line[None], sent_ref.shape)


def sum_rows(sent_ref, stats):
    line = jnp.sum(sent_ref[...], axis=0)
    width = stats.shape[1]
    for at in range(line.shape[1] // width):
        stats[at : at + 1, :] = line[:, at * width : (at + 1) * width]


def held_rows(step, rows):
    return pl.ds(pl.multiple_of(step * rows, rows), rows)


def forward_kernel(
    node_count,
    edge_count,
    node_ref,
    edge_ref,
    source_ref,
    target_ref,
    gcn_weight,
    edge_weight,
    attend_weight,
    attend_out,
    local_ref,
    attend_ref,
    inverse_ref,
    ratio_ref,
    gate_ref,
    sent_ref,
    slope_ref,
    qkv_ref,
    prob_ref,
    attended_ref,
    sent_stats,
    stats,
):
    step = pl.program_id(0)
    first = step * GROUP
    width = node_ref.shape[1]
    slots = node_ref.shape[0] // GROUP
    edges = edge_ref.shape[0] // GROUP

    @pl.when(step == 0)
    def _():
        stats[...] = jnp.zeros_like(stats)

    node = node_ref[...]
    inputs = node.astype(F32)
    proj = dot(node, gcn_weight[...])
    parts = proj[:, width:].astype(LOW)
    edge_proj = dot(edge_ref[...], edge_weight[...])
    qkv = dot(node, attend_weight[...]).astype(LOW)
    qkv_ref[...] = qkv
    edge_grid = lax.broadcasted_iota(jnp.int32, (edges, width), 0)
    node_grid = lax.broadcasted_iota(jnp.int32, (slots, 2 * HALF), 0)
    nothing = jnp.zeros((slots, width), LOW)
    hots, gathered = [], []
    for at in range(GROUP):
        rows = slice(at * slots, (at + 1) * slots)
        hots.append(end_hots(source_ref, target_ref, at, slots))
        spread = jnp.concatenate(
            [
                jnp.concatenate([parts[rows, 2 * width :], parts[rows, :width]], axis=1),
                jnp.concatenate([parts[rows, width : 2 * width], nothing], axis=1),
            ],
            axis=0,
        )
        gathered.append(dot_tn(hots[at], spread))
    masks = head_masks(slots)
    scores = {}
    for at in range(GROUP):
        rows = slice(at * slots, (at + 1) * slots)
        for half in range(width // HALF):
            query = qkv[rows, half * HALF : (half + 1) * HALF]
            key = qkv[rows, width + half * HALF : width + (half + 1) * HALF]
            scores[at, half] = dot(key, head_blocks_t(query, masks))
    messages = []
    for at in range(GROUP):
        edge_rows = slice(at * edges, (at + 1) * edges)
        sent = gathered[at][:, width:]
        gate_sig = sigmoid(edge_proj[edge_rows] + gathered[at][:, :width])
        kept = jnp.where(edge_grid < edge_count[first + at], gate_sig, 0.0)
        gate = kept.astype(LOW)
        gate_ref[edge_rows, :] = gate
        sent_ref[edge_rows, :] = sent.astype(LOW)
        slope_ref[edge_rows, :] = (kept * (1.0 - gate_sig)).astype(LOW)
        message = (gate.astype(F32) * sent).astype(LOW)
        messages.append(jnp.concatenate([message, gate], axis=1))
    pooled = [dot(hots[at][slots:], messages[at]) for at in range(GROUP)]
    probs = {}
    for at in range(GROUP):
        rows = slice(at * slots, (at + 1) * slots)
        key_kept = node_grid < node_count[first + at]
        for half in range(width // HALF):
            shown = jnp.where(key_kept, scores[at, half], -1e30)
            expo = jnp.exp2((shown - jnp.max(shown, axis=0, keepdims=True)) * EXP2_SCALE)
            probs[at, half] = (expo * (1.0 / column_sum(expo))).astype(LOW)
            prob_ref[rows, half * 2 * HALF : (half + 1) * 2 * HALF] = probs[at, half]
    spreads = {}
    for at in range(GROUP):
        rows = slice(at * slots, (at + 1) * slots)
        for half in range(width // HALF):
            value = qkv[rows, 2 * width + half * HALF : 2 * width + (half + 1) * HALF]
            spreads[at, half] = dot_tn(probs[at, half], value)
    local_pres = []
    for at in range(GROUP):
        rows = slice(at * slots, (at + 1) * slots)
        inverse = 1.0 / (pooled[at][:, width:] + 1e-06)
        ratio = pooled[at][:, :width] * inverse
        inverse_ref[rows, :] = inverse.astype(LOW)
        ratio_ref[rows, :] = ratio.astype(LOW)
        local_pres.append(inputs[rows] + proj[rows, :width] + ratio)
    for at in range(GROUP):
        rows = slice(at * slots, (at + 1) * slots)
        for half in range(width // HALF):
            merged = head_merge(spreads[at, half], slots)
            attended_ref[rows, half * HALF : (half + 1) * HALF] = merged.astype(LOW)
    attend_pre = inputs + dot(attended_ref[...], attend_out[...])
    attend_ref[...] = attend_pre
    local_pre = jnp.concatenate(local_pres, axis=0)
    local_ref[...] = local_pre
    mask = row_mask(node_count, first, GROUP, slots, width)
    local_kept = mask * local_pre
    attend_kept = mask * attend_pre
    add_rows(
        stats,
        (
            column_sum(local_kept),
            column_sum(local_kept * local_pre),
            column_sum(attend_kept),
            column_sum(attend_kept * attend_pre),
            column_sum(mask),
        ),
    )
    send_rows(stats, sent_stats)


def mix_kernel(
    node_count,
    local_ref,
    attend_ref,
    cotangent_ref,
    sent_branch,
    gains,
    hidden_weight,
    hidden_bias,
    output_weight,
    local_hat_ref,
    attend_hat_ref,
    mixed_ref,
    pre_ref,
    final_ref,
    branch_stats,
    sent_stats,
    stats,
):
    step = pl.program_id(0)
    first = step * MIX_GROUP
    rows, width = cotangent_ref.shape
    slots = rows // MIX_GROUP

    @pl.when(step == 0)
    def _():
        stats[...] = jnp.zeros_like(stats)
        sum_rows(sent_branch, branch_stats)

    count = branch_stats[4:5, :]
    local_center, local_inv = norm_rows(branch_stats[0:1, :], branch_stats[1:2, :], count)
    attend_center, attend_inv = norm_rows(branch_stats[2:3, :], branch_stats[3:4, :], count)
    part, graphs = rows // PARTS, MIX_GROUP // PARTS
    owns = [slice(at * part, (at + 1) * part) for at in range(PARTS)]
    places = [held_rows(step * PARTS + at, part) for at in range(PARTS)]
    scaled, pres = [], []
    for own, place in zip(owns, places):
        local_hat = (local_ref[own, :] - local_center) * local_inv
        attend_hat = (attend_ref[own, :] - attend_center) * attend_inv
        local_hat_ref[place, :] = local_hat.astype(LOW)
        attend_hat_ref[place, :] = attend_hat.astype(LOW)
        scaled.append(local_hat * gains[0:1, :] + attend_hat * gains[2:3, :])
        mixed = (scaled[-1] + (gains[1:2, :] + gains[3:4, :])).astype(LOW)
        mixed_ref[place, :] = mixed
        pres.append(dot(mixed, hidden_weight[...]))
    finals = []
    for at, own in enumerate(owns):
        pre = pres[at] + hidden_bias[...]
        pre_ref[own, :] = pre.astype(LOW)
        act = (pre * sigmoid(pre)).astype(LOW)
        finals.append(scaled[at] + dot(act, output_weight[...]))
    for at, own in enumerate(owns):
        final = finals[at]
        final_ref[own, :] = final
        mask = row_mask(node_count, first + at * graphs, graphs, slots, width)
        kept = mask * final
        up = mask * cotangent_ref[own, :].astype(F32)
        add_rows(
            stats,
            (column_sum(kept), column_sum(kept * final), column_sum(up), column_sum(up * final)),
        )
    send_rows(stats, sent_stats)


def mix_back_kernel(
    node_count,
    final_ref,
    pre_ref,
    local_hat_ref,
    attend_hat_ref,
    mixed_ref,
    cotangent_ref,
    branch_stats,
    sent_final,
    gains,
    hidden_weight,
    output_weight,
    d_mixed_ref,
    result_ref,
    weight_grad,
    final_sums,
    sent_stats,
    stats,
):
    step = pl.program_id(0)
    first = step * MIX_GROUP
    rows, width = cotangent_ref.shape
    slots = rows // MIX_GROUP

    @pl.when(step == 0)
    def _():
        stats[...] = jnp.zeros_like(stats)
        weight_grad[...] = jnp.zeros_like(weight_grad)
        sum_rows(sent_final, final_sums)

    count = branch_stats[4:5, :]
    per_node = 1.0 / count
    center, inv = norm_rows(final_sums[0:1, :], final_sums[1:2, :], count)
    shift_grad = final_sums[2:3, :]
    gain_grad = inv * (final_sums[3:4, :] - center * shift_grad)
    final_sums[4:5, :] = gain_grad
    part, graphs = rows // PARTS, MIX_GROUP // PARTS
    owns = [slice(at * part, (at + 1) * part) for at in range(PARTS)]
    places = [held_rows(step * PARTS + at, part) for at in range(PARTS)]
    d_finals, d_branches, d_acts = [], [], []
    for at, own in enumerate(owns):
        mask = row_mask(node_count, first + at * graphs, graphs, slots, width)
        final_hat = (final_ref[own, :] - center) * inv
        result_ref[own, :] = (mask * (final_hat * gains[4:5, :] + gains[5:6, :])).astype(LOW)
        pulled = shift_grad * per_node + final_hat * (gain_grad * per_node)
        d_finals.append(
            (inv * gains[4:5, :]) * (mask * (cotangent_ref[own, :].astype(F32) - pulled))
        )
        d_branches.append(d_finals[-1].astype(LOW))
        d_acts.append(dot_nt(d_branches[-1], output_weight[...]))
    acts, d_pres, bias_sums = [], [], []
    for at, own in enumerate(owns):
        pre = pre_ref[own, :].astype(F32)
        sig = sigmoid(pre)
        acts.append((pre * sig).astype(LOW))
        d_pres.append((d_acts[at] * (sig * (1.0 + pre * (1.0 - sig)))).astype(LOW))
        bias_sums.append(column_sum(d_pres[-1].astype(F32)))
    backs = [dot_nt(d_pre, hidden_weight[...]) for d_pre in d_pres]
    d_pre = jnp.concatenate(d_pres, axis=0)
    weight_grad[2 * width :, :] += dot_tn(
        jnp.concatenate(acts, axis=0), jnp.concatenate(d_branches, axis=0)
    )
    mixed = mixed_ref[held_rows(step, rows), :]
    for at in range(2):
        weight_grad[at * width : (at + 1) * width, :] += dot_tn(
            mixed, d_pre[:, at * width : (at + 1) * width]
        )
    for at, place in enumerate(places):
        d_mixed = d_finals[at] + backs[at]
        d_mixed_ref[owns[at], :] = d_mixed
        add_rows(
            stats,
            (
                column_sum(d_mixed),
                column_sum(d_mixed * local_hat_ref[place, :].astype(F32)),
                column_sum(d_mixed * attend_hat_ref[place, :].astype(F32)),
                bias_sums[at][:, :width],
                bias_sums[at][:, width:],
            ),
        )
    send_rows(stats, sent_stats)


def branch_back(d_mixed, hat, mask, scale, shift_grad, gain_grad, count):
    per_node = 1.0 / count
    return scale * (d_mixed - mask * (shift_grad * per_node + hat * (gain_grad * per_node)))


def gcn_back_kernel(
    node_count,
    d_mixed_ref,
    local_hat_ref,
    inverse_ref,
    ratio_ref,
    gate_ref,
    sent_ref,
    slope_ref,
    node_ref,
    edge_ref,
    source_ref,
    target_ref,
    branch_stats,
    sent_back,
    gains,
    gcn_weight,
    edge_weight,
    node_part_ref,
    edge_out_ref,
    weight_grad,
    back_stats,
    d_proj,
    d_hats,
):
    step = pl.program_id(0)
    first = step * GROUP
    width = node_ref.shape[1]
    slots = node_ref.shape[0] // GROUP
    edges = edge_ref.shape[0] // GROUP

    @pl.when(step == 0)
    def _():
        weight_grad[...] = jnp.zeros_like(weight_grad)
        sum_rows(sent_back, back_stats)

    count = branch_stats[4:5, :]
    _, inv = norm_rows(branch_stats[0:1, :], branch_stats[1:2, :], count)
    mask = row_mask(node_count, first, GROUP, slots, width)
    d_local = branch_back(
        d_mixed_ref[...],
        local_hat_ref[...].astype(F32),
        mask,
        inv * gains[0:1, :],
        back_stats[0:1, :],
        back_stats[1:2, :],
        count,
    )
    numer = d_local * inverse_ref[...].astype(F32)
    d_denom = (-numer * ratio_ref[...].astype(F32)).astype(LOW)
    d_numer = numer.astype(LOW)
    d_proj[:, :width] = d_local.astype(LOW)
    hots = [end_hots(source_ref, target_ref, at, slots) for at in range(GROUP)]
    backs = []
    for at in range(GROUP):
        rows = slice(at * slots, (at + 1) * slots)
        pair = jnp.concatenate([d_numer[rows], d_denom[rows]], axis=1)
        backs.append(dot_tn(hots[at][slots:], pair))
    pairs = []
    for at in range(GROUP):
        edge_rows = slice(at * edges, (at + 1) * edges)
        d_message = backs[at][:, :width]
        d_gate = backs[at][:, width:] + d_message * sent_ref[edge_rows, :].astype(F32)
        d_sent = (d_message * gate_ref[edge_rows, :].astype(F32)).astype(LOW)
        d_hat = (d_gate * slope_ref[edge_rows, :].astype(F32)).astype(LOW)
        d_hats[edge_rows, :] = d_hat
        pairs.append(jnp.concatenate([d_sent, d_hat], axis=1))
    pulls = [dot(hots[at], pairs[at]) for at in range(GROUP)]
    for at in range(GROUP):
        rows = slice(at * slots, (at + 1) * slots)
        pulled = pulls[at].astype(LOW)
        d_proj[rows, width : 2 * width] = pulled[:slots, :width]
        d_proj[rows, 2 * width : 3 * width] = pulled[slots:, width:]
        d_proj[rows, 3 * width :] = pulled[:slots, width:]
    weight_grad[4 * width :, :] += dot_tn(edge_ref[...], d_hats[...])
    edge_out_ref[...] = dot_nt(d_hats[...], edge_weight[...])
    for at in range(4):
        columns = slice(at * width, (at + 1) * width)
        weight_grad[columns, :] += dot_tn(node_ref[...], d_proj[:, columns])
    node_part_ref[...] = d_local + dot_nt(d_proj[...], gcn_weight[...])


def attend_back_kernel(
    node_count,
    d_mixed_ref,
    attend_hat_ref,
    qkv_ref,
    prob_ref,
    attended_ref,
    node_ref,
    node_part_ref,
    branch_stats,
    back_stats,
    gains,
    attend_weight,
    attend_out,
    node_out_ref,
    weight_grad,
    d_qkv,
):
    step = pl.program_id(0)
    first = step * GROUP
    width = node_ref.shape[1]
    slots = node_ref.shape[0] // GROUP

    @pl.when(step == 0)
    def _():
        weight_grad[...] = jnp.zeros_like(weight_grad)

    count = branch_stats[4:5, :]
    _, inv = norm_rows(branch_stats[2:3, :], branch_stats[3:4, :], count)
    mask = row_mask(node_count, first, GROUP, slots, width)
    d_attend = branch_back(
        d_mixed_ref[...],
        attend_hat_ref[...].astype(F32),
        mask,
        inv * gains[2:3, :],
        back_stats[0:1, :],
        back_stats[2:3, :],
        count,
    )
    d_attn = d_attend.astype(LOW)
    weight_grad[3 * width :, :] += dot_tn(attended_ref[...], d_attn)
    d_att = dot_nt(d_attn, attend_out[...]).astype(LOW)
    scale = HEAD_SIZE ** (-0.5)
    pieces = [(at, half) for at in range(GROUP) for half in range(width // HALF)]

    def place(at, half, part=0):
        first_lane = part * width + half * HALF
        return slice(at * slots, (at + 1) * slots), slice(first_lane, first_lane + HALF)

    def prob_place(at, half):
        return slice(at * slots, (at + 1) * slots), slice(half * 2 * HALF, (half + 1) * 2 * HALF)

    masks = head_masks(slots)
    d_att_blocks = {key: head_blocks(d_att[place(*key)], masks) for key in pieces}
    d_probs = {key: dot_nt(qkv_ref[place(*key, 2)], d_att_blocks[key]) for key in pieces}
    for key in pieces:
        d_values = dot(prob_ref[prob_place(*key)], d_att_blocks[key])
        d_qkv[place(*key, 2)] = d_values.astype(LOW)
    d_scores = {}
    for key in pieces:
        probs = prob_ref[prob_place(*key)].astype(F32)
        weighted = probs * d_probs[key]
        d_scores[key] = (weighted - probs * column_sum(weighted)).astype(LOW)
    for key in pieces:
        d_keys = dot(d_scores[key], head_blocks(qkv_ref[place(*key)], masks))
        d_qkv[place(*key, 1)] = (d_keys * scale).astype(LOW)
    stacks = {key: dot_tn(d_scores[key], qkv_ref[place(*key, 1)]) for key in pieces}
    for key in pieces:
        d_qkv[place(*key)] = (head_merge(stacks[key], slots) * scale).astype(LOW)
    for at in range(3):
        columns = slice(at * width, (at + 1) * width)
        weight_grad[columns, :] += dot_tn(node_ref[...], d_qkv[:, columns])
    node_out_ref[...] = node_part_ref[...] + d_attend + dot_nt(d_qkv[...], attend_weight[...])


def run_blocks(kernel, steps, limit, args, outs, scratch=(), flops=0):
    def spec(kind, shape):
        if kind == "scalar":
            return pl.BlockSpec(memory_space=pltpu.SMEM)
        if kind == "held":
            return pl.BlockSpec(memory_space=pltpu.VMEM)
        if kind == "rows":
            return pl.BlockSpec((shape[0] // steps, shape[1]), lambda step: (step, 0))
        return pl.BlockSpec(shape, lambda step: (0,) * len(shape))

    def keep(kind, item):
        return pltpu.with_memory_space_constraint(item, pltpu.VMEM) if kind == "held" else item

    moved = sum(item.size * item.dtype.itemsize for _, item in args)
    return pl.pallas_call(
        kernel,
        grid=(steps,),
        in_specs=[spec(kind, item.shape) for kind, item in args],
        out_specs=[spec(kind, shape) for kind, shape, _ in outs],
        out_shape=[
            (pltpu.VMEM if kind == "held" else jax.ShapeDtypeStruct)(shape, dtype)
            for kind, shape, dtype in outs
        ],
        scratch_shapes=list(scratch),
        compiler_params=pltpu.CompilerParams(
            dimension_semantics=("arbitrary",), vmem_limit_bytes=limit * MIB
        ),
        cost_estimate=pl.CostEstimate(flops=flops, bytes_accessed=moved, transcendentals=0),
    )(*[keep(kind, item) for kind, item in args])


def all_share(values):
    return lax.all_to_all(values, "graphs", 0, 0)


def swap(values, mask, devices):
    return lax.ppermute(values, "graphs", [(at, at ^ mask) for at in range(devices)])


def side(mask):
    return (lax.axis_index("graphs") // mask) % 2


def halve(values, mask, devices):
    pair = values.reshape((2, values.shape[0] // 2) + values.shape[1:])
    mine = lax.dynamic_index_in_dim(pair, side(mask), 0, keepdims=False)
    other = lax.dynamic_index_in_dim(pair, 1 - side(mask), 0, keepdims=False)
    return mine, swap(other, mask, devices)


def keep_half(values, mask, devices):
    mine, other = halve(values, mask, devices)
    return mine + other


def join_halves(values, mask, devices):
    other = swap(values, mask, devices)
    lower = side(mask) == 0
    return jnp.where(
        lower, jnp.concatenate([values, other]), jnp.concatenate([other, values])
    )


def chip_orders(devices):
    masks = [1 << bit for bit in range(1, devices.bit_length() - 1)]
    return masks, masks[1::-1] + masks[2:]


def weight_sums(parts, devices):
    orders = chip_orders(devices)
    for at in range(len(orders[0])):
        parts = [
            part if at == 0 and part is parts[0] else keep_half(part, order[at], devices)
            for part, order in zip(parts, orders)
        ]
    for at in reversed(range(len(orders[0]))):
        parts = [join_halves(part, order[at], devices) for part, order in zip(parts, orders)]
    return parts, [swap(part, 1, devices) for part in parts]


def place_kernel(chunks, core, *refs):
    mine, other, outs = refs[:2], refs[2:4], refs[4:]
    for flip in range(2):

        @pl.when(core[0] == flip)
        def _():
            for part, row, rows, places in chunks:
                for half, (out, to_row, to_column) in enumerate(places):
                    source = (mine if half == flip else other)[part]
                    columns = slice(to_column, to_column + source.shape[1])
                    outs[out][to_row : to_row + rows, columns] = source[row : row + rows, :]


def place_sums(parts, others, stacks, shapes):
    width = parts[0].shape[1]
    unit = width // 2
    chunks, at = [], 0
    for index, stack in enumerate(stacks):
        starts, begin = [], 0
        for out in (2 * index, 2 * index + 1):
            rows, columns = shapes[out]
            starts.append((begin, out, rows))
            begin += rows * columns // width

        def place(row):
            begin, out, rows = starts[0] if row < starts[1][0] else starts[1]
            return out, (row - begin) % rows, (row - begin) // rows * width

        half = stack.shape[0] // 2
        for row in range(0, half, unit):
            part = 0 if at < parts[0].shape[0] else 1
            chunks.append((part, at - part * parts[0].shape[0], unit, (place(row), place(half + row))))
            at += unit
    core = side(1).astype(jnp.int32)[None]
    inside = pl.BlockSpec(memory_space=pltpu.VMEM)
    return pl.pallas_call(
        functools.partial(place_kernel, chunks),
        in_specs=[pl.BlockSpec(memory_space=pltpu.SMEM)] + [inside] * 4,
        out_specs=[inside] * len(shapes),
        out_shape=[jax.ShapeDtypeStruct(shape, F32) for shape in shapes],
        compiler_params=pltpu.CompilerParams(vmem_limit_bytes=40 * MIB),
    )(core, *parts, *others)


def on_device(
    devices,
    node_input,
    edge_input,
    node_count,
    edge_count,
    edge_source,
    edge_target,
    gcn_weight,
    edge_weight,
    attend_weight,
    attend_out,
    local_gain,
    local_shift,
    attend_gain,
    attend_shift,
    hidden_weight,
    hidden_bias,
    output_weight,
    final_gain,
    final_shift,
    cotangent,
):
    graphs, edges = edge_source.shape
    node_rows, width = node_input.shape
    edge_rows = edge_input.shape[0]
    slots = node_rows // graphs
    hidden = hidden_weight.shape[1]
    steps = graphs // GROUP
    gains = jnp.stack(
        [local_gain, local_shift, attend_gain, attend_shift, final_gain, final_shift, final_gain, final_shift]
    )
    counts = ("scalar", node_count)
    node_arg = ("rows", node_input)
    edge_arg = ("rows", edge_input)
    cotangent_arg = ("rows", cotangent)
    ends = [("rows", edge_source), ("rows", edge_target)]
    gains_arg = ("whole", gains)
    node_shape, edge_shape = node_input.shape, edge_input.shape
    sums, shares = (8, width), (devices, 1, 5 * width)
    stats = pltpu.VMEM(sums, F32)
    (
        local_pre,
        attend_pre,
        inverse,
        ratio,
        gate,
        sent,
        slope,
        qkv,
        probs,
        attended,
        branch_shares,
    ) = run_blocks(
        forward_kernel,
        steps,
        60,
        [counts, ("scalar", edge_count), node_arg, edge_arg]
        + ends
        + [("whole", item) for item in (gcn_weight, edge_weight, attend_weight, attend_out)],
        [
            ("rows", node_shape, F32),
            ("rows", node_shape, F32),
            ("rows", node_shape, LOW),
            ("rows", node_shape, LOW),
            ("rows", edge_shape, LOW),
            ("rows", edge_shape, LOW),
            ("rows", edge_shape, LOW),
            ("rows", (node_rows, 3 * width), LOW),
            ("rows", (node_rows, (width // HEAD_SIZE) * slots), LOW),
            ("rows", node_shape, LOW),
            ("whole", shares, F32),
        ],
        scratch=[stats],
    )
    local_hat, attend_hat, mixed, pre, final, branch_stats, final_shares = run_blocks(
        mix_kernel,
        graphs // MIX_GROUP,
        50,
        [counts, ("rows", local_pre), ("rows", attend_pre), cotangent_arg]
        + [("whole", all_share(branch_shares)), gains_arg, ("whole", hidden_weight)]
        + [("whole", hidden_bias[None]), ("whole", output_weight)],
        [
            ("held", node_shape, LOW),
            ("held", node_shape, LOW),
            ("held", node_shape, LOW),
            ("rows", (node_rows, hidden), LOW),
            ("rows", node_shape, F32),
            ("whole", sums, F32),
            ("whole", (devices, 1, 4 * width), F32),
        ],
        scratch=[stats],
    )
    branch_arg = ("whole", branch_stats)
    d_mixed, result, mix_grads, final_sums, back_shares = run_blocks(
        mix_back_kernel,
        graphs // MIX_GROUP,
        50,
        [counts, ("rows", final), ("rows", pre), ("held", local_hat), ("held", attend_hat)]
        + [("held", mixed), cotangent_arg, branch_arg, ("whole", all_share(final_shares))]
        + [gains_arg, ("whole", hidden_weight), ("whole", output_weight)],
        [
            ("rows", node_shape, F32),
            ("rows", node_shape, LOW),
            ("whole", (2 * hidden, width), F32),
            ("whole", sums, F32),
            ("whole", shares, F32),
        ],
        scratch=[stats],
        flops=8 * node_rows * width * hidden,
    )
    node_part, edge_out, gcn_grads, back_stats = run_blocks(
        gcn_back_kernel,
        steps,
        60,
        [counts, ("rows", d_mixed), ("rows", local_hat), ("rows", inverse), ("rows", ratio)]
        + [("rows", gate), ("rows", sent), ("rows", slope), node_arg, edge_arg]
        + ends
        + [branch_arg, ("whole", all_share(back_shares)), gains_arg]
        + [("whole", gcn_weight), ("whole", edge_weight)],
        [
            ("rows", node_shape, F32),
            ("rows", edge_shape, F32),
            ("whole", (5 * width, width), F32),
            ("whole", sums, F32),
        ],
        scratch=[
            pltpu.VMEM((node_rows // steps, 4 * width), LOW),
            pltpu.VMEM((edge_rows // steps, width), LOW),
        ],
    )
    gcn_core = keep_half(gcn_grads, 1, devices)
    orders = chip_orders(devices)
    unit = 8 << len(orders[0])
    sum_rows_all = (mix_grads.shape[0] + gcn_grads.shape[0] + 4 * width) // 2
    cut = -(-sum_rows_all // (2 * unit)) * unit - mix_grads.shape[0] // 2
    early = jnp.concatenate([keep_half(mix_grads, 1, devices), gcn_core[:cut]])
    early, got = halve(early, orders[0][0], devices)
    early, qkv = lax.optimization_barrier((early, qkv))
    node_out, attend_grads = run_blocks(
        attend_back_kernel,
        steps,
        60,
        [counts, ("rows", d_mixed), ("rows", attend_hat), ("rows", qkv), ("rows", probs)]
        + [("rows", attended), node_arg, ("rows", node_part), branch_arg, ("whole", back_stats)]
        + [gains_arg, ("whole", attend_weight), ("whole", attend_out)],
        [
            ("rows", node_shape, F32),
            ("whole", (4 * width, width), F32),
        ],
        scratch=[pltpu.VMEM((node_rows // steps, 3 * width), LOW)],
    )
    got, attend_grads = lax.optimization_barrier((got, attend_grads))
    late = jnp.concatenate([gcn_core[cut:], keep_half(attend_grads, 1, devices)])
    parts, others = weight_sums([early + got, late], devices)
    hidden_grad, output_grad, gcn_grad, edge_grad, attend_grad, attend_out_grad = place_sums(
        parts,
        others,
        (mix_grads, gcn_grads, attend_grads),
        [hidden_weight.shape, output_weight.shape, gcn_weight.shape]
        + [edge_weight.shape, attend_weight.shape, attend_out.shape],
    )
    return (
        result,
        node_out,
        edge_out,
        gcn_grad,
        edge_grad,
        attend_grad,
        attend_out_grad,
        back_stats[1],
        back_stats[0],
        back_stats[2],
        back_stats[0],
        hidden_grad,
        back_stats[3:5].reshape(-1),
        output_grad,
        final_sums[4],
        final_sums[2],
    )


def solution(mesh):
    rows = P("graphs", None)
    each = P("graphs")
    return jax.shard_map(
        functools.partial(on_device, mesh.shape["graphs"]),
        mesh=mesh,
        in_specs=(rows, rows, each, each, rows, rows) + (P(),) * 13 + (rows,),
        out_specs=(rows, rows, rows) + (P(),) * 13,
        check_vma=False,
    )
```

```python
import functools
import math

import jax
import jax.numpy as jnp
from jax import lax
from jax.experimental import pallas as pl
from jax.experimental.pallas import tpu as pltpu
from jax.sharding import PartitionSpec as P

HEAD_SIZE = 32
HALF = 128
EXP2_SCALE = HEAD_SIZE ** (-0.5) / math.log(2.0)
GROUP = 16
MIX_GROUP = 16
SUB = 4
PARTS = 4
EPS = 1e-05
F32 = jnp.float32
LOW = jnp.bfloat16
MIB = 1024 * 1024


def dot(left, right):
    return jnp.dot(left, right, preferred_element_type=F32)


def dot_nt(left, right):
    return lax.dot_general(left, right, (((1,), (1,)), ((), ())), preferred_element_type=F32)


def dot_tn(left, right):
    return lax.dot_general(left, right, (((0,), (0,)), ((), ())), preferred_element_type=F32)


def sigmoid(values):
    return 0.5 * jnp.tanh(0.5 * values) + 0.5


def norm_rows(total, squares, count):
    center = total / count
    return center, lax.rsqrt(squares / count - center * center + EPS)


def one_hot(index_row, slots):
    grid = lax.broadcasted_iota(jnp.int32, (slots, index_row.shape[1]), 0)
    return jnp.where(grid == index_row, 1.0, 0.0)


def end_hots(source_ref, target_ref, at, slots):
    ends = [one_hot(ref[at : at + 1, :], slots) for ref in (source_ref, target_ref)]
    return jnp.concatenate(ends, axis=0).astype(LOW)


def row_mask(counts, first, graphs, slots, width):
    grid = lax.broadcasted_iota(jnp.int32, (slots, width), 0)
    return jnp.concatenate(
        [jnp.where(grid < counts[first + at], 1.0, 0.0) for at in range(graphs)], axis=0
    )


def head_masks(slots):
    head = lax.broadcasted_iota(jnp.int32, (slots, HALF), 1) // HEAD_SIZE
    flat = [jnp.where(head == at, 1.0, 0.0).astype(LOW) for at in range(HALF // HEAD_SIZE)]
    row = lax.broadcasted_iota(jnp.int32, (HALF, 2 * slots), 0) // HEAD_SIZE
    lane = lax.broadcasted_iota(jnp.int32, (HALF, 2 * slots), 1) // slots
    tall = [jnp.where(row == lane + at, 1.0, 0.0).astype(LOW) for at in range(0, HALF // HEAD_SIZE, 2)]
    return flat, tall


def head_blocks(rows, masks):
    return jnp.concatenate([rows * mask for mask in masks[0]], axis=0)


def head_blocks_t(rows, masks):
    turned = rows.T
    twice = jnp.concatenate([turned, turned], axis=1)
    return jnp.concatenate([twice * mask for mask in masks[1]], axis=1)


def heads_turn(wide, slots):
    pairs = [wide[:, at : at + 2 * slots].T for at in range(0, wide.shape[1], 2 * slots)]
    return jnp.concatenate(
        [part for pair in pairs for part in (pair[:slots], pair[slots:])], axis=1
    )


def head_merge(stacked, slots):
    head = lax.broadcasted_iota(jnp.int32, (slots, HALF), 1) // HEAD_SIZE
    merged = stacked[:slots]
    for at in range(1, HALF // HEAD_SIZE):
        merged = jnp.where(head == at, stacked[at * slots : (at + 1) * slots], merged)
    return merged


def column_sum(values):
    return jnp.sum(values, axis=0, keepdims=True)


def add_rows(stats, rows):
    for at, row in enumerate(rows):
        stats[at : at + 1, :] += row


def send_rows(stats, sent_ref):
    @pl.when(pl.program_id(0) == pl.num_programs(0) - 1)
    def _():
        rows = sent_ref.shape[2] // stats.shape[1]
        line = jnp.concatenate([stats[at : at + 1, :] for at in range(rows)], axis=1)
        sent_ref[...] = jnp.broadcast_to(line[None], sent_ref.shape)


def sum_rows(sent_ref, stats):
    line = jnp.sum(sent_ref[...], axis=0)
    width = stats.shape[1]
    for at in range(line.shape[1] // width):
        stats[at : at + 1, :] = line[:, at * width : (at + 1) * width]


def held_rows(step, rows):
    return pl.ds(pl.multiple_of(step * rows, rows), rows)


def forward_kernel(
    node_count,
    edge_count,
    node_ref,
    edge_ref,
    source_ref,
    target_ref,
    gcn_weight,
    edge_weight,
    attend_weight,
    attend_out,
    local_ref,
    attend_ref,
    inverse_ref,
    ratio_ref,
    gate_ref,
    sent_ref,
    slope_ref,
    qkv_ref,
    prob_ref,
    attended_ref,
    sent_stats,
    stats,
):
    step = pl.program_id(0)
    first = step * GROUP
    width = node_ref.shape[1]
    slots = node_ref.shape[0] // GROUP
    edges = edge_ref.shape[0] // GROUP

    @pl.when(step == 0)
    def _():
        stats[...] = jnp.zeros_like(stats)

    edge_grid = lax.broadcasted_iota(jnp.int32, (edges, width), 0)
    node_grid = lax.broadcasted_iota(jnp.int32, (slots, 2 * HALF), 0)
    nothing = jnp.zeros((slots, width), LOW)
    masks = head_masks(slots)
    halves = range(width // HALF)
    held = {}

    def node_rows(at):
        return slice(at * slots, (at + 1) * slots)

    def edge_rows(at):
        return slice(at * edges, (at + 1) * edges)

    def take(name, at, height):
        row = at % SUB * height
        return held[name, at // SUB][row : row + height]

    def project_nodes(sub):
        rows = slice(sub * SUB * slots, (sub + 1) * SUB * slots)
        proj = dot(node_ref[rows, :], gcn_weight[...])
        held["own", sub] = proj[:, :width]
        held["parts", sub] = proj[:, width:].astype(LOW)

    def project_edges(sub):
        rows = slice(sub * SUB * edges, (sub + 1) * SUB * edges)
        held["edge", sub] = dot(edge_ref[rows, :], edge_weight[...])

    def project_heads(sub):
        rows = slice(sub * SUB * slots, (sub + 1) * SUB * slots)
        held["qkv", sub] = dot(node_ref[rows, :], attend_weight[...]).astype(LOW)
        qkv_ref[rows, :] = held["qkv", sub]

    def gather(at):
        parts = take("parts", at, slots)
        held["hot", at] = end_hots(source_ref, target_ref, at, slots)
        spread = jnp.concatenate(
            [
                jnp.concatenate([parts[:, 2 * width :], parts[:, :width]], axis=1),
                jnp.concatenate([parts[:, width : 2 * width], nothing], axis=1),
            ],
            axis=0,
        )
        held["gathered", at] = dot_tn(held["hot", at], spread)

    def score(at):
        qkv = take("qkv", at, slots)
        for half in halves:
            query = qkv[:, half * HALF : (half + 1) * HALF]
            key = qkv[:, width + half * HALF : width + (half + 1) * HALF]
            held["scores", at, half] = dot(key, head_blocks_t(query, masks))

    def message(at):
        rows, gathered = edge_rows(at), held.pop(("gathered", at))
        sent = gathered[:, width:]
        gate_sig = sigmoid(take("edge", at, edges) + gathered[:, :width])
        kept = jnp.where(edge_grid < edge_count[first + at], gate_sig, 0.0)
        gate = kept.astype(LOW)
        gate_ref[rows, :] = gate
        sent_ref[rows, :] = sent.astype(LOW)
        slope_ref[rows, :] = (kept * (1.0 - gate_sig)).astype(LOW)
        sent_on = (gate.astype(F32) * sent).astype(LOW)
        held["message", at] = jnp.concatenate([sent_on, gate], axis=1)

    def soften(at):
        key_kept = node_grid < node_count[first + at]
        for half in halves:
            shown = jnp.where(key_kept, held.pop(("scores", at, half)), -1e30)
            expo = jnp.exp2((shown - jnp.max(shown, axis=0, keepdims=True)) * EXP2_SCALE)
            probs = (expo * (1.0 / column_sum(expo))).astype(LOW)
            held["probs", at, half] = probs
            prob_ref[node_rows(at), half * 2 * HALF : (half + 1) * 2 * HALF] = probs

    def pool(at):
        held["pooled", at] = dot(held.pop(("hot", at))[slots:], held.pop(("message", at)))

    def attend(at):
        qkv = take("qkv", at, slots)
        for half in halves:
            value = qkv[:, 2 * width + half * HALF : 2 * width + (half + 1) * HALF]
            held["spread", at, half] = dot_tn(held.pop(("probs", at, half)), value)

    def finish(at):
        rows, pooled = node_rows(at), held.pop(("pooled", at))
        inverse = 1.0 / (pooled[:, width:] + 1e-06)
        ratio = pooled[:, :width] * inverse
        inverse_ref[rows, :] = inverse.astype(LOW)
        ratio_ref[rows, :] = ratio.astype(LOW)
        local_ref[rows, :] = node_ref[rows, :].astype(F32) + take("own", at, slots) + ratio
        for half in halves:
            merged = head_merge(held.pop(("spread", at, half)), slots)
            attended_ref[rows, half * HALF : (half + 1) * HALF] = merged.astype(LOW)

    dense = (project_nodes, project_edges, project_heads)
    for stage in dense:
        stage(0)
    for tick in range(GROUP + 3):
        sub, phase = tick // SUB + 1, tick % SUB
        if sub < GROUP // SUB and phase < len(dense):
            dense[phase](sub)
        for lag, stages in enumerate(((gather, score), (message, soften), (pool, attend), (finish,))):
            if 0 <= tick - lag < GROUP:
                for stage in stages:
                    stage(tick - lag)
    attend_pre = node_ref[...].astype(F32) + dot(attended_ref[...], attend_out[...])
    attend_ref[...] = attend_pre
    local_pre = local_ref[...]
    mask = row_mask(node_count, first, GROUP, slots, width)
    local_kept = mask * local_pre
    attend_kept = mask * attend_pre
    add_rows(
        stats,
        (
            column_sum(local_kept),
            column_sum(local_kept * local_pre),
            column_sum(attend_kept),
            column_sum(attend_kept * attend_pre),
            column_sum(mask),
        ),
    )
    send_rows(stats, sent_stats)


def mix_kernel(
    node_count,
    local_ref,
    attend_ref,
    cotangent_ref,
    sent_branch,
    gains,
    hidden_weight,
    hidden_bias,
    output_weight,
    local_hat_ref,
    attend_hat_ref,
    mixed_ref,
    pre_ref,
    final_ref,
    branch_stats,
    sent_stats,
    stats,
):
    step = pl.program_id(0)
    first = step * MIX_GROUP
    rows, width = cotangent_ref.shape
    slots = rows // MIX_GROUP

    @pl.when(step == 0)
    def _():
        stats[...] = jnp.zeros_like(stats)
        sum_rows(sent_branch, branch_stats)

    count = branch_stats[4:5, :]
    local_center, local_inv = norm_rows(branch_stats[0:1, :], branch_stats[1:2, :], count)
    attend_center, attend_inv = norm_rows(branch_stats[2:3, :], branch_stats[3:4, :], count)
    part, graphs = rows // PARTS, MIX_GROUP // PARTS
    owns = [slice(at * part, (at + 1) * part) for at in range(PARTS)]
    places = [held_rows(step * PARTS + at, part) for at in range(PARTS)]
    scaled, pres = [], []
    for own, place in zip(owns, places):
        local_hat = (local_ref[own, :] - local_center) * local_inv
        attend_hat = (attend_ref[own, :] - attend_center) * attend_inv
        local_hat_ref[place, :] = local_hat.astype(LOW)
        attend_hat_ref[place, :] = attend_hat.astype(LOW)
        scaled.append(local_hat * gains[0:1, :] + attend_hat * gains[2:3, :])
        mixed = (scaled[-1] + (gains[1:2, :] + gains[3:4, :])).astype(LOW)
        mixed_ref[place, :] = mixed
        pres.append(dot(mixed, hidden_weight[...]))
    finals = []
    for at, own in enumerate(owns):
        pre = pres[at] + hidden_bias[...]
        pre_ref[own, :] = pre.astype(LOW)
        act = (pre * sigmoid(pre)).astype(LOW)
        finals.append(scaled[at] + dot(act, output_weight[...]))
    for at, own in enumerate(owns):
        final = finals[at]
        final_ref[own, :] = final
        mask = row_mask(node_count, first + at * graphs, graphs, slots, width)
        kept = mask * final
        up = mask * cotangent_ref[own, :].astype(F32)
        add_rows(
            stats,
            (column_sum(kept), column_sum(kept * final), column_sum(up), column_sum(up * final)),
        )
    send_rows(stats, sent_stats)


def mix_back_kernel(
    node_count,
    final_ref,
    pre_ref,
    local_hat_ref,
    attend_hat_ref,
    mixed_ref,
    cotangent_ref,
    branch_stats,
    sent_final,
    gains,
    hidden_weight,
    output_weight,
    d_mixed_ref,
    result_ref,
    weight_grad,
    final_sums,
    sent_stats,
    stats,
):
    step = pl.program_id(0)
    first = step * MIX_GROUP
    rows, width = cotangent_ref.shape
    slots = rows // MIX_GROUP

    @pl.when(step == 0)
    def _():
        stats[...] = jnp.zeros_like(stats)
        weight_grad[...] = jnp.zeros_like(weight_grad)
        sum_rows(sent_final, final_sums)

    count = branch_stats[4:5, :]
    per_node = 1.0 / count
    center, inv = norm_rows(final_sums[0:1, :], final_sums[1:2, :], count)
    shift_grad = final_sums[2:3, :]
    gain_grad = inv * (final_sums[3:4, :] - center * shift_grad)
    final_sums[4:5, :] = gain_grad
    part, graphs = rows // PARTS, MIX_GROUP // PARTS
    owns = [slice(at * part, (at + 1) * part) for at in range(PARTS)]
    places = [held_rows(step * PARTS + at, part) for at in range(PARTS)]
    d_finals, d_branches, d_acts = [], [], []
    for at, own in enumerate(owns):
        mask = row_mask(node_count, first + at * graphs, graphs, slots, width)
        final_hat = (final_ref[own, :] - center) * inv
        result_ref[own, :] = (mask * (final_hat * gains[4:5, :] + gains[5:6, :])).astype(LOW)
        pulled = shift_grad * per_node + final_hat * (gain_grad * per_node)
        d_finals.append(
            (inv * gains[4:5, :]) * (mask * (cotangent_ref[own, :].astype(F32) - pulled))
        )
        d_branches.append(d_finals[-1].astype(LOW))
        d_acts.append(dot_nt(d_branches[-1], output_weight[...]))
    acts, d_pres, bias_sums = [], [], []
    for at, own in enumerate(owns):
        pre = pre_ref[own, :].astype(F32)
        sig = sigmoid(pre)
        acts.append((pre * sig).astype(LOW))
        d_pres.append((d_acts[at] * (sig * (1.0 + pre * (1.0 - sig)))).astype(LOW))
        bias_sums.append(column_sum(d_pres[-1].astype(F32)))
    backs = [dot_nt(d_pre, hidden_weight[...]) for d_pre in d_pres]
    d_pre = jnp.concatenate(d_pres, axis=0)
    weight_grad[2 * width :, :] += dot_tn(
        jnp.concatenate(acts, axis=0), jnp.concatenate(d_branches, axis=0)
    )
    mixed = mixed_ref[held_rows(step, rows), :]
    for at in range(2):
        weight_grad[at * width : (at + 1) * width, :] += dot_tn(
            mixed, d_pre[:, at * width : (at + 1) * width]
        )
    for at, place in enumerate(places):
        d_mixed = d_finals[at] + backs[at]
        d_mixed_ref[owns[at], :] = d_mixed.astype(LOW)
        add_rows(
            stats,
            (
                column_sum(d_mixed),
                column_sum(d_mixed * local_hat_ref[place, :].astype(F32)),
                column_sum(d_mixed * attend_hat_ref[place, :].astype(F32)),
                bias_sums[at][:, :width],
                bias_sums[at][:, width:],
            ),
        )
    send_rows(stats, sent_stats)


def branch_back(d_mixed, hat, mask, scale, shift_grad, gain_grad, count):
    per_node = 1.0 / count
    return scale * (d_mixed - mask * (shift_grad * per_node + hat * (gain_grad * per_node)))


def gcn_back_kernel(
    node_count,
    d_mixed_ref,
    local_hat_ref,
    inverse_ref,
    ratio_ref,
    gate_ref,
    sent_ref,
    slope_ref,
    node_ref,
    edge_ref,
    source_ref,
    target_ref,
    branch_stats,
    sent_back,
    gains,
    gcn_weight,
    node_part_ref,
    d_hats,
    weight_grad,
    back_stats,
    d_proj,
):
    step = pl.program_id(0)
    first = step * GROUP
    width = node_ref.shape[1]
    slots = node_ref.shape[0] // GROUP
    edges = edge_ref.shape[0] // GROUP

    @pl.when(step == 0)
    def _():
        weight_grad[...] = jnp.zeros_like(weight_grad)
        sum_rows(sent_back, back_stats)

    count = branch_stats[4:5, :]
    _, inv = norm_rows(branch_stats[0:1, :], branch_stats[1:2, :], count)
    mask = row_mask(node_count, first, GROUP, slots, width)
    d_local = branch_back(
        d_mixed_ref[...].astype(F32),
        local_hat_ref[...].astype(F32),
        mask,
        inv * gains[0:1, :],
        back_stats[0:1, :],
        back_stats[1:2, :],
        count,
    )
    numer = d_local * inverse_ref[...].astype(F32)
    d_denom = (-numer * ratio_ref[...].astype(F32)).astype(LOW)
    d_numer = numer.astype(LOW)
    d_proj[:, :width] = d_local.astype(LOW)
    hots = [end_hots(source_ref, target_ref, at, slots) for at in range(GROUP)]
    backs = []
    for at in range(GROUP):
        rows = slice(at * slots, (at + 1) * slots)
        pair = jnp.concatenate([d_numer[rows], d_denom[rows]], axis=1)
        backs.append(dot_tn(hots[at][slots:], pair))
    pairs = []
    for at in range(GROUP):
        edge_rows = slice(at * edges, (at + 1) * edges)
        d_message = backs[at][:, :width]
        d_gate = backs[at][:, width:] + d_message * sent_ref[edge_rows, :].astype(F32)
        d_sent = (d_message * gate_ref[edge_rows, :].astype(F32)).astype(LOW)
        d_hat = (d_gate * slope_ref[edge_rows, :].astype(F32)).astype(LOW)
        d_hats[edge_rows, :] = d_hat
        pairs.append(jnp.concatenate([d_sent, d_hat], axis=1))
    pulls = [dot(hots[at], pairs[at]) for at in range(GROUP)]
    for at in range(GROUP):
        rows = slice(at * slots, (at + 1) * slots)
        pulled = pulls[at].astype(LOW)
        d_proj[rows, width : 2 * width] = pulled[:slots, :width]
        d_proj[rows, 2 * width : 3 * width] = pulled[slots:, width:]
        d_proj[rows, 3 * width :] = pulled[:slots, width:]
    weight_grad[4 * width :, :] += dot_tn(edge_ref[...], d_hats[...])
    for at in range(4):
        columns = slice(at * width, (at + 1) * width)
        weight_grad[columns, :] += dot_tn(node_ref[...], d_proj[:, columns])
    node_part_ref[...] = (d_local + dot_nt(d_proj[...], gcn_weight[...])).astype(LOW)


def attend_back_kernel(
    node_count,
    d_mixed_ref,
    attend_hat_ref,
    qkv_ref,
    prob_ref,
    attended_ref,
    node_ref,
    node_part_ref,
    branch_stats,
    back_stats,
    gains,
    attend_out,
    direct_ref,
    d_qkv,
    weight_grad,
):
    step = pl.program_id(0)
    first = step * GROUP
    width = node_ref.shape[1]
    slots = node_ref.shape[0] // GROUP

    @pl.when(step == 0)
    def _():
        weight_grad[...] = jnp.zeros_like(weight_grad)

    count = branch_stats[4:5, :]
    _, inv = norm_rows(branch_stats[2:3, :], branch_stats[3:4, :], count)
    mask = row_mask(node_count, first, GROUP, slots, width)
    d_attend = branch_back(
        d_mixed_ref[...].astype(F32),
        attend_hat_ref[...].astype(F32),
        mask,
        inv * gains[2:3, :],
        back_stats[0:1, :],
        back_stats[2:3, :],
        count,
    )
    d_attn = d_attend.astype(LOW)
    weight_grad[3 * width :, :] += dot_tn(attended_ref[...], d_attn)
    d_att = dot_nt(d_attn, attend_out[...]).astype(LOW)
    scale = HEAD_SIZE ** (-0.5)
    pieces = [(at, half) for at in range(GROUP) for half in range(width // HALF)]

    def place(at, half, part=0):
        first_lane = part * width + half * HALF
        return slice(at * slots, (at + 1) * slots), slice(first_lane, first_lane + HALF)

    def prob_place(at, half):
        return slice(at * slots, (at + 1) * slots), slice(half * 2 * HALF, (half + 1) * 2 * HALF)

    masks = head_masks(slots)
    d_att_blocks = {key: head_blocks(d_att[place(*key)], masks) for key in pieces}
    d_probs = {key: dot_nt(qkv_ref[place(*key, 2)], d_att_blocks[key]) for key in pieces}
    for key in pieces:
        d_values = dot(prob_ref[prob_place(*key)], d_att_blocks[key])
        d_qkv[place(*key, 2)] = d_values.astype(LOW)
    d_scores = {}
    for key in pieces:
        probs = prob_ref[prob_place(*key)].astype(F32)
        weighted = probs * d_probs[key]
        d_scores[key] = (weighted - probs * column_sum(weighted)).astype(LOW)
    for key in pieces:
        d_keys = dot(d_scores[key], head_blocks(qkv_ref[place(*key)], masks))
        d_qkv[place(*key, 1)] = (d_keys * scale).astype(LOW)
    stacks = {key: dot_tn(d_scores[key], qkv_ref[place(*key, 1)]) for key in pieces}
    for key in pieces:
        d_qkv[place(*key)] = (head_merge(stacks[key], slots) * scale).astype(LOW)
    for at in range(3):
        columns = slice(at * width, (at + 1) * width)
        weight_grad[columns, :] += dot_tn(node_ref[...], d_qkv[:, columns])
    direct_ref[...] = (node_part_ref[...].astype(F32) + d_attend).astype(LOW)


def edge_out_kernel(d_hat_ref, edge_weight, edge_out_ref):
    edge_out_ref[...] = dot_nt(d_hat_ref[...], edge_weight[...])


def node_out_kernel(direct_ref, d_qkv_ref, attend_weight, node_out_ref):
    node_out_ref[...] = direct_ref[...].astype(F32) + dot_nt(d_qkv_ref[...], attend_weight[...])


def run_blocks(kernel, steps, limit, args, outs, scratch=(), flops=0):
    def spec(kind, shape):
        if kind == "scalar":
            return pl.BlockSpec(memory_space=pltpu.SMEM)
        if kind == "held":
            return pl.BlockSpec(memory_space=pltpu.VMEM)
        if kind == "rows":
            return pl.BlockSpec((shape[0] // steps, shape[1]), lambda step: (step, 0))
        return pl.BlockSpec(shape, lambda step: (0,) * len(shape))

    def keep(kind, item):
        return pltpu.with_memory_space_constraint(item, pltpu.VMEM) if kind == "held" else item

    moved = sum(item.size * item.dtype.itemsize for _, item in args)
    return pl.pallas_call(
        kernel,
        grid=(steps,),
        in_specs=[spec(kind, item.shape) for kind, item in args],
        out_specs=[spec(kind, shape) for kind, shape, _ in outs],
        out_shape=[
            (pltpu.VMEM if kind == "held" else jax.ShapeDtypeStruct)(shape, dtype)
            for kind, shape, dtype in outs
        ],
        scratch_shapes=list(scratch),
        compiler_params=pltpu.CompilerParams(
            dimension_semantics=("arbitrary",), vmem_limit_bytes=limit * MIB
        ),
        cost_estimate=pl.CostEstimate(flops=flops, bytes_accessed=moved, transcendentals=0),
    )(*[keep(kind, item) for kind, item in args])


def all_share(values):
    return lax.all_to_all(values, "graphs", 0, 0)


def swap(values, mask, devices):
    return lax.ppermute(values, "graphs", [(at, at ^ mask) for at in range(devices)])


def side(mask):
    return (lax.axis_index("graphs") // mask) % 2


def halve(values, mask, devices):
    pair = values.reshape((2, values.shape[0] // 2) + values.shape[1:])
    mine = lax.dynamic_index_in_dim(pair, side(mask), 0, keepdims=False)
    other = lax.dynamic_index_in_dim(pair, 1 - side(mask), 0, keepdims=False)
    return mine, swap(other, mask, devices)


def keep_half(values, mask, devices):
    mine, other = halve(values, mask, devices)
    return mine + other


def chip_orders(devices):
    masks = [1 << bit for bit in range(1, devices.bit_length() - 1)]
    return masks, masks[1::-1] + masks[2:]


def work_beside(mine, others, work):
    if work is None:
        return mine, others, None
    kernel, item = work
    last, item = lax.optimization_barrier((mine[0], item))
    got, out = lax.optimization_barrier((others[0], kernel(item)))
    mine, others = [last, *mine[1:]], [got, *others[1:]]
    return mine, others, out


def weight_sums(parts, devices, beside):
    first, second = chip_orders(devices)
    outs, step = [], 0
    for masks in zip(first[1:] + [0], second):
        halves = [halve(part, mask, devices) if mask else (part, None) for part, mask in zip(parts, masks)]
        mine = [pair[0] for pair in halves]
        others = [pair[1] for pair in halves if pair[1] is not None]
        mine, others, out = work_beside(mine, others, beside.get(step))
        offset = len(parts) - len(others)
        parts = list(mine)
        if offset:
            parts[1] = parts[1] + others[0]
        else:
            parts = [own + other for own, other in zip(mine, others)]
        outs, step = outs + [out], step + 1
    for masks in zip(reversed(first), reversed(second)):
        others = [swap(part, mask, devices) for part, mask in zip(parts, masks)]
        parts, others, out = work_beside(parts, others, beside.get(step))
        parts = [
            jnp.where(side(mask) == 0, jnp.concatenate([own, other]), jnp.concatenate([other, own]))
            for own, other, mask in zip(parts, others, masks)
        ]
        outs, step = outs + [out], step + 1
    others = [swap(part, 1, devices) for part in parts]
    return parts, others, [out for out in outs if out is not None]


def place_kernel(chunks, core, *refs):
    mine, other, outs = refs[:2], refs[2:4], refs[4:]
    for flip in range(2):

        @pl.when(core[0] == flip)
        def _():
            for part, row, rows, places in chunks:
                for half, (out, to_row, to_column) in enumerate(places):
                    source = (mine if half == flip else other)[part]
                    columns = slice(to_column, to_column + source.shape[1])
                    outs[out][to_row : to_row + rows, columns] = source[row : row + rows, :]


def place_sums(parts, others, stacks, shapes):
    width = parts[0].shape[1]
    unit = width // 2
    chunks, at = [], 0
    for index, stack in enumerate(stacks):
        starts, begin = [], 0
        for out in (2 * index, 2 * index + 1):
            rows, columns = shapes[out]
            starts.append((begin, out, rows))
            begin += rows * columns // width

        def place(row):
            begin, out, rows = starts[0] if row < starts[1][0] else starts[1]
            return out, (row - begin) % rows, (row - begin) // rows * width

        half = stack.shape[0] // 2
        for row in range(0, half, unit):
            part = 0 if at < parts[0].shape[0] else 1
            chunks.append((part, at - part * parts[0].shape[0], unit, (place(row), place(half + row))))
            at += unit
    core = side(1).astype(jnp.int32)[None]
    inside = pl.BlockSpec(memory_space=pltpu.VMEM)
    return pl.pallas_call(
        functools.partial(place_kernel, chunks),
        in_specs=[pl.BlockSpec(memory_space=pltpu.SMEM)] + [inside] * 4,
        out_specs=[inside] * len(shapes),
        out_shape=[jax.ShapeDtypeStruct(shape, F32) for shape in shapes],
        compiler_params=pltpu.CompilerParams(vmem_limit_bytes=40 * MIB),
    )(core, *parts, *others)


def on_device(
    devices,
    node_input,
    edge_input,
    node_count,
    edge_count,
    edge_source,
    edge_target,
    gcn_weight,
    edge_weight,
    attend_weight,
    attend_out,
    local_gain,
    local_shift,
    attend_gain,
    attend_shift,
    hidden_weight,
    hidden_bias,
    output_weight,
    final_gain,
    final_shift,
    cotangent,
):
    graphs, edges = edge_source.shape
    node_rows, width = node_input.shape
    edge_rows = edge_input.shape[0]
    slots = node_rows // graphs
    hidden = hidden_weight.shape[1]
    steps = graphs // GROUP
    gains = jnp.stack(
        [local_gain, local_shift, attend_gain, attend_shift, final_gain, final_shift, final_gain, final_shift]
    )
    counts = ("scalar", node_count)
    node_arg = ("rows", node_input)
    edge_arg = ("rows", edge_input)
    cotangent_arg = ("rows", cotangent)
    ends = [("rows", edge_source), ("rows", edge_target)]
    gains_arg = ("whole", gains)
    node_shape, edge_shape = node_input.shape, edge_input.shape
    sums, shares = (8, width), (devices, 1, 5 * width)
    stats = pltpu.VMEM(sums, F32)
    (
        local_pre,
        attend_pre,
        inverse,
        ratio,
        gate,
        sent,
        slope,
        qkv,
        probs,
        attended,
        branch_shares,
    ) = run_blocks(
        forward_kernel,
        steps,
        60,
        [counts, ("scalar", edge_count), node_arg, edge_arg]
        + ends
        + [("whole", item) for item in (gcn_weight, edge_weight, attend_weight, attend_out)],
        [
            ("rows", node_shape, F32),
            ("rows", node_shape, F32),
            ("rows", node_shape, LOW),
            ("rows", node_shape, LOW),
            ("rows", edge_shape, LOW),
            ("rows", edge_shape, LOW),
            ("rows", edge_shape, LOW),
            ("rows", (node_rows, 3 * width), LOW),
            ("rows", (node_rows, (width // HEAD_SIZE) * slots), LOW),
            ("rows", node_shape, LOW),
            ("whole", shares, F32),
        ],
        scratch=[stats],
    )
    local_hat, attend_hat, mixed, pre, final, branch_stats, final_shares = run_blocks(
        mix_kernel,
        graphs // MIX_GROUP,
        50,
        [counts, ("rows", local_pre), ("rows", attend_pre), cotangent_arg]
        + [("whole", all_share(branch_shares)), gains_arg, ("whole", hidden_weight)]
        + [("whole", hidden_bias[None]), ("whole", output_weight)],
        [
            ("held", node_shape, LOW),
            ("held", node_shape, LOW),
            ("held", node_shape, LOW),
            ("rows", (node_rows, hidden), LOW),
            ("rows", node_shape, F32),
            ("whole", sums, F32),
            ("whole", (devices, 1, 4 * width), F32),
        ],
        scratch=[stats],
    )
    branch_arg = ("whole", branch_stats)
    d_mixed, result, mix_grads, final_sums, back_shares = run_blocks(
        mix_back_kernel,
        graphs // MIX_GROUP,
        50,
        [counts, ("rows", final), ("rows", pre), ("held", local_hat), ("held", attend_hat)]
        + [("held", mixed), cotangent_arg, branch_arg, ("whole", all_share(final_shares))]
        + [gains_arg, ("whole", hidden_weight), ("whole", output_weight)],
        [
            ("rows", node_shape, LOW),
            ("rows", node_shape, LOW),
            ("whole", (2 * hidden, width), F32),
            ("whole", sums, F32),
            ("whole", shares, F32),
        ],
        scratch=[stats],
        flops=8 * node_rows * width * hidden,
    )
    node_part, d_hats, gcn_grads, back_stats = run_blocks(
        gcn_back_kernel,
        steps,
        60,
        [counts, ("rows", d_mixed), ("rows", local_hat), ("rows", inverse), ("rows", ratio)]
        + [("rows", gate), ("rows", sent), ("rows", slope), node_arg, edge_arg]
        + ends
        + [branch_arg, ("whole", all_share(back_shares)), gains_arg, ("whole", gcn_weight)],
        [
            ("rows", node_shape, LOW),
            ("rows", edge_shape, LOW),
            ("whole", (5 * width, width), F32),
            ("whole", sums, F32),
        ],
        scratch=[pltpu.VMEM((node_rows // steps, 4 * width), LOW)],
    )
    gcn_core = keep_half(gcn_grads, 1, devices)
    orders = chip_orders(devices)
    cut = 2 * width
    early = jnp.concatenate([keep_half(mix_grads, 1, devices), gcn_core[:cut]])
    early, got = halve(early, orders[0][0], devices)
    early, qkv = lax.optimization_barrier((early, qkv))
    direct, d_qkv, attend_grads = run_blocks(
        attend_back_kernel,
        steps,
        60,
        [counts, ("rows", d_mixed), ("rows", attend_hat), ("rows", qkv), ("rows", probs)]
        + [("rows", attended), node_arg, ("rows", node_part), branch_arg, ("whole", back_stats)]
        + [gains_arg, ("whole", attend_out)],
        [
            ("rows", node_shape, LOW),
            ("rows", (node_rows, 3 * width), LOW),
            ("whole", (4 * width, width), F32),
        ],
    )

    def give_edges(d_hats):
        return run_blocks(
            edge_out_kernel,
            graphs // MIX_GROUP,
            60,
            [("rows", d_hats), ("whole", edge_weight)],
            [("rows", edge_shape, F32)],
            flops=2 * edge_rows * width * width,
        )[0]

    def give_nodes(d_qkv):
        return run_blocks(
            node_out_kernel,
            graphs // MIX_GROUP,
            60,
            [("rows", direct), ("rows", d_qkv), ("whole", attend_weight)],
            [("rows", node_shape, F32)],
            flops=6 * node_rows * width * width,
        )[0]

    got, attend_grads = lax.optimization_barrier((got, attend_grads))
    late = jnp.concatenate([gcn_core[cut:], keep_half(attend_grads, 1, devices)])
    beside = {0: (give_edges, d_hats), 2 * len(orders[0]) - 1: (give_nodes, d_qkv)}
    parts, others, (edge_out, node_out) = weight_sums([early + got, late], devices, beside)
    hidden_grad, output_grad, gcn_grad, edge_grad, attend_grad, attend_out_grad = place_sums(
        parts,
        others,
        (mix_grads, gcn_grads, attend_grads),
        [hidden_weight.shape, output_weight.shape, gcn_weight.shape]
        + [edge_weight.shape, attend_weight.shape, attend_out.shape],
    )
    return (
        result,
        node_out,
        edge_out,
        gcn_grad,
        edge_grad,
        attend_grad,
        attend_out_grad,
        back_stats[1],
        back_stats[0],
        back_stats[2],
        back_stats[0],
        hidden_grad,
        back_stats[3:5].reshape(-1),
        output_grad,
        final_sums[4],
        final_sums[2],
    )


def solution(mesh):
    rows = P("graphs", None)
    each = P("graphs")
    return jax.shard_map(
        functools.partial(on_device, mesh.shape["graphs"]),
        mesh=mesh,
        in_specs=(rows, rows, each, each, rows, rows) + (P(),) * 13 + (rows,),
        out_specs=(rows, rows, rows) + (P(),) * 13,
        check_vma=False,
    )
```

```python
import functools
import math

import jax
import jax.numpy as jnp
from jax import lax
from jax.experimental import pallas as pl
from jax.experimental.pallas import tpu as pltpu
from jax.sharding import PartitionSpec as P

HEAD_SIZE = 32
HALF = 128
EXP2_SCALE = HEAD_SIZE ** (-0.5) / math.log(2.0)
GROUP = 16
MIX_GROUP = 16
SUB = 4
PARTS = 4
EPS = 1e-05
F32 = jnp.float32
LOW = jnp.bfloat16
MIB = 1024 * 1024


def dot(left, right):
    return jnp.dot(left, right, preferred_element_type=F32)


def dot_nt(left, right):
    return lax.dot_general(left, right, (((1,), (1,)), ((), ())), preferred_element_type=F32)


def dot_tn(left, right):
    return lax.dot_general(left, right, (((0,), (0,)), ((), ())), preferred_element_type=F32)


def sigmoid(values):
    return 0.5 * jnp.tanh(0.5 * values) + 0.5


def norm_rows(total, squares, count):
    center = total / count
    return center, lax.rsqrt(squares / count - center * center + EPS)


def one_hot(index_row, slots):
    grid = lax.broadcasted_iota(jnp.int32, (slots, index_row.shape[1]), 0)
    return jnp.where(grid == index_row, 1.0, 0.0)


def end_hots(source_ref, target_ref, at, slots):
    ends = [one_hot(ref[at : at + 1, :], slots) for ref in (source_ref, target_ref)]
    return jnp.concatenate(ends, axis=0).astype(LOW)


def row_mask(counts, first, graphs, slots, width):
    grid = lax.broadcasted_iota(jnp.int32, (slots, width), 0)
    return jnp.concatenate(
        [jnp.where(grid < counts[first + at], 1.0, 0.0) for at in range(graphs)], axis=0
    )


def head_masks(slots):
    head = lax.broadcasted_iota(jnp.int32, (slots, HALF), 1) // HEAD_SIZE
    flat = [jnp.where(head == at, 1.0, 0.0).astype(LOW) for at in range(HALF // HEAD_SIZE)]
    row = lax.broadcasted_iota(jnp.int32, (HALF, 2 * slots), 0) // HEAD_SIZE
    lane = lax.broadcasted_iota(jnp.int32, (HALF, 2 * slots), 1) // slots
    tall = [jnp.where(row == lane + at, 1.0, 0.0).astype(LOW) for at in range(0, HALF // HEAD_SIZE, 2)]
    return flat, tall


def head_blocks(rows, masks):
    return jnp.concatenate([rows * mask for mask in masks[0]], axis=0)


def head_blocks_t(rows, masks):
    turned = rows.T
    twice = jnp.concatenate([turned, turned], axis=1)
    return jnp.concatenate([twice * mask for mask in masks[1]], axis=1)


def heads_turn(wide, slots):
    pairs = [wide[:, at : at + 2 * slots].T for at in range(0, wide.shape[1], 2 * slots)]
    return jnp.concatenate(
        [part for pair in pairs for part in (pair[:slots], pair[slots:])], axis=1
    )


def head_merge(stacked, slots):
    head = lax.broadcasted_iota(jnp.int32, (slots, HALF), 1) // HEAD_SIZE
    merged = stacked[:slots]
    for at in range(1, HALF // HEAD_SIZE):
        merged = jnp.where(head == at, stacked[at * slots : (at + 1) * slots], merged)
    return merged


def column_sum(values):
    return jnp.sum(values, axis=0, keepdims=True)


def add_rows(stats, rows):
    for at, row in enumerate(rows):
        stats[at : at + 1, :] += row


def send_rows(stats, sent_ref):
    @pl.when(pl.program_id(0) == pl.num_programs(0) - 1)
    def _():
        rows = sent_ref.shape[2] // stats.shape[1]
        line = jnp.concatenate([stats[at : at + 1, :] for at in range(rows)], axis=1)
        sent_ref[...] = jnp.broadcast_to(line[None], sent_ref.shape)


def sum_rows(sent_ref, stats):
    line = jnp.sum(sent_ref[...], axis=0)
    width = stats.shape[1]
    for at in range(line.shape[1] // width):
        stats[at : at + 1, :] = line[:, at * width : (at + 1) * width]


def held_rows(step, rows):
    return pl.ds(pl.multiple_of(step * rows, rows), rows)


def forward_kernel(
    node_count,
    edge_count,
    node_ref,
    edge_ref,
    source_ref,
    target_ref,
    gcn_weight,
    edge_weight,
    attend_weight,
    attend_out,
    local_ref,
    attend_ref,
    inverse_ref,
    ratio_ref,
    gate_ref,
    sent_ref,
    slope_ref,
    qkv_ref,
    prob_ref,
    attended_ref,
    sent_stats,
    stats,
):
    step = pl.program_id(0)
    first = step * GROUP
    width = node_ref.shape[1]
    slots = node_ref.shape[0] // GROUP
    edges = edge_ref.shape[0] // GROUP

    @pl.when(step == 0)
    def _():
        stats[...] = jnp.zeros_like(stats)

    edge_grid = lax.broadcasted_iota(jnp.int32, (edges, width), 0)
    node_grid = lax.broadcasted_iota(jnp.int32, (slots, 2 * HALF), 0)
    nothing = jnp.zeros((slots, width), LOW)
    masks = head_masks(slots)
    halves = range(width // HALF)
    held = {}

    def node_rows(at):
        return slice(at * slots, (at + 1) * slots)

    def edge_rows(at):
        return slice(at * edges, (at + 1) * edges)

    def take(name, at, height):
        row = at % SUB * height
        return held[name, at // SUB][row : row + height]

    def project_nodes(sub):
        rows = slice(sub * SUB * slots, (sub + 1) * SUB * slots)
        proj = dot(node_ref[rows, :], gcn_weight[...])
        held["own", sub] = proj[:, :width]
        held["parts", sub] = proj[:, width:].astype(LOW)

    def project_edges(sub):
        rows = slice(sub * SUB * edges, (sub + 1) * SUB * edges)
        held["edge", sub] = dot(edge_ref[rows, :], edge_weight[...])

    def project_heads(sub):
        rows = slice(sub * SUB * slots, (sub + 1) * SUB * slots)
        held["qkv", sub] = dot(node_ref[rows, :], attend_weight[...]).astype(LOW)
        qkv_ref[rows, :] = held["qkv", sub]

    def gather(at):
        parts = take("parts", at, slots)
        held["hot", at] = end_hots(source_ref, target_ref, at, slots)
        spread = jnp.concatenate(
            [
                jnp.concatenate([parts[:, 2 * width :], parts[:, :width]], axis=1),
                jnp.concatenate([parts[:, width : 2 * width], nothing], axis=1),
            ],
            axis=0,
        )
        held["gathered", at] = dot_tn(held["hot", at], spread)

    def score(at):
        qkv = take("qkv", at, slots)
        for half in halves:
            query = qkv[:, half * HALF : (half + 1) * HALF]
            key = qkv[:, width + half * HALF : width + (half + 1) * HALF]
            held["scores", at, half] = dot(key, head_blocks_t(query, masks))

    def message(at):
        rows, gathered = edge_rows(at), held.pop(("gathered", at))
        sent = gathered[:, width:]
        gate_sig = sigmoid(take("edge", at, edges) + gathered[:, :width])
        kept = jnp.where(edge_grid < edge_count[first + at], gate_sig, 0.0)
        gate = kept.astype(LOW)
        gate_ref[rows, :] = gate
        sent_ref[rows, :] = sent.astype(LOW)
        slope_ref[rows, :] = (kept * (1.0 - gate_sig)).astype(LOW)
        sent_on = (gate.astype(F32) * sent).astype(LOW)
        held["message", at] = jnp.concatenate([sent_on, gate], axis=1)

    def soften(at):
        key_kept = node_grid < node_count[first + at]
        for half in halves:
            shown = jnp.where(key_kept, held.pop(("scores", at, half)), -1e30)
            expo = jnp.exp2((shown - jnp.max(shown, axis=0, keepdims=True)) * EXP2_SCALE)
            probs = (expo * (1.0 / column_sum(expo))).astype(LOW)
            held["probs", at, half] = probs
            prob_ref[node_rows(at), half * 2 * HALF : (half + 1) * 2 * HALF] = probs

    def pool(at):
        held["pooled", at] = dot(held.pop(("hot", at))[slots:], held.pop(("message", at)))

    def attend(at):
        qkv = take("qkv", at, slots)
        for half in halves:
            value = qkv[:, 2 * width + half * HALF : 2 * width + (half + 1) * HALF]
            held["spread", at, half] = dot_tn(held.pop(("probs", at, half)), value)

    def finish(at):
        rows, pooled = node_rows(at), held.pop(("pooled", at))
        inverse = 1.0 / (pooled[:, width:] + 1e-06)
        ratio = pooled[:, :width] * inverse
        inverse_ref[rows, :] = inverse.astype(LOW)
        ratio_ref[rows, :] = ratio.astype(LOW)
        local_ref[rows, :] = node_ref[rows, :].astype(F32) + take("own", at, slots) + ratio
        for half in halves:
            merged = head_merge(held.pop(("spread", at, half)), slots)
            attended_ref[rows, half * HALF : (half + 1) * HALF] = merged.astype(LOW)

    dense = (project_nodes, project_edges, project_heads)
    for stage in dense:
        stage(0)
    for tick in range(GROUP + 3):
        sub, phase = tick // SUB + 1, tick % SUB
        if sub < GROUP // SUB and phase < len(dense):
            dense[phase](sub)
        for lag, stages in enumerate(((gather, score), (message, soften), (pool, attend), (finish,))):
            if 0 <= tick - lag < GROUP:
                for stage in stages:
                    stage(tick - lag)
    attend_pre = node_ref[...].astype(F32) + dot(attended_ref[...], attend_out[...])
    attend_ref[...] = attend_pre
    local_pre = local_ref[...]
    mask = row_mask(node_count, first, GROUP, slots, width)
    local_kept = mask * local_pre
    attend_kept = mask * attend_pre
    add_rows(
        stats,
        (
            column_sum(local_kept),
            column_sum(local_kept * local_pre),
            column_sum(attend_kept),
            column_sum(attend_kept * attend_pre),
            column_sum(mask),
        ),
    )
    send_rows(stats, sent_stats)


def mix_kernel(
    node_count,
    local_ref,
    attend_ref,
    cotangent_ref,
    sent_branch,
    local_gain,
    local_shift,
    attend_gain,
    attend_shift,
    hidden_weight,
    hidden_bias,
    output_weight,
    local_hat_ref,
    attend_hat_ref,
    mixed_ref,
    pre_ref,
    final_ref,
    branch_stats,
    sent_stats,
    stats,
):
    step = pl.program_id(0)
    first = step * MIX_GROUP
    rows, width = cotangent_ref.shape
    slots = rows // MIX_GROUP

    @pl.when(step == 0)
    def _():
        stats[...] = jnp.zeros_like(stats)
        sum_rows(sent_branch, branch_stats)

    count = branch_stats[4:5, :]
    local_center, local_inv = norm_rows(branch_stats[0:1, :], branch_stats[1:2, :], count)
    attend_center, attend_inv = norm_rows(branch_stats[2:3, :], branch_stats[3:4, :], count)
    part, graphs = rows // PARTS, MIX_GROUP // PARTS
    owns = [slice(at * part, (at + 1) * part) for at in range(PARTS)]
    places = [held_rows(step * PARTS + at, part) for at in range(PARTS)]
    scaled, pres = [], []
    for own, place in zip(owns, places):
        local_hat = (local_ref[own, :] - local_center) * local_inv
        attend_hat = (attend_ref[own, :] - attend_center) * attend_inv
        local_hat_ref[place, :] = local_hat.astype(LOW)
        attend_hat_ref[place, :] = attend_hat.astype(LOW)
        scaled.append(local_hat * local_gain[...] + attend_hat * attend_gain[...])
        mixed = (scaled[-1] + (local_shift[...] + attend_shift[...])).astype(LOW)
        mixed_ref[place, :] = mixed
        pres.append(dot(mixed, hidden_weight[...]))
    finals = []
    for at, own in enumerate(owns):
        pre = pres[at] + hidden_bias[...]
        pre_ref[own, :] = pre.astype(LOW)
        act = (pre * sigmoid(pre)).astype(LOW)
        finals.append(scaled[at] + dot(act, output_weight[...]))
    for at, own in enumerate(owns):
        final = finals[at]
        final_ref[own, :] = final
        mask = row_mask(node_count, first + at * graphs, graphs, slots, width)
        kept = mask * final
        up = mask * cotangent_ref[own, :].astype(F32)
        add_rows(
            stats,
            (column_sum(kept), column_sum(kept * final), column_sum(up), column_sum(up * final)),
        )
    send_rows(stats, sent_stats)


def mix_back_kernel(
    node_count,
    final_ref,
    pre_ref,
    local_hat_ref,
    attend_hat_ref,
    mixed_ref,
    cotangent_ref,
    branch_stats,
    sent_final,
    final_gain,
    final_shift,
    hidden_weight,
    output_weight,
    d_mixed_ref,
    result_ref,
    weight_grad,
    final_gain_grad,
    final_shift_grad,
    sent_stats,
    stats,
    final_sums,
):
    step = pl.program_id(0)
    first = step * MIX_GROUP
    rows, width = cotangent_ref.shape
    slots = rows // MIX_GROUP

    @pl.when(step == 0)
    def _():
        stats[...] = jnp.zeros_like(stats)
        weight_grad[...] = jnp.zeros_like(weight_grad)
        sum_rows(sent_final, final_sums)

    count = branch_stats[4:5, :]
    per_node = 1.0 / count
    center, inv = norm_rows(final_sums[0:1, :], final_sums[1:2, :], count)
    shift_grad = final_sums[2:3, :]
    gain_grad = inv * (final_sums[3:4, :] - center * shift_grad)
    final_gain_grad[...] = gain_grad
    final_shift_grad[...] = shift_grad
    part, graphs = rows // PARTS, MIX_GROUP // PARTS
    owns = [slice(at * part, (at + 1) * part) for at in range(PARTS)]
    places = [held_rows(step * PARTS + at, part) for at in range(PARTS)]
    d_finals, d_branches, d_acts = [], [], []
    for at, own in enumerate(owns):
        mask = row_mask(node_count, first + at * graphs, graphs, slots, width)
        final_hat = (final_ref[own, :] - center) * inv
        result_ref[own, :] = (mask * (final_hat * final_gain[...] + final_shift[...])).astype(LOW)
        pulled = shift_grad * per_node + final_hat * (gain_grad * per_node)
        d_finals.append(
            (inv * final_gain[...]) * (mask * (cotangent_ref[own, :].astype(F32) - pulled))
        )
        d_branches.append(d_finals[-1].astype(LOW))
        d_acts.append(dot_nt(d_branches[-1], output_weight[...]))
    acts, d_pres, bias_sums = [], [], []
    for at, own in enumerate(owns):
        pre = pre_ref[own, :].astype(F32)
        sig = sigmoid(pre)
        acts.append((pre * sig).astype(LOW))
        d_pres.append((d_acts[at] * (sig * (1.0 + pre * (1.0 - sig)))).astype(LOW))
        bias_sums.append(column_sum(d_pres[-1].astype(F32)))
    backs = [dot_nt(d_pre, hidden_weight[...]) for d_pre in d_pres]
    d_pre = jnp.concatenate(d_pres, axis=0)
    weight_grad[2 * width :, :] += dot_tn(
        jnp.concatenate(acts, axis=0), jnp.concatenate(d_branches, axis=0)
    )
    mixed = mixed_ref[held_rows(step, rows), :]
    for at in range(2):
        weight_grad[at * width : (at + 1) * width, :] += dot_tn(
            mixed, d_pre[:, at * width : (at + 1) * width]
        )
    for at, place in enumerate(places):
        d_mixed = d_finals[at] + backs[at]
        d_mixed_ref[owns[at], :] = d_mixed.astype(LOW)
        add_rows(
            stats,
            (
                column_sum(d_mixed),
                column_sum(d_mixed * local_hat_ref[place, :].astype(F32)),
                column_sum(d_mixed * attend_hat_ref[place, :].astype(F32)),
                bias_sums[at][:, :width],
                bias_sums[at][:, width:],
            ),
        )
    send_rows(stats, sent_stats)


def branch_back(d_mixed, hat, mask, scale, shift_grad, gain_grad, count):
    per_node = 1.0 / count
    return scale * (d_mixed - mask * (shift_grad * per_node + hat * (gain_grad * per_node)))


def gcn_back_kernel(
    node_count,
    d_mixed_ref,
    local_hat_ref,
    inverse_ref,
    ratio_ref,
    gate_ref,
    sent_ref,
    slope_ref,
    node_ref,
    edge_ref,
    source_ref,
    target_ref,
    branch_stats,
    sent_back,
    local_gain,
    gcn_weight,
    node_part_ref,
    d_hats,
    weight_grad,
    back_stats,
    local_gain_grad,
    local_shift_grad,
    attend_gain_grad,
    attend_shift_grad,
    bias_grad,
    d_proj,
):
    step = pl.program_id(0)
    first = step * GROUP
    width = node_ref.shape[1]
    slots = node_ref.shape[0] // GROUP
    edges = edge_ref.shape[0] // GROUP

    @pl.when(step == 0)
    def _():
        weight_grad[...] = jnp.zeros_like(weight_grad)
        sum_rows(sent_back, back_stats)
        local_shift_grad[...] = back_stats[0:1, :]
        local_gain_grad[...] = back_stats[1:2, :]
        attend_shift_grad[...] = back_stats[0:1, :]
        attend_gain_grad[...] = back_stats[2:3, :]
        bias_grad[:, :width] = back_stats[3:4, :]
        bias_grad[:, width:] = back_stats[4:5, :]

    count = branch_stats[4:5, :]
    _, inv = norm_rows(branch_stats[0:1, :], branch_stats[1:2, :], count)
    mask = row_mask(node_count, first, GROUP, slots, width)
    d_local = branch_back(
        d_mixed_ref[...].astype(F32),
        local_hat_ref[...].astype(F32),
        mask,
        inv * local_gain[...],
        back_stats[0:1, :],
        back_stats[1:2, :],
        count,
    )
    numer = d_local * inverse_ref[...].astype(F32)
    d_denom = (-numer * ratio_ref[...].astype(F32)).astype(LOW)
    d_numer = numer.astype(LOW)
    d_proj[:, :width] = d_local.astype(LOW)
    hots = [end_hots(source_ref, target_ref, at, slots) for at in range(GROUP)]
    backs = []
    for at in range(GROUP):
        rows = slice(at * slots, (at + 1) * slots)
        pair = jnp.concatenate([d_numer[rows], d_denom[rows]], axis=1)
        backs.append(dot_tn(hots[at][slots:], pair))
    pairs = []
    for at in range(GROUP):
        edge_rows = slice(at * edges, (at + 1) * edges)
        d_message = backs[at][:, :width]
        d_gate = backs[at][:, width:] + d_message * sent_ref[edge_rows, :].astype(F32)
        d_sent = (d_message * gate_ref[edge_rows, :].astype(F32)).astype(LOW)
        d_hat = (d_gate * slope_ref[edge_rows, :].astype(F32)).astype(LOW)
        d_hats[edge_rows, :] = d_hat
        pairs.append(jnp.concatenate([d_sent, d_hat], axis=1))
    pulls = [dot(hots[at], pairs[at]) for at in range(GROUP)]
    for at in range(GROUP):
        rows = slice(at * slots, (at + 1) * slots)
        pulled = pulls[at].astype(LOW)
        d_proj[rows, width : 2 * width] = pulled[:slots, :width]
        d_proj[rows, 2 * width : 3 * width] = pulled[slots:, width:]
        d_proj[rows, 3 * width :] = pulled[:slots, width:]
    weight_grad[4 * width :, :] += dot_tn(edge_ref[...], d_hats[...])
    for at in range(4):
        columns = slice(at * width, (at + 1) * width)
        weight_grad[columns, :] += dot_tn(node_ref[...], d_proj[:, columns])
    node_part_ref[...] = (d_local + dot_nt(d_proj[...], gcn_weight[...])).astype(LOW)


def attend_back_kernel(
    node_count,
    d_mixed_ref,
    attend_hat_ref,
    qkv_ref,
    prob_ref,
    attended_ref,
    node_ref,
    node_part_ref,
    branch_stats,
    back_stats,
    attend_gain,
    attend_out,
    direct_ref,
    d_qkv,
    weight_grad,
):
    step = pl.program_id(0)
    first = step * GROUP
    width = node_ref.shape[1]
    slots = node_ref.shape[0] // GROUP

    @pl.when(step == 0)
    def _():
        weight_grad[...] = jnp.zeros_like(weight_grad)

    count = branch_stats[4:5, :]
    _, inv = norm_rows(branch_stats[2:3, :], branch_stats[3:4, :], count)
    mask = row_mask(node_count, first, GROUP, slots, width)
    d_attend = branch_back(
        d_mixed_ref[...].astype(F32),
        attend_hat_ref[...].astype(F32),
        mask,
        inv * attend_gain[...],
        back_stats[0:1, :],
        back_stats[2:3, :],
        count,
    )
    d_attn = d_attend.astype(LOW)
    weight_grad[3 * width :, :] += dot_tn(attended_ref[...], d_attn)
    d_att = dot_nt(d_attn, attend_out[...]).astype(LOW)
    scale = HEAD_SIZE ** (-0.5)
    pieces = [(at, half) for at in range(GROUP) for half in range(width // HALF)]

    def place(at, half, part=0):
        first_lane = part * width + half * HALF
        return slice(at * slots, (at + 1) * slots), slice(first_lane, first_lane + HALF)

    def prob_place(at, half):
        return slice(at * slots, (at + 1) * slots), slice(half * 2 * HALF, (half + 1) * 2 * HALF)

    masks = head_masks(slots)
    d_att_blocks = {key: head_blocks(d_att[place(*key)], masks) for key in pieces}
    d_probs = {key: dot_nt(qkv_ref[place(*key, 2)], d_att_blocks[key]) for key in pieces}
    for key in pieces:
        d_values = dot(prob_ref[prob_place(*key)], d_att_blocks[key])
        d_qkv[place(*key, 2)] = d_values.astype(LOW)
    d_scores = {}
    for key in pieces:
        probs = prob_ref[prob_place(*key)].astype(F32)
        weighted = probs * d_probs[key]
        d_scores[key] = (weighted - probs * column_sum(weighted)).astype(LOW)
    for key in pieces:
        d_keys = dot(d_scores[key], head_blocks(qkv_ref[place(*key)], masks))
        d_qkv[place(*key, 1)] = (d_keys * scale).astype(LOW)
    stacks = {key: dot_tn(d_scores[key], qkv_ref[place(*key, 1)]) for key in pieces}
    for key in pieces:
        d_qkv[place(*key)] = (head_merge(stacks[key], slots) * scale).astype(LOW)
    for at in range(3):
        columns = slice(at * width, (at + 1) * width)
        weight_grad[columns, :] += dot_tn(node_ref[...], d_qkv[:, columns])
    direct_ref[...] = (node_part_ref[...].astype(F32) + d_attend).astype(LOW)


def edge_out_kernel(d_hat_ref, edge_weight, edge_out_ref):
    edge_out_ref[...] = dot_nt(d_hat_ref[...], edge_weight[...])


def node_out_kernel(direct_ref, d_qkv_ref, attend_weight, node_out_ref):
    node_out_ref[...] = direct_ref[...].astype(F32) + dot_nt(d_qkv_ref[...], attend_weight[...])


def run_blocks(kernel, steps, limit, args, outs, scratch=(), flops=0):
    def spec(kind, shape):
        if kind == "scalar":
            return pl.BlockSpec(memory_space=pltpu.SMEM)
        if kind == "held":
            return pl.BlockSpec(memory_space=pltpu.VMEM)
        if kind == "rows":
            return pl.BlockSpec((shape[0] // steps, shape[1]), lambda step: (step, 0))
        return pl.BlockSpec(shape, lambda step: (0,) * len(shape))

    def keep(kind, item):
        return pltpu.with_memory_space_constraint(item, pltpu.VMEM) if kind == "held" else item

    moved = sum(item.size * item.dtype.itemsize for _, item in args)
    return pl.pallas_call(
        kernel,
        grid=(steps,),
        in_specs=[spec(kind, item.shape) for kind, item in args],
        out_specs=[spec(kind, shape) for kind, shape, _ in outs],
        out_shape=[
            (pltpu.VMEM if kind == "held" else jax.ShapeDtypeStruct)(shape, dtype)
            for kind, shape, dtype in outs
        ],
        scratch_shapes=list(scratch),
        compiler_params=pltpu.CompilerParams(
            dimension_semantics=("arbitrary",), vmem_limit_bytes=limit * MIB
        ),
        cost_estimate=pl.CostEstimate(flops=flops, bytes_accessed=moved, transcendentals=0),
    )(*[keep(kind, item) for kind, item in args])


def all_share(values):
    return lax.all_to_all(values, "graphs", 0, 0)


def swap(values, mask, devices):
    return lax.ppermute(values, "graphs", [(at, at ^ mask) for at in range(devices)])


def side(mask):
    return (lax.axis_index("graphs") // mask) % 2


def halve(values, mask, devices):
    pair = values.reshape((2, values.shape[0] // 2) + values.shape[1:])
    mine = lax.dynamic_index_in_dim(pair, side(mask), 0, keepdims=False)
    other = lax.dynamic_index_in_dim(pair, 1 - side(mask), 0, keepdims=False)
    return mine, swap(other, mask, devices)


def keep_half(values, mask, devices):
    mine, other = halve(values, mask, devices)
    return mine + other


def chip_orders(devices):
    masks = [1 << bit for bit in range(1, devices.bit_length() - 1)]
    return masks, masks[1::-1] + masks[2:]


def work_beside(mine, others, work):
    if work is None:
        return mine, others, None
    kernel, item = work
    last, item = lax.optimization_barrier((mine[0], item))
    got, out = lax.optimization_barrier((others[0], kernel(item)))
    mine, others = [last, *mine[1:]], [got, *others[1:]]
    return mine, others, out


def weight_sums(parts, devices, beside):
    first, second = chip_orders(devices)
    outs, step = [], 0
    for masks in zip(first[1:] + [0], second):
        halves = [halve(part, mask, devices) if mask else (part, None) for part, mask in zip(parts, masks)]
        mine = [pair[0] for pair in halves]
        others = [pair[1] for pair in halves if pair[1] is not None]
        mine, others, out = work_beside(mine, others, beside.get(step))
        offset = len(parts) - len(others)
        parts = list(mine)
        if offset:
            parts[1] = parts[1] + others[0]
        else:
            parts = [own + other for own, other in zip(mine, others)]
        outs, step = outs + [out], step + 1
    for masks in zip(reversed(first), reversed(second)):
        others = [swap(part, mask, devices) for part, mask in zip(parts, masks)]
        parts, others, out = work_beside(parts, others, beside.get(step))
        parts = [
            jnp.where(side(mask) == 0, jnp.concatenate([own, other]), jnp.concatenate([other, own]))
            for own, other, mask in zip(parts, others, masks)
        ]
        outs, step = outs + [out], step + 1
    others = [swap(part, 1, devices) for part in parts]
    return parts, others, [out for out in outs if out is not None]


def place_kernel(chunks, core, *refs):
    mine, other, outs = refs[:2], refs[2:4], refs[4:]
    for flip in range(2):

        @pl.when(core[0] == flip)
        def _():
            for part, row, rows, places in chunks:
                for half, (out, to_row, to_column) in enumerate(places):
                    source = (mine if half == flip else other)[part]
                    columns = slice(to_column, to_column + source.shape[1])
                    outs[out][to_row : to_row + rows, columns] = source[row : row + rows, :]


def place_sums(parts, others, stacks, shapes):
    width = parts[0].shape[1]
    unit = width // 2
    chunks, at = [], 0
    for index, stack in enumerate(stacks):
        starts, begin = [], 0
        for out in (2 * index, 2 * index + 1):
            rows, columns = shapes[out]
            starts.append((begin, out, rows))
            begin += rows * columns // width

        def place(row):
            begin, out, rows = starts[0] if row < starts[1][0] else starts[1]
            return out, (row - begin) % rows, (row - begin) // rows * width

        half = stack.shape[0] // 2
        for row in range(0, half, unit):
            part = 0 if at < parts[0].shape[0] else 1
            chunks.append((part, at - part * parts[0].shape[0], unit, (place(row), place(half + row))))
            at += unit
    core = side(1).astype(jnp.int32)[None]
    inside = pl.BlockSpec(memory_space=pltpu.VMEM)
    return pl.pallas_call(
        functools.partial(place_kernel, chunks),
        in_specs=[pl.BlockSpec(memory_space=pltpu.SMEM)] + [inside] * 4,
        out_specs=[inside] * len(shapes),
        out_shape=[jax.ShapeDtypeStruct(shape, F32) for shape in shapes],
        compiler_params=pltpu.CompilerParams(vmem_limit_bytes=40 * MIB),
    )(core, *parts, *others)


def on_device(
    devices,
    node_input,
    edge_input,
    node_count,
    edge_count,
    edge_source,
    edge_target,
    gcn_weight,
    edge_weight,
    attend_weight,
    attend_out,
    local_gain,
    local_shift,
    attend_gain,
    attend_shift,
    hidden_weight,
    hidden_bias,
    output_weight,
    final_gain,
    final_shift,
    cotangent,
):
    graphs, edges = edge_source.shape
    node_rows, width = node_input.shape
    edge_rows = edge_input.shape[0]
    slots = node_rows // graphs
    hidden = hidden_weight.shape[1]
    steps = graphs // GROUP
    local_gain, local_shift, attend_gain, attend_shift, final_gain, final_shift = [
        ("whole", item[None])
        for item in (local_gain, local_shift, attend_gain, attend_shift, final_gain, final_shift)
    ]
    counts = ("scalar", node_count)
    node_arg = ("rows", node_input)
    edge_arg = ("rows", edge_input)
    cotangent_arg = ("rows", cotangent)
    ends = [("rows", edge_source), ("rows", edge_target)]
    node_shape, edge_shape = node_input.shape, edge_input.shape
    sums, shares = (8, width), (devices, 1, 5 * width)
    stats = pltpu.VMEM(sums, F32)
    (
        local_pre,
        attend_pre,
        inverse,
        ratio,
        gate,
        sent,
        slope,
        qkv,
        probs,
        attended,
        branch_shares,
    ) = run_blocks(
        forward_kernel,
        steps,
        60,
        [counts, ("scalar", edge_count), node_arg, edge_arg]
        + ends
        + [("whole", item) for item in (gcn_weight, edge_weight, attend_weight, attend_out)],
        [
            ("rows", node_shape, F32),
            ("rows", node_shape, F32),
            ("rows", node_shape, LOW),
            ("rows", node_shape, LOW),
            ("rows", edge_shape, LOW),
            ("rows", edge_shape, LOW),
            ("rows", edge_shape, LOW),
            ("rows", (node_rows, 3 * width), LOW),
            ("rows", (node_rows, (width // HEAD_SIZE) * slots), LOW),
            ("rows", node_shape, LOW),
            ("whole", shares, F32),
        ],
        scratch=[stats],
    )
    local_hat, attend_hat, mixed, pre, final, branch_stats, final_shares = run_blocks(
        mix_kernel,
        graphs // MIX_GROUP,
        50,
        [counts, ("rows", local_pre), ("rows", attend_pre), cotangent_arg]
        + [("whole", all_share(branch_shares)), local_gain, local_shift, attend_gain, attend_shift]
        + [("whole", hidden_weight)]
        + [("whole", hidden_bias[None]), ("whole", output_weight)],
        [
            ("held", node_shape, LOW),
            ("held", node_shape, LOW),
            ("held", node_shape, LOW),
            ("rows", (node_rows, hidden), LOW),
            ("rows", node_shape, F32),
            ("whole", sums, F32),
            ("whole", (devices, 1, 4 * width), F32),
        ],
        scratch=[stats],
    )
    branch_arg = ("whole", branch_stats)
    d_mixed, result, mix_grads, final_gain_grad, final_shift_grad, back_shares = run_blocks(
        mix_back_kernel,
        graphs // MIX_GROUP,
        50,
        [counts, ("rows", final), ("rows", pre), ("held", local_hat)]
        + [("held", attend_hat), ("held", mixed), cotangent_arg, branch_arg]
        + [("whole", all_share(final_shares)), final_gain, final_shift]
        + [("whole", hidden_weight), ("whole", output_weight)],
        [
            ("rows", node_shape, LOW),
            ("rows", node_shape, LOW),
            ("whole", (2 * hidden, width), F32),
            ("whole", (1, width), F32),
            ("whole", (1, width), F32),
            ("whole", shares, F32),
        ],
        scratch=[stats, stats],
        flops=8 * node_rows * width * hidden,
    )
    (
        node_part,
        d_hats,
        gcn_grads,
        back_stats,
        local_gain_grad,
        local_shift_grad,
        attend_gain_grad,
        attend_shift_grad,
        bias_grad,
    ) = run_blocks(
        gcn_back_kernel,
        steps,
        60,
        [counts, ("rows", d_mixed), ("rows", local_hat), ("rows", inverse), ("rows", ratio)]
        + [("rows", gate), ("rows", sent), ("rows", slope), node_arg, edge_arg]
        + ends
        + [branch_arg, ("whole", all_share(back_shares)), local_gain, ("whole", gcn_weight)],
        [
            ("rows", node_shape, LOW),
            ("rows", edge_shape, LOW),
            ("whole", (5 * width, width), F32),
            ("whole", sums, F32),
        ]
        + [("whole", (1, width), F32)] * 4
        + [("whole", (1, hidden), F32)],
        scratch=[pltpu.VMEM((node_rows // steps, 4 * width), LOW)],
    )
    gcn_core = keep_half(gcn_grads, 1, devices)
    orders = chip_orders(devices)
    cut = 2 * width
    early = jnp.concatenate([keep_half(mix_grads, 1, devices), gcn_core[:cut]])
    early, got = halve(early, orders[0][0], devices)
    early, qkv = lax.optimization_barrier((early, qkv))
    direct, d_qkv, attend_grads = run_blocks(
        attend_back_kernel,
        steps,
        60,
        [counts, ("rows", d_mixed), ("rows", attend_hat), ("rows", qkv), ("rows", probs)]
        + [("rows", attended), node_arg, ("rows", node_part), branch_arg, ("whole", back_stats)]
        + [attend_gain, ("whole", attend_out)],
        [
            ("rows", node_shape, LOW),
            ("rows", (node_rows, 3 * width), LOW),
            ("whole", (4 * width, width), F32),
        ],
    )

    def give_edges(d_hats):
        return run_blocks(
            edge_out_kernel,
            graphs // MIX_GROUP,
            60,
            [("rows", d_hats), ("whole", edge_weight)],
            [("rows", edge_shape, F32)],
            flops=2 * edge_rows * width * width,
        )[0]

    def give_nodes(d_qkv):
        return run_blocks(
            node_out_kernel,
            graphs // MIX_GROUP,
            60,
            [("rows", direct), ("rows", d_qkv), ("whole", attend_weight)],
            [("rows", node_shape, F32)],
            flops=6 * node_rows * width * width,
        )[0]

    got, attend_grads = lax.optimization_barrier((got, attend_grads))
    late = jnp.concatenate([gcn_core[cut:], keep_half(attend_grads, 1, devices)])
    beside = {0: (give_edges, d_hats), 2 * len(orders[0]) - 1: (give_nodes, d_qkv)}
    parts, others, (edge_out, node_out) = weight_sums([early + got, late], devices, beside)
    hidden_grad, output_grad, gcn_grad, edge_grad, attend_grad, attend_out_grad = place_sums(
        parts,
        others,
        (mix_grads, gcn_grads, attend_grads),
        [hidden_weight.shape, output_weight.shape, gcn_weight.shape]
        + [edge_weight.shape, attend_weight.shape, attend_out.shape],
    )
    return (
        result,
        node_out,
        edge_out,
        gcn_grad,
        edge_grad,
        attend_grad,
        attend_out_grad,
        local_gain_grad[0],
        local_shift_grad[0],
        attend_gain_grad[0],
        attend_shift_grad[0],
        hidden_grad,
        bias_grad[0],
        output_grad,
        final_gain_grad[0],
        final_shift_grad[0],
    )


def solution(mesh):
    rows = P("graphs", None)
    each = P("graphs")
    return jax.shard_map(
        functools.partial(on_device, mesh.shape["graphs"]),
        mesh=mesh,
        in_specs=(rows, rows, each, each, rows, rows) + (P(),) * 13 + (rows,),
        out_specs=(rows, rows, rows) + (P(),) * 13,
        check_vma=False,
    )
```

```python
import functools
import math

import jax
import jax.numpy as jnp
from jax import lax
from jax.experimental import pallas as pl
from jax.experimental.pallas import tpu as pltpu
from jax.sharding import PartitionSpec as P

HEAD_SIZE = 32
HALF = 128
EXP2_SCALE = HEAD_SIZE ** (-0.5) / math.log(2.0)
GROUP = 16
MIX_GROUP = 16
SUB = 4
PARTS = 2
EPS = 1e-05
F32 = jnp.float32
LOW = jnp.bfloat16
MIB = 1024 * 1024


def dot(left, right):
    return jnp.dot(left, right, preferred_element_type=F32)


def dot_nt(left, right):
    return lax.dot_general(left, right, (((1,), (1,)), ((), ())), preferred_element_type=F32)


def dot_tn(left, right):
    return lax.dot_general(left, right, (((0,), (0,)), ((), ())), preferred_element_type=F32)


def sigmoid(values):
    return 0.5 * jnp.tanh(0.5 * values) + 0.5


def norm_rows(total, squares, count):
    center = total / count
    return center, lax.rsqrt(squares / count - center * center + EPS)


def one_hot(index_row, slots):
    grid = lax.broadcasted_iota(jnp.int32, (slots, index_row.shape[1]), 0)
    return jnp.where(grid == index_row, 1.0, 0.0)


def end_hots(source_ref, target_ref, at, slots):
    ends = [one_hot(ref[at : at + 1, :], slots) for ref in (source_ref, target_ref)]
    return jnp.concatenate(ends, axis=0).astype(LOW)


def row_mask(counts, first, graphs, slots, width):
    grid = lax.broadcasted_iota(jnp.int32, (slots, width), 0)
    return jnp.concatenate(
        [jnp.where(grid < counts[first + at], 1.0, 0.0) for at in range(graphs)], axis=0
    )


def head_masks(slots):
    head = lax.broadcasted_iota(jnp.int32, (slots, HALF), 1) // HEAD_SIZE
    flat = [jnp.where(head == at, 1.0, 0.0).astype(LOW) for at in range(HALF // HEAD_SIZE)]
    row = lax.broadcasted_iota(jnp.int32, (HALF, 2 * slots), 0) // HEAD_SIZE
    lane = lax.broadcasted_iota(jnp.int32, (HALF, 2 * slots), 1) // slots
    tall = [jnp.where(row == lane + at, 1.0, 0.0).astype(LOW) for at in range(0, HALF // HEAD_SIZE, 2)]
    return flat, tall


def head_blocks(rows, masks):
    return jnp.concatenate([rows * mask for mask in masks[0]], axis=0)


def head_blocks_t(rows, masks):
    turned = rows.T
    twice = jnp.concatenate([turned, turned], axis=1)
    return jnp.concatenate([twice * mask for mask in masks[1]], axis=1)


def heads_turn(wide, slots):
    pairs = [wide[:, at : at + 2 * slots].T for at in range(0, wide.shape[1], 2 * slots)]
    return jnp.concatenate(
        [part for pair in pairs for part in (pair[:slots], pair[slots:])], axis=1
    )


def head_merge(stacked, slots):
    head = lax.broadcasted_iota(jnp.int32, (slots, HALF), 1) // HEAD_SIZE
    merged = stacked[:slots]
    for at in range(1, HALF // HEAD_SIZE):
        merged = jnp.where(head == at, stacked[at * slots : (at + 1) * slots], merged)
    return merged


def column_sum(values):
    return jnp.sum(values, axis=0, keepdims=True)


def add_rows(stats, rows):
    for at, row in enumerate(rows):
        stats[at : at + 1, :] += row


def send_rows(stats, sent_ref):
    @pl.when(pl.program_id(0) == pl.num_programs(0) - 1)
    def _():
        rows = sent_ref.shape[2] // stats.shape[1]
        line = jnp.concatenate([stats[at : at + 1, :] for at in range(rows)], axis=1)
        sent_ref[...] = jnp.broadcast_to(line[None], sent_ref.shape)


def sum_rows(sent_ref, stats):
    line = jnp.sum(sent_ref[...], axis=0)
    width = stats.shape[1]
    for at in range(line.shape[1] // width):
        stats[at : at + 1, :] = line[:, at * width : (at + 1) * width]


def held_rows(step, rows):
    return pl.ds(pl.multiple_of(step * rows, rows), rows)


def forward_kernel(
    node_count,
    edge_count,
    node_ref,
    edge_ref,
    source_ref,
    target_ref,
    gcn_weight,
    edge_weight,
    attend_weight,
    attend_out,
    local_ref,
    attend_ref,
    inverse_ref,
    ratio_ref,
    gate_ref,
    sent_ref,
    slope_ref,
    qkv_ref,
    prob_ref,
    attended_ref,
    sent_stats,
    stats,
):
    step = pl.program_id(0)
    first = step * GROUP
    width = node_ref.shape[1]
    slots = node_ref.shape[0] // GROUP
    edges = edge_ref.shape[0] // GROUP

    @pl.when(step == 0)
    def _():
        stats[...] = jnp.zeros_like(stats)

    edge_grid = lax.broadcasted_iota(jnp.int32, (edges, width), 0)
    node_grid = lax.broadcasted_iota(jnp.int32, (slots, 2 * HALF), 0)
    nothing = jnp.zeros((slots, width), LOW)
    masks = head_masks(slots)
    halves = range(width // HALF)
    held = {}

    def node_rows(at):
        return slice(at * slots, (at + 1) * slots)

    def edge_rows(at):
        return slice(at * edges, (at + 1) * edges)

    def take(name, at, height):
        row = at % SUB * height
        return held[name, at // SUB][row : row + height]

    def project_nodes(sub):
        rows = slice(sub * SUB * slots, (sub + 1) * SUB * slots)
        proj = dot(node_ref[rows, :], gcn_weight[...])
        held["own", sub] = proj[:, :width]
        held["parts", sub] = proj[:, width:].astype(LOW)

    def project_edges(sub):
        rows = slice(sub * SUB * edges, (sub + 1) * SUB * edges)
        held["edge", sub] = dot(edge_ref[rows, :], edge_weight[...])

    def project_heads(sub):
        rows = slice(sub * SUB * slots, (sub + 1) * SUB * slots)
        held["qkv", sub] = dot(node_ref[rows, :], attend_weight[...]).astype(LOW)
        qkv_ref[rows, :] = held["qkv", sub]

    def gather(at):
        parts = take("parts", at, slots)
        held["hot", at] = end_hots(source_ref, target_ref, at, slots)
        spread = jnp.concatenate(
            [
                jnp.concatenate([parts[:, 2 * width :], parts[:, :width]], axis=1),
                jnp.concatenate([parts[:, width : 2 * width], nothing], axis=1),
            ],
            axis=0,
        )
        held["gathered", at] = dot_tn(held["hot", at], spread)

    def score(at):
        qkv = take("qkv", at, slots)
        for half in halves:
            query = qkv[:, half * HALF : (half + 1) * HALF]
            key = qkv[:, width + half * HALF : width + (half + 1) * HALF]
            held["scores", at, half] = dot(key, head_blocks_t(query, masks))

    def message(at):
        rows, gathered = edge_rows(at), held.pop(("gathered", at))
        sent = gathered[:, width:]
        gate_sig = sigmoid(take("edge", at, edges) + gathered[:, :width])
        kept = jnp.where(edge_grid < edge_count[first + at], gate_sig, 0.0)
        gate = kept.astype(LOW)
        gate_ref[rows, :] = gate
        sent_ref[rows, :] = sent.astype(LOW)
        slope_ref[rows, :] = (kept * (1.0 - gate_sig)).astype(LOW)
        sent_on = (gate.astype(F32) * sent).astype(LOW)
        held["message", at] = jnp.concatenate([sent_on, gate], axis=1)

    def soften(at):
        key_kept = node_grid < node_count[first + at]
        for half in halves:
            shown = jnp.where(key_kept, held.pop(("scores", at, half)), -1e30)
            expo = jnp.exp2((shown - jnp.max(shown, axis=0, keepdims=True)) * EXP2_SCALE)
            probs = (expo * (1.0 / column_sum(expo))).astype(LOW)
            held["probs", at, half] = probs
            prob_ref[node_rows(at), half * 2 * HALF : (half + 1) * 2 * HALF] = probs

    def pool(at):
        held["pooled", at] = dot(held.pop(("hot", at))[slots:], held.pop(("message", at)))

    def attend(at):
        qkv = take("qkv", at, slots)
        for half in halves:
            value = qkv[:, 2 * width + half * HALF : 2 * width + (half + 1) * HALF]
            held["spread", at, half] = dot_tn(held.pop(("probs", at, half)), value)

    def finish(at):
        rows, pooled = node_rows(at), held.pop(("pooled", at))
        inverse = 1.0 / (pooled[:, width:] + 1e-06)
        ratio = pooled[:, :width] * inverse
        inverse_ref[rows, :] = inverse.astype(LOW)
        ratio_ref[rows, :] = ratio.astype(LOW)
        local_ref[rows, :] = node_ref[rows, :].astype(F32) + take("own", at, slots) + ratio
        for half in halves:
            merged = head_merge(held.pop(("spread", at, half)), slots)
            attended_ref[rows, half * HALF : (half + 1) * HALF] = merged.astype(LOW)

    dense = (project_nodes, project_edges, project_heads)
    for stage in dense:
        stage(0)
    for tick in range(GROUP + 3):
        sub, phase = tick // SUB + 1, tick % SUB
        if sub < GROUP // SUB and phase < len(dense):
            dense[phase](sub)
        for lag, stages in enumerate(((gather, score), (message, soften), (pool, attend), (finish,))):
            if 0 <= tick - lag < GROUP:
                for stage in stages:
                    stage(tick - lag)
    attend_pre = node_ref[...].astype(F32) + dot(attended_ref[...], attend_out[...])
    attend_ref[...] = attend_pre
    local_pre = local_ref[...]
    mask = row_mask(node_count, first, GROUP, slots, width)
    local_kept = mask * local_pre
    attend_kept = mask * attend_pre
    add_rows(
        stats,
        (
            column_sum(local_kept),
            column_sum(local_kept * local_pre),
            column_sum(attend_kept),
            column_sum(attend_kept * attend_pre),
            column_sum(mask),
        ),
    )
    send_rows(stats, sent_stats)


def mix_kernel(
    node_count,
    local_ref,
    attend_ref,
    cotangent_ref,
    sent_branch,
    local_gain,
    local_shift,
    attend_gain,
    attend_shift,
    hidden_weight,
    hidden_bias,
    output_weight,
    local_hat_ref,
    attend_hat_ref,
    mixed_ref,
    pre_ref,
    final_ref,
    branch_stats,
    sent_stats,
    stats,
):
    step = pl.program_id(0)
    first = step * MIX_GROUP
    rows, width = cotangent_ref.shape
    slots = rows // MIX_GROUP

    @pl.when(step == 0)
    def _():
        stats[...] = jnp.zeros_like(stats)
        sum_rows(sent_branch, branch_stats)

    count = branch_stats[4:5, :]
    local_center, local_inv = norm_rows(branch_stats[0:1, :], branch_stats[1:2, :], count)
    attend_center, attend_inv = norm_rows(branch_stats[2:3, :], branch_stats[3:4, :], count)
    part, graphs = rows // PARTS, MIX_GROUP // PARTS
    owns = [slice(at * part, (at + 1) * part) for at in range(PARTS)]
    places = [held_rows(step * PARTS + at, part) for at in range(PARTS)]
    scaled, pres = [], []
    for own, place in zip(owns, places):
        local_hat = (local_ref[own, :] - local_center) * local_inv
        attend_hat = (attend_ref[own, :] - attend_center) * attend_inv
        local_hat_ref[place, :] = local_hat.astype(LOW)
        attend_hat_ref[place, :] = attend_hat.astype(LOW)
        scaled.append(local_hat * local_gain[...] + attend_hat * attend_gain[...])
        mixed = (scaled[-1] + (local_shift[...] + attend_shift[...])).astype(LOW)
        mixed_ref[place, :] = mixed
        pres.append(dot(mixed, hidden_weight[...]))
    finals = []
    for at, own in enumerate(owns):
        pre = pres[at] + hidden_bias[...]
        pre_ref[own, :] = pre.astype(LOW)
        act = (pre * sigmoid(pre)).astype(LOW)
        finals.append(scaled[at] + dot(act, output_weight[...]))
    for at, own in enumerate(owns):
        final = finals[at]
        final_ref[own, :] = final
        mask = row_mask(node_count, first + at * graphs, graphs, slots, width)
        kept = mask * final
        up = mask * cotangent_ref[own, :].astype(F32)
        add_rows(
            stats,
            (column_sum(kept), column_sum(kept * final), column_sum(up), column_sum(up * final)),
        )
    send_rows(stats, sent_stats)


def mix_back_kernel(
    node_count,
    final_ref,
    pre_ref,
    local_hat_ref,
    attend_hat_ref,
    mixed_ref,
    cotangent_ref,
    branch_stats,
    sent_final,
    final_gain,
    final_shift,
    hidden_weight,
    output_weight,
    d_mixed_ref,
    result_ref,
    weight_grad,
    final_gain_grad,
    final_shift_grad,
    sent_stats,
    stats,
    final_sums,
):
    step = pl.program_id(0)
    first = step * MIX_GROUP
    rows, width = cotangent_ref.shape
    slots = rows // MIX_GROUP

    @pl.when(step == 0)
    def _():
        stats[...] = jnp.zeros_like(stats)
        weight_grad[...] = jnp.zeros_like(weight_grad)
        sum_rows(sent_final, final_sums)

    count = branch_stats[4:5, :]
    per_node = 1.0 / count
    center, inv = norm_rows(final_sums[0:1, :], final_sums[1:2, :], count)
    shift_grad = final_sums[2:3, :]
    gain_grad = inv * (final_sums[3:4, :] - center * shift_grad)
    final_gain_grad[...] = gain_grad
    final_shift_grad[...] = shift_grad
    part, graphs = rows // PARTS, MIX_GROUP // PARTS
    owns = [slice(at * part, (at + 1) * part) for at in range(PARTS)]
    places = [held_rows(step * PARTS + at, part) for at in range(PARTS)]
    d_finals, d_branches, d_acts = [], [], []
    for at, own in enumerate(owns):
        mask = row_mask(node_count, first + at * graphs, graphs, slots, width)
        final_hat = (final_ref[own, :] - center) * inv
        result_ref[own, :] = (mask * (final_hat * final_gain[...] + final_shift[...])).astype(LOW)
        pulled = shift_grad * per_node + final_hat * (gain_grad * per_node)
        d_finals.append(
            (inv * final_gain[...]) * (mask * (cotangent_ref[own, :].astype(F32) - pulled))
        )
        d_branches.append(d_finals[-1].astype(LOW))
        d_acts.append(dot_nt(d_branches[-1], output_weight[...]))
    acts, d_pres, bias_sums = [], [], []
    for at, own in enumerate(owns):
        pre = pre_ref[own, :].astype(F32)
        sig = sigmoid(pre)
        acts.append((pre * sig).astype(LOW))
        d_pres.append((d_acts[at] * (sig * (1.0 + pre * (1.0 - sig)))).astype(LOW))
        bias_sums.append(column_sum(d_pres[-1].astype(F32)))
    backs = [dot_nt(d_pre, hidden_weight[...]) for d_pre in d_pres]
    d_pre = jnp.concatenate(d_pres, axis=0)
    weight_grad[2 * width :, :] += dot_tn(
        jnp.concatenate(acts, axis=0), jnp.concatenate(d_branches, axis=0)
    )
    mixed = mixed_ref[held_rows(step, rows), :]
    for at in range(2):
        weight_grad[at * width : (at + 1) * width, :] += dot_tn(
            mixed, d_pre[:, at * width : (at + 1) * width]
        )
    for at, place in enumerate(places):
        d_mixed = d_finals[at] + backs[at]
        d_mixed_ref[owns[at], :] = d_mixed.astype(LOW)
        add_rows(
            stats,
            (
                column_sum(d_mixed),
                column_sum(d_mixed * local_hat_ref[place, :].astype(F32)),
                column_sum(d_mixed * attend_hat_ref[place, :].astype(F32)),
                bias_sums[at][:, :width],
                bias_sums[at][:, width:],
            ),
        )
    send_rows(stats, sent_stats)


def branch_back(d_mixed, hat, mask, scale, shift_grad, gain_grad, count):
    per_node = 1.0 / count
    return scale * (d_mixed - mask * (shift_grad * per_node + hat * (gain_grad * per_node)))


def gcn_back_kernel(
    node_count,
    d_mixed_ref,
    local_hat_ref,
    inverse_ref,
    ratio_ref,
    gate_ref,
    sent_ref,
    slope_ref,
    node_ref,
    edge_ref,
    source_ref,
    target_ref,
    branch_stats,
    sent_back,
    local_gain,
    gcn_weight,
    node_part_ref,
    d_hats,
    weight_grad,
    back_stats,
    local_gain_grad,
    local_shift_grad,
    attend_gain_grad,
    attend_shift_grad,
    bias_grad,
    d_proj,
):
    step = pl.program_id(0)
    first = step * GROUP
    width = node_ref.shape[1]
    slots = node_ref.shape[0] // GROUP
    edges = edge_ref.shape[0] // GROUP

    @pl.when(step == 0)
    def _():
        weight_grad[...] = jnp.zeros_like(weight_grad)
        sum_rows(sent_back, back_stats)
        local_shift_grad[...] = back_stats[0:1, :]
        local_gain_grad[...] = back_stats[1:2, :]
        attend_shift_grad[...] = back_stats[0:1, :]
        attend_gain_grad[...] = back_stats[2:3, :]
        bias_grad[:, :width] = back_stats[3:4, :]
        bias_grad[:, width:] = back_stats[4:5, :]

    count = branch_stats[4:5, :]
    _, inv = norm_rows(branch_stats[0:1, :], branch_stats[1:2, :], count)
    mask = row_mask(node_count, first, GROUP, slots, width)
    d_local = branch_back(
        d_mixed_ref[...].astype(F32),
        local_hat_ref[...].astype(F32),
        mask,
        inv * local_gain[...],
        back_stats[0:1, :],
        back_stats[1:2, :],
        count,
    )
    numer = d_local * inverse_ref[...].astype(F32)
    d_denom = (-numer * ratio_ref[...].astype(F32)).astype(LOW)
    d_numer = numer.astype(LOW)
    d_proj[:, :width] = d_local.astype(LOW)
    hots = [end_hots(source_ref, target_ref, at, slots) for at in range(GROUP)]
    backs = []
    for at in range(GROUP):
        rows = slice(at * slots, (at + 1) * slots)
        pair = jnp.concatenate([d_numer[rows], d_denom[rows]], axis=1)
        backs.append(dot_tn(hots[at][slots:], pair))
    pairs = []
    for at in range(GROUP):
        edge_rows = slice(at * edges, (at + 1) * edges)
        d_message = backs[at][:, :width]
        d_gate = backs[at][:, width:] + d_message * sent_ref[edge_rows, :].astype(F32)
        d_sent = (d_message * gate_ref[edge_rows, :].astype(F32)).astype(LOW)
        d_hat = (d_gate * slope_ref[edge_rows, :].astype(F32)).astype(LOW)
        d_hats[edge_rows, :] = d_hat
        pairs.append(jnp.concatenate([d_sent, d_hat], axis=1))
    pulls = [dot(hots[at], pairs[at]) for at in range(GROUP)]
    for at in range(GROUP):
        rows = slice(at * slots, (at + 1) * slots)
        pulled = pulls[at].astype(LOW)
        d_proj[rows, width : 2 * width] = pulled[:slots, :width]
        d_proj[rows, 2 * width : 3 * width] = pulled[slots:, width:]
        d_proj[rows, 3 * width :] = pulled[:slots, width:]
    weight_grad[4 * width :, :] += dot_tn(edge_ref[...], d_hats[...])
    for at in range(4):
        columns = slice(at * width, (at + 1) * width)
        weight_grad[columns, :] += dot_tn(node_ref[...], d_proj[:, columns])
    node_part_ref[...] = (d_local + dot_nt(d_proj[...], gcn_weight[...])).astype(LOW)


def attend_back_kernel(
    node_count,
    d_mixed_ref,
    attend_hat_ref,
    qkv_ref,
    prob_ref,
    attended_ref,
    node_ref,
    node_part_ref,
    branch_stats,
    back_stats,
    attend_gain,
    attend_out,
    direct_ref,
    d_qkv,
    weight_grad,
):
    step = pl.program_id(0)
    first = step * GROUP
    width = node_ref.shape[1]
    slots = node_ref.shape[0] // GROUP

    @pl.when(step == 0)
    def _():
        weight_grad[...] = jnp.zeros_like(weight_grad)

    count = branch_stats[4:5, :]
    _, inv = norm_rows(branch_stats[2:3, :], branch_stats[3:4, :], count)
    mask = row_mask(node_count, first, GROUP, slots, width)
    d_attend = branch_back(
        d_mixed_ref[...].astype(F32),
        attend_hat_ref[...].astype(F32),
        mask,
        inv * attend_gain[...],
        back_stats[0:1, :],
        back_stats[2:3, :],
        count,
    )
    d_attn = d_attend.astype(LOW)
    weight_grad[3 * width :, :] += dot_tn(attended_ref[...], d_attn)
    d_att = dot_nt(d_attn, attend_out[...]).astype(LOW)
    scale = HEAD_SIZE ** (-0.5)
    pieces = [(at, half) for at in range(GROUP) for half in range(width // HALF)]

    def place(at, half, part=0):
        first_lane = part * width + half * HALF
        return slice(at * slots, (at + 1) * slots), slice(first_lane, first_lane + HALF)

    def prob_place(at, half):
        return slice(at * slots, (at + 1) * slots), slice(half * 2 * HALF, (half + 1) * 2 * HALF)

    masks = head_masks(slots)
    d_att_blocks = {key: head_blocks(d_att[place(*key)], masks) for key in pieces}
    d_probs = {key: dot_nt(qkv_ref[place(*key, 2)], d_att_blocks[key]) for key in pieces}
    for key in pieces:
        d_values = dot(prob_ref[prob_place(*key)], d_att_blocks[key])
        d_qkv[place(*key, 2)] = d_values.astype(LOW)
    d_scores = {}
    for key in pieces:
        probs = prob_ref[prob_place(*key)].astype(F32)
        weighted = probs * d_probs[key]
        d_scores[key] = (weighted - probs * column_sum(weighted)).astype(LOW)
    for key in pieces:
        d_keys = dot(d_scores[key], head_blocks(qkv_ref[place(*key)], masks))
        d_qkv[place(*key, 1)] = (d_keys * scale).astype(LOW)
    stacks = {key: dot_tn(d_scores[key], qkv_ref[place(*key, 1)]) for key in pieces}
    for key in pieces:
        d_qkv[place(*key)] = (head_merge(stacks[key], slots) * scale).astype(LOW)
    for at in range(3):
        columns = slice(at * width, (at + 1) * width)
        weight_grad[columns, :] += dot_tn(node_ref[...], d_qkv[:, columns])
    direct_ref[...] = (node_part_ref[...].astype(F32) + d_attend).astype(LOW)


def edge_out_kernel(d_hat_ref, edge_weight, edge_out_ref):
    edge_out_ref[...] = dot_nt(d_hat_ref[...], edge_weight[...])


def node_out_kernel(direct_ref, d_qkv_ref, attend_weight, node_out_ref):
    node_out_ref[...] = direct_ref[...].astype(F32) + dot_nt(d_qkv_ref[...], attend_weight[...])


def run_blocks(kernel, steps, limit, args, outs, scratch=(), flops=0):
    def spec(kind, shape):
        if kind == "scalar":
            return pl.BlockSpec(memory_space=pltpu.SMEM)
        if kind == "held":
            return pl.BlockSpec(memory_space=pltpu.VMEM)
        if kind == "rows":
            return pl.BlockSpec((shape[0] // steps, shape[1]), lambda step: (step, 0))
        return pl.BlockSpec(shape, lambda step: (0,) * len(shape))

    def keep(kind, item):
        return pltpu.with_memory_space_constraint(item, pltpu.VMEM) if kind == "held" else item

    moved = sum(item.size * item.dtype.itemsize for _, item in args)
    return pl.pallas_call(
        kernel,
        grid=(steps,),
        in_specs=[spec(kind, item.shape) for kind, item in args],
        out_specs=[spec(kind, shape) for kind, shape, _ in outs],
        out_shape=[
            (pltpu.VMEM if kind == "held" else jax.ShapeDtypeStruct)(shape, dtype)
            for kind, shape, dtype in outs
        ],
        scratch_shapes=list(scratch),
        compiler_params=pltpu.CompilerParams(
            dimension_semantics=("arbitrary",), vmem_limit_bytes=limit * MIB
        ),
        cost_estimate=pl.CostEstimate(flops=flops, bytes_accessed=moved, transcendentals=0),
    )(*[keep(kind, item) for kind, item in args])


def all_share(values):
    return lax.all_to_all(values, "graphs", 0, 0)


def swap(values, mask, devices):
    return lax.ppermute(values, "graphs", [(at, at ^ mask) for at in range(devices)])


def side(mask):
    return (lax.axis_index("graphs") // mask) % 2


def halve(values, mask, devices):
    pair = values.reshape((2, values.shape[0] // 2) + values.shape[1:])
    mine = lax.dynamic_index_in_dim(pair, side(mask), 0, keepdims=False)
    other = lax.dynamic_index_in_dim(pair, 1 - side(mask), 0, keepdims=False)
    return mine, swap(other, mask, devices)


def keep_half(values, mask, devices):
    mine, other = halve(values, mask, devices)
    return mine + other


def chip_orders(devices):
    masks = [1 << bit for bit in range(1, devices.bit_length() - 1)]
    return masks, masks[1::-1] + masks[2:]


def work_beside(mine, others, work):
    if work is None:
        return mine, others, None
    kernel, item = work
    last, item = lax.optimization_barrier((mine[0], item))
    got, out = lax.optimization_barrier((others[0], kernel(item)))
    mine, others = [last, *mine[1:]], [got, *others[1:]]
    return mine, others, out


def weight_sums(parts, devices, beside):
    first, second = chip_orders(devices)
    outs, step = [], 0
    for masks in zip(first[1:] + [0], second):
        halves = [halve(part, mask, devices) if mask else (part, None) for part, mask in zip(parts, masks)]
        mine = [pair[0] for pair in halves]
        others = [pair[1] for pair in halves if pair[1] is not None]
        mine, others, out = work_beside(mine, others, beside.get(step))
        offset = len(parts) - len(others)
        parts = list(mine)
        if offset:
            parts[1] = parts[1] + others[0]
        else:
            parts = [own + other for own, other in zip(mine, others)]
        outs, step = outs + [out], step + 1
    for masks in zip(reversed(first), reversed(second)):
        others = [swap(part, mask, devices) for part, mask in zip(parts, masks)]
        parts, others, out = work_beside(parts, others, beside.get(step))
        parts = [
            jnp.where(side(mask) == 0, jnp.concatenate([own, other]), jnp.concatenate([other, own]))
            for own, other, mask in zip(parts, others, masks)
        ]
        outs, step = outs + [out], step + 1
    others = [swap(part, 1, devices) for part in parts]
    return parts, others, [out for out in outs if out is not None]


def place_kernel(chunks, core, *refs):
    mine, other, outs = refs[:2], refs[2:4], refs[4:]
    for flip in range(2):

        @pl.when(core[0] == flip)
        def _():
            for part, row, rows, places in chunks:
                for half, (out, to_row, to_column) in enumerate(places):
                    source = (mine if half == flip else other)[part]
                    columns = slice(to_column, to_column + source.shape[1])
                    outs[out][to_row : to_row + rows, columns] = source[row : row + rows, :]


def place_sums(parts, others, stacks, shapes):
    width = parts[0].shape[1]
    unit = width // 2
    chunks, at = [], 0
    for index, stack in enumerate(stacks):
        starts, begin = [], 0
        for out in (2 * index, 2 * index + 1):
            rows, columns = shapes[out]
            starts.append((begin, out, rows))
            begin += rows * columns // width

        def place(row):
            begin, out, rows = starts[0] if row < starts[1][0] else starts[1]
            return out, (row - begin) % rows, (row - begin) // rows * width

        half = stack.shape[0] // 2
        for row in range(0, half, unit):
            part = 0 if at < parts[0].shape[0] else 1
            chunks.append((part, at - part * parts[0].shape[0], unit, (place(row), place(half + row))))
            at += unit
    core = side(1).astype(jnp.int32)[None]
    inside = pl.BlockSpec(memory_space=pltpu.VMEM)
    return pl.pallas_call(
        functools.partial(place_kernel, chunks),
        in_specs=[pl.BlockSpec(memory_space=pltpu.SMEM)] + [inside] * 4,
        out_specs=[inside] * len(shapes),
        out_shape=[jax.ShapeDtypeStruct(shape, F32) for shape in shapes],
        compiler_params=pltpu.CompilerParams(vmem_limit_bytes=40 * MIB),
    )(core, *parts, *others)


def on_device(
    devices,
    node_input,
    edge_input,
    node_count,
    edge_count,
    edge_source,
    edge_target,
    gcn_weight,
    edge_weight,
    attend_weight,
    attend_out,
    local_gain,
    local_shift,
    attend_gain,
    attend_shift,
    hidden_weight,
    hidden_bias,
    output_weight,
    final_gain,
    final_shift,
    cotangent,
):
    graphs, edges = edge_source.shape
    node_rows, width = node_input.shape
    edge_rows = edge_input.shape[0]
    slots = node_rows // graphs
    hidden = hidden_weight.shape[1]
    steps = graphs // GROUP
    local_gain, local_shift, attend_gain, attend_shift, final_gain, final_shift = [
        ("whole", item[None])
        for item in (local_gain, local_shift, attend_gain, attend_shift, final_gain, final_shift)
    ]
    counts = ("scalar", node_count)
    node_arg = ("rows", node_input)
    edge_arg = ("rows", edge_input)
    cotangent_arg = ("rows", cotangent)
    ends = [("rows", edge_source), ("rows", edge_target)]
    node_shape, edge_shape = node_input.shape, edge_input.shape
    sums, shares = (8, width), (devices, 1, 5 * width)
    stats = pltpu.VMEM(sums, F32)
    (
        local_pre,
        attend_pre,
        inverse,
        ratio,
        gate,
        sent,
        slope,
        qkv,
        probs,
        attended,
        branch_shares,
    ) = run_blocks(
        forward_kernel,
        steps,
        60,
        [counts, ("scalar", edge_count), node_arg, edge_arg]
        + ends
        + [("whole", item) for item in (gcn_weight, edge_weight, attend_weight, attend_out)],
        [
            ("rows", node_shape, F32),
            ("rows", node_shape, F32),
            ("rows", node_shape, LOW),
            ("rows", node_shape, LOW),
            ("rows", edge_shape, LOW),
            ("rows", edge_shape, LOW),
            ("rows", edge_shape, LOW),
            ("rows", (node_rows, 3 * width), LOW),
            ("rows", (node_rows, (width // HEAD_SIZE) * slots), LOW),
            ("rows", node_shape, LOW),
            ("whole", shares, F32),
        ],
        scratch=[stats],
    )
    local_hat, attend_hat, mixed, pre, final, branch_stats, final_shares = run_blocks(
        mix_kernel,
        graphs // MIX_GROUP,
        50,
        [counts, ("rows", local_pre), ("rows", attend_pre), cotangent_arg]
        + [("whole", all_share(branch_shares)), local_gain, local_shift, attend_gain, attend_shift]
        + [("whole", hidden_weight)]
        + [("whole", hidden_bias[None]), ("whole", output_weight)],
        [
            ("held", node_shape, LOW),
            ("held", node_shape, LOW),
            ("held", node_shape, LOW),
            ("rows", (node_rows, hidden), LOW),
            ("rows", node_shape, F32),
            ("whole", sums, F32),
            ("whole", (devices, 1, 4 * width), F32),
        ],
        scratch=[stats],
    )
    branch_arg = ("whole", branch_stats)
    d_mixed, result, mix_grads, final_gain_grad, final_shift_grad, back_shares = run_blocks(
        mix_back_kernel,
        graphs // MIX_GROUP,
        50,
        [counts, ("rows", final), ("rows", pre), ("held", local_hat)]
        + [("held", attend_hat), ("held", mixed), cotangent_arg, branch_arg]
        + [("whole", all_share(final_shares)), final_gain, final_shift]
        + [("whole", hidden_weight), ("whole", output_weight)],
        [
            ("rows", node_shape, LOW),
            ("rows", node_shape, LOW),
            ("whole", (2 * hidden, width), F32),
            ("whole", (1, width), F32),
            ("whole", (1, width), F32),
            ("whole", shares, F32),
        ],
        scratch=[stats, stats],
        flops=8 * node_rows * width * hidden,
    )
    (
        node_part,
        d_hats,
        gcn_grads,
        back_stats,
        local_gain_grad,
        local_shift_grad,
        attend_gain_grad,
        attend_shift_grad,
        bias_grad,
    ) = run_blocks(
        gcn_back_kernel,
        steps,
        60,
        [counts, ("rows", d_mixed), ("rows", local_hat), ("rows", inverse), ("rows", ratio)]
        + [("rows", gate), ("rows", sent), ("rows", slope), node_arg, edge_arg]
        + ends
        + [branch_arg, ("whole", all_share(back_shares)), local_gain, ("whole", gcn_weight)],
        [
            ("rows", node_shape, LOW),
            ("rows", edge_shape, LOW),
            ("whole", (5 * width, width), F32),
            ("whole", sums, F32),
        ]
        + [("whole", (1, width), F32)] * 4
        + [("whole", (1, hidden), F32)],
        scratch=[pltpu.VMEM((node_rows // steps, 4 * width), LOW)],
    )
    gcn_core = keep_half(gcn_grads, 1, devices)
    orders = chip_orders(devices)
    early = jnp.concatenate([keep_half(mix_grads, 1, devices), gcn_core])
    early, got = halve(early, orders[0][0], devices)
    early, qkv = lax.optimization_barrier((early, qkv))
    direct, d_qkv, attend_grads = run_blocks(
        attend_back_kernel,
        steps,
        60,
        [counts, ("rows", d_mixed), ("rows", attend_hat), ("rows", qkv), ("rows", probs)]
        + [("rows", attended), node_arg, ("rows", node_part), branch_arg, ("whole", back_stats)]
        + [attend_gain, ("whole", attend_out)],
        [
            ("rows", node_shape, LOW),
            ("rows", (node_rows, 3 * width), LOW),
            ("whole", (4 * width, width), F32),
        ],
    )

    def give_edges(d_hats):
        return run_blocks(
            edge_out_kernel,
            graphs // MIX_GROUP,
            60,
            [("rows", d_hats), ("whole", edge_weight)],
            [("rows", edge_shape, F32)],
            flops=2 * edge_rows * width * width,
        )[0]

    def give_nodes(d_qkv):
        return run_blocks(
            node_out_kernel,
            graphs // MIX_GROUP,
            60,
            [("rows", direct), ("rows", d_qkv), ("whole", attend_weight)],
            [("rows", node_shape, F32)],
            flops=6 * node_rows * width * width,
        )[0]

    got, attend_grads = lax.optimization_barrier((got, attend_grads))
    late = keep_half(attend_grads, 1, devices)
    beside = {0: (give_edges, d_hats), 2 * len(orders[0]) - 1: (give_nodes, d_qkv)}
    parts, others, (edge_out, node_out) = weight_sums([early + got, late], devices, beside)
    hidden_grad, output_grad, gcn_grad, edge_grad, attend_grad, attend_out_grad = place_sums(
        parts,
        others,
        (mix_grads, gcn_grads, attend_grads),
        [hidden_weight.shape, output_weight.shape, gcn_weight.shape]
        + [edge_weight.shape, attend_weight.shape, attend_out.shape],
    )
    return (
        result,
        node_out,
        edge_out,
        gcn_grad,
        edge_grad,
        attend_grad,
        attend_out_grad,
        local_gain_grad[0],
        local_shift_grad[0],
        attend_gain_grad[0],
        attend_shift_grad[0],
        hidden_grad,
        bias_grad[0],
        output_grad,
        final_gain_grad[0],
        final_shift_grad[0],
    )


def solution(mesh):
    rows = P("graphs", None)
    each = P("graphs")
    return jax.shard_map(
        functools.partial(on_device, mesh.shape["graphs"]),
        mesh=mesh,
        in_specs=(rows, rows, each, each, rows, rows) + (P(),) * 13 + (rows,),
        out_specs=(rows, rows, rows) + (P(),) * 13,
        check_vma=False,
    )
```
